32 devices in a mesh: dp: 8 (over z, y), tp: 4 (over x, core).
Axes of the slice: x: 2, y: 2, z: 4, core: 2. Of those that a mesh axis runs over, the one named last changes fastest.
Arguments:
- tile_vectors: bfloat16 [16384, 768], P(('dp', 'tp')), may hold values from -6 to 6
- snapshot_horizon_slot: int32 [8], P('dp'), may hold values from 0 to 39
- horizon_sample_tally: int32 [40], replicated, may hold values from 1 to 9
- specialist_outlooks: bfloat16 [3, 69, 64, 16384], P(None, None, None, ('dp', 'tp')), may hold values from -6 to 6
- early_layernorm_scale: float32 [768], replicated, may hold values from 0.5 to 1.5
- early_layernorm_shift: float32 [768], replicated, may hold values from -1.75 to 1.75
- horizon_vectors: float32 [40, 768], replicated, may hold values from -3 to 3
- triple_head_matrix: bfloat16 [3, 768, 768], P(None, None, 'tp'), may hold values from -0.21875 to 0.21875
- attending_matrix: bfloat16 [768, 768], P('tp'), may hold values from -3.5 to 3.5
- attending_offset: float32 [768], replicated, may hold values from -1.75 to 1.75
- later_layernorm_scale: float32 [768], replicated, may hold values from 0.5 to 1.5
- later_layernorm_shift: float32 [768], replicated, may hold values from -1.75 to 1.75
- widening_matrix: bfloat16 [768, 3072], P(None, 'tp'), may hold values from -0.21875 to 0.21875
- widening_offset: float32 [3072], P('tp'), may hold values from -3 to 3
- narrowing_matrix: bfloat16 [3072, 768], P('tp'), may hold values from -0.109375 to 0.109375
- narrowing_offset: float32 [768], replicated, may hold values from -1.75 to 1.75
- router_matrix: bfloat16 [768, 207], replicated, may hold values from -0.109375 to 0.109375
- router_offset: float32 [207], replicated, may hold values from -1.75 to 1.75
- adjuster_matrix: bfloat16 [768, 69], replicated, may hold values from -0.21875 to 0.21875
- adjuster_offset: float32 [69], replicated, may hold values from -3 to 3
- combined_loss_slope: bfloat16 [69, 64, 16384], P(None, None, ('dp', 'tp')), may hold values from -6 to 6
Outputs:
- blended: float32 [69, 64, 16384], P(None, None, ('dp', 'tp'))
- tokens_grad: float32 [16384, 768], P(('dp', 'tp'))
- first_gain_grad: float32 [768], replicated
- first_shift_grad: float32 [768], replicated
- lead_table_grad: float32 [40, 768], replicated
- qkv_weight_grad: float32 [3, 768, 768], P(None, None, 'tp')
- proj_weight_grad: float32 [768, 768], P('tp')
- proj_bias_grad: float32 [768], replicated
- second_gain_grad: float32 [768], replicated
- second_shift_grad: float32 [768], replicated
- in_weight_grad: float32 [768, 3072], P(None, 'tp')
- in_bias_grad: float32 [3072], P('tp')
- out_weight_grad: float32 [3072, 768], P('tp')
- out_bias_grad: float32 [768], replicated
- gate_weight_grad: float32 [768, 207], replicated
- gate_bias_grad: float32 [207], replicated
- correct_weight_grad: float32 [768, 69], replicated
- correct_bias_grad: float32 [69], replicated
The draws below stay inside these ranges and needn't reach their ends.
All inputs are finite; a program needn't handle non-finite values.
Results may differ from the reference program's by a relative error of at most 0.017.
The reference program's roundings to bfloat16 on the way count: a program that leaves them out, or rounds other values in their place, can miss the bound.
Values may be sent and summed in bfloat16 or wider, within the bound.
A program may use at most 128 MiB of HBM per device.

```python
import jax
import jax.numpy as jnp
from jax import lax

D = 768
HEADS = 12
HEAD_DIM = 64
FF = 3072
ATMOS_FIELDS = 69
TILE_GRID_SITES = 64
LEADS = 40
SPECIALIST_TOTAL = 3
TILES_PER_SHOT = 2048
QBLOCK = 512
SNAPSHOT_TOTAL = 8
TILE_TOTAL = 16384


def with_ends(entries, stream_key, low, top_value):
    longest = entries.shape.index(max(entries.shape))
    spots = []
    for shift in (0, 1):
        where = [jax.random.randint(jax.random.fold_in(stream_key, axis), (), 0, length) for axis, length in enumerate(entries.shape)]
        where[longest] = (where[longest] + shift) % entries.shape[longest]
        spots.append(tuple(where))
    return entries.at[spots[0]].set(low).at[spots[1]].set(top_value)


def block_scale(rng, dims, shards, smallest, top_value):
    loudness = 1.0
    for position, parts in shards:
        heights = jax.random.uniform(jax.random.fold_in(jax.random.fold_in(rng, 6), position), (parts,), jnp.float32, smallest / len(shards), top_value / len(shards))
        loudness = loudness * jnp.repeat(jnp.exp(heights), dims[position] // parts).reshape((-1,) + (1,) * (len(dims) - 1 - position))
    return loudness


def normal_values(rng, shape, width, reach, cuts=(), kind=jnp.bfloat16):
    drawn = jax.random.normal(rng, shape, jnp.float32) * width
    if len(cuts) > 0:
        drawn = block_scale(rng, shape, cuts, -0.22, 0.18) * drawn
    return jnp.clip(drawn, min=-reach, max=reach).astype(kind)


def setup_inputs(seed: int = 0) -> dict:
    keys = jax.random.split(jax.random.key(seed), 22)
    return {
        "tile_vectors": normal_values(keys[0], (TILE_TOTAL, D), 1.0, 6.0, ((0, 32),)),
        "snapshot_horizon_slot": with_ends(jax.random.randint(keys[1], (SNAPSHOT_TOTAL,), 0, LEADS), jax.random.fold_in(keys[1], 1), 0, LEADS - 1).astype(jnp.int32),
        "horizon_sample_tally": with_ends(jax.random.randint(keys[2], (LEADS,), 1, 10), jax.random.fold_in(keys[2], 1), 1, 9).astype(jnp.int32),
        "specialist_outlooks": normal_values(keys[3], (SPECIALIST_TOTAL, ATMOS_FIELDS, TILE_GRID_SITES, TILE_TOTAL), 1.0, 6.0, ((3, 32),)),
        "early_layernorm_scale": jnp.clip(1.0 + 0.1 * jax.random.normal(keys[4], (D,), jnp.float32), 0.5, 1.5),
        "early_layernorm_shift": normal_values(keys[5], (D,), 0.3, 1.75, (), jnp.float32),
        "horizon_vectors": normal_values(keys[6], (LEADS, D), 0.5, 3.0, (), jnp.float32),
        "triple_head_matrix": normal_values(keys[7], (3, D, D), D ** -0.5, 0.21875, ((2, 4),)),
        "attending_matrix": normal_values(keys[8], (D, D), (max(D // 256, 1)) ** -0.5, 3.5, ((0, 4),)),
        "attending_offset": normal_values(keys[9], (D,), 0.3, 1.75, (), jnp.float32),
        "later_layernorm_scale": jnp.clip(1.0 + 0.1 * jax.random.normal(keys[10], (D,), jnp.float32), 0.5, 1.5),
        "later_layernorm_shift": normal_values(keys[11], (D,), 0.3, 1.75, (), jnp.float32),
        "widening_matrix": normal_values(keys[12], (D, FF), D ** -0.5, 0.21875, ((1, 4),)),
        "widening_offset": normal_values(keys[13], (FF,), 0.5, 3.0, ((0, 4),), jnp.float32),
        "narrowing_matrix": normal_values(keys[14], (FF, D), FF ** -0.5, 0.109375, ((0, 4),)),
        "narrowing_offset": normal_values(keys[15], (D,), 0.3, 1.75, (), jnp.float32),
        "router_matrix": normal_values(keys[16], (D, SPECIALIST_TOTAL * ATMOS_FIELDS), (4 * D) ** -0.5, 0.109375),
        "router_offset": normal_values(keys[17], (SPECIALIST_TOTAL * ATMOS_FIELDS,), 0.3, 1.75, (), jnp.float32),
        "adjuster_matrix": normal_values(keys[18], (D, ATMOS_FIELDS), D ** -0.5, 0.21875),
        "adjuster_offset": normal_values(keys[19], (ATMOS_FIELDS,), 0.5, 3.0, (), jnp.float32),
        "combined_loss_slope": normal_values(keys[20], (ATMOS_FIELDS, TILE_GRID_SITES, TILE_TOTAL), 1.0, 6.0, ((2, 32),)),
    }


HIGH = lax.Precision.HIGHEST
EPSILON = 1e-05

@jax.custom_vjp
def low(v):
    return lax.optimization_barrier(v.astype(jnp.bfloat16)).astype(jnp.float32)

@jax.custom_vjp
def low_back(v):
    return v

def low_keep(v):
    return (low(v), None)

def low_pass(kept, grad):
    return (grad,)

def back_keep(v):
    return (v, None)

def back_low(kept, grad):
    return (low(grad),)
low.defvjp(low_keep, low_pass)
low_back.defvjp(back_keep, back_low)

def layer_norm(values, gain_vec, shift_vec):
    center = values - lax.optimization_barrier(jnp.mean(values, axis=-1, keepdims=True))
    spread = lax.optimization_barrier(jnp.mean(center * center, axis=-1, keepdims=True))
    return center * lax.rsqrt(spread + EPSILON) * gain_vec + shift_vec

def softmax_axis(scores, axis_num):
    highest = lax.optimization_barrier(jnp.max(scores, axis=axis_num, keepdims=True))
    raised = jnp.exp(scores - highest)
    return raised / lax.optimization_barrier(jnp.sum(raised, axis=axis_num, keepdims=True))

def frame_forward(weight_set, frame_rows, snapshot_estimate, lead_id, row_scale):
    early_layernorm_scale, early_layernorm_shift, horizon_vectors, triple_head_matrix, attending_matrix, attending_offset, later_layernorm_scale, later_layernorm_shift, widening_matrix, widening_offset, narrowing_matrix, narrowing_offset, router_matrix, router_offset, adjuster_matrix, adjuster_offset = weight_set
    length = frame_rows.shape[0]
    attn_in = low(layer_norm(frame_rows, early_layernorm_scale, early_layernorm_shift) + horizon_vectors[lead_id][None, :])
    projected = low(low_back(jnp.einsum('td,sdh->sth', attn_in, triple_head_matrix, precision=HIGH)))
    queries = projected[0].reshape(length, HEADS, HEAD_DIM)
    keys_all = projected[1].reshape(length, HEADS, HEAD_DIM)
    values_all = projected[2].reshape(length, HEADS, HEAD_DIM)

    def attend_block(block_id):
        query_part = lax.dynamic_slice_in_dim(queries, block_id * QBLOCK, QBLOCK, 0)
        scores = low_back(jnp.einsum('qhd,khd->hqk', query_part, keys_all, precision=HIGH) * HEAD_DIM ** (-0.5))
        prob_rows = low(softmax_axis(scores, -1))
        return jnp.einsum('hqk,khd->qhd', prob_rows, values_all, precision=HIGH)
    mixed_out = lax.map(jax.checkpoint(attend_block), jnp.arange(length // QBLOCK, dtype=jnp.int32))
    attended = low(low_back(mixed_out.reshape(length, D)))
    after_attn = frame_rows + low_back(jnp.dot(attended, attending_matrix, precision=HIGH)) + attending_offset
    mlp_in = low(layer_norm(after_attn, later_layernorm_scale, later_layernorm_shift))
    hidden = low_back(jnp.dot(mlp_in, widening_matrix, precision=HIGH) + widening_offset)
    activated = low(jax.nn.gelu(hidden, approximate=False))
    after_mlp = after_attn + low_back(jnp.dot(activated, narrowing_matrix, precision=HIGH)) + narrowing_offset
    head_in = low(after_mlp)
    logits = low_back(jnp.dot(head_in, router_matrix, precision=HIGH) + router_offset).reshape(length, SPECIALIST_TOTAL, ATMOS_FIELDS)
    correction = low_back(jnp.dot(head_in, adjuster_matrix, precision=HIGH) + adjuster_offset) * row_scale
    gate_probabilities = softmax_axis(logits, 1)
    expert_mixture = jnp.einsum('tec,ecpt->cpt', gate_probabilities, snapshot_estimate, precision=HIGH)
    return expert_mixture + correction.T[:, None, :]

def reference(tile_vectors, snapshot_horizon_slot, horizon_sample_tally, specialist_outlooks, early_layernorm_scale, early_layernorm_shift, horizon_vectors, triple_head_matrix, attending_matrix, attending_offset, later_layernorm_scale, later_layernorm_shift, widening_matrix, widening_offset, narrowing_matrix, narrowing_offset, router_matrix, router_offset, adjuster_matrix, adjuster_offset, combined_loss_slope):
    weight_set = tuple((weight_arg.astype(jnp.float32) for weight_arg in (early_layernorm_scale, early_layernorm_shift, horizon_vectors, triple_head_matrix, attending_matrix, attending_offset, later_layernorm_scale, later_layernorm_shift, widening_matrix, widening_offset, narrowing_matrix, narrowing_offset, router_matrix, router_offset, adjuster_matrix, adjuster_offset)))
    frame_rows = tile_vectors.astype(jnp.float32).reshape(SNAPSHOT_TOTAL, TILES_PER_SHOT, D)
    snapshot_estimate = jnp.transpose(specialist_outlooks.astype(jnp.float32).reshape(SPECIALIST_TOTAL, ATMOS_FIELDS, TILE_GRID_SITES, SNAPSHOT_TOTAL, TILES_PER_SHOT), (3, 0, 1, 2, 4))
    frame_scale = lax.rsqrt(horizon_sample_tally.astype(jnp.float32)[snapshot_horizon_slot])

    def forward(weights_in, rows_in):

        def one_frame(carry, pieces):
            rows_one, fore_one, lead_one, scale_one = pieces
            return (carry, frame_forward(weights_in, rows_one, fore_one, lead_one, scale_one))
        unused, stacked = lax.scan(jax.checkpoint(one_frame), jnp.zeros((), jnp.float32), (rows_in, snapshot_estimate, snapshot_horizon_slot, frame_scale))
        return stacked
    blend_frames, pullback = jax.vjp(forward, weight_set, frame_rows)
    cotangent = jnp.transpose(combined_loss_slope.astype(jnp.float32).reshape(ATMOS_FIELDS, TILE_GRID_SITES, SNAPSHOT_TOTAL, TILES_PER_SHOT), (2, 0, 1, 3))
    weight_grads, rows_grad = pullback(cotangent)
    blended = jnp.transpose(blend_frames, (1, 2, 0, 3)).reshape(ATMOS_FIELDS, TILE_GRID_SITES, TILE_TOTAL)
    return (blended, rows_grad.reshape(TILE_TOTAL, D), weight_grads[0], weight_grads[1], weight_grads[2], weight_grads[3], weight_grads[4], weight_grads[5], weight_grads[6], weight_grads[7], weight_grads[8], weight_grads[9], weight_grads[10], weight_grads[11], weight_grads[12], weight_grads[13], weight_grads[14], weight_grads[15])
```

```python
import functools
import jax
import jax.numpy as jnp
from jax import lax
from jax.experimental import pallas as pl
from jax.experimental.pallas import tpu as pltpu
from jax.sharding import PartitionSpec as P

HD = 64
EXPERTS = 3
EPSILON = 1e-05
F32 = jnp.float32
BF16 = jnp.bfloat16


def dot(a, b, dims=((1,), (0,))):
    return lax.dot_general(a, b, (dims, ((), ())), preferred_element_type=F32)


def fwd_kernel(q_ref, k_ref, v_ref, o_ref, lse_ref, ks, *, scale):
    @pl.when(pl.program_id(1) == 0)
    def _():
        ks[...] = k_ref[0, 0].T

    q = q_ref[0, 0] * jnp.bfloat16(scale)
    s = dot(ks[...], q)
    m = jnp.max(s, axis=0, keepdims=True)
    p = jnp.exp(s - m)
    l = jnp.sum(p, axis=0, keepdims=True)
    o = dot(v_ref[0, 0], p.astype(BF16))
    o_ref[0] = (o / l).astype(BF16)
    lse_ref[0] = m + jnp.log(l)


def attn_fwd(qkv, scale, bq):
    _, heads, _, rows = qkv.shape
    return pl.pallas_call(
        functools.partial(fwd_kernel, scale=scale),
        grid=(heads, rows // bq),
        in_specs=[
            pl.BlockSpec((1, 1, HD, bq), lambda h, i: (0, h, 0, i)),
            pl.BlockSpec((1, 1, HD, rows), lambda h, i: (1, h, 0, 0)),
            pl.BlockSpec((1, 1, HD, rows), lambda h, i: (2, h, 0, 0)),
        ],
        out_specs=[
            pl.BlockSpec((1, HD, bq), lambda h, i: (h, 0, i)),
            pl.BlockSpec((1, 1, bq), lambda h, i: (h, 0, i)),
        ],
        out_shape=[
            jax.ShapeDtypeStruct((heads, HD, rows), BF16),
            jax.ShapeDtypeStruct((heads, 1, rows), F32),
        ],
        scratch_shapes=[pltpu.VMEM((rows, HD), BF16)],
        compiler_params=pltpu.CompilerParams(vmem_limit_bytes=50 << 20),
        cost_estimate=pl.CostEstimate(
            flops=24_000_000_000, bytes_accessed=4 << 20, transcendentals=heads * rows * rows
        ),
        name="attn_fwd",
    )(qkv, qkv, qkv)


def bwd_kernel(
    q_ref, k_ref, v_ref, o_ref, do_ref, lse_ref, dq_ref, dk_ref, dv_ref, ks, vs, dks, dvs, *, scale
):
    i = pl.program_id(1)

    @pl.when(i == 0)
    def _():
        ks[...] = k_ref[0, 0].T
        vs[...] = v_ref[0, 0].T
        dks[...] = jnp.zeros_like(dks)
        dvs[...] = jnp.zeros_like(dvs)

    qt = q_ref[0, 0] * jnp.bfloat16(scale)
    dot_t = do_ref[0]
    dsum = jnp.sum(dot_t.astype(F32) * o_ref[0].astype(F32), axis=0, keepdims=True)
    s = dot(ks[...], qt)
    p = jnp.exp(s - lse_ref[0])
    dp = dot(vs[...], dot_t)
    ds = (p * (dp - dsum)).astype(BF16)
    dq_ref[0] = (dot(k_ref[0, 0], ds) * scale).astype(BF16)
    dvs[...] += dot(p.astype(BF16), dot_t.T)
    dks[...] += dot(ds, qt.T)

    @pl.when(i == pl.num_programs(1) - 1)
    def _():
        dk_ref[0] = dks[...].astype(BF16).T
        dv_ref[0] = dvs[...].astype(BF16).T


def attn_bwd(qkv, o, do, lse, scale, bq):
    _, heads, _, rows = qkv.shape

    def blk(j):
        return pl.BlockSpec((1, 1, HD, bq), lambda h, i: (j, h, 0, i))

    def full(j):
        return pl.BlockSpec((1, 1, HD, rows), lambda h, i: (j, h, 0, 0))

    return pl.pallas_call(
        functools.partial(bwd_kernel, scale=scale),
        grid=(heads, rows // bq),
        in_specs=[
            blk(0),
            full(1),
            full(2),
            pl.BlockSpec((1, HD, bq), lambda h, i: (h, 0, i)),
            pl.BlockSpec((1, HD, bq), lambda h, i: (h, 0, i)),
            pl.BlockSpec((1, 1, bq), lambda h, i: (h, 0, i)),
        ],
        out_specs=[
            pl.BlockSpec((1, HD, bq), lambda h, i: (h, 0, i)),
            pl.BlockSpec((1, HD, rows), lambda h, i: (h, 0, 0)),
            pl.BlockSpec((1, HD, rows), lambda h, i: (h, 0, 0)),
        ],
        out_shape=[jax.ShapeDtypeStruct((heads, HD, rows), BF16)] * 3,
        scratch_shapes=[pltpu.VMEM((rows, HD), BF16)] * 2 + [pltpu.VMEM((rows, HD), F32)] * 2,
        compiler_params=pltpu.CompilerParams(vmem_limit_bytes=50 << 20),
        cost_estimate=pl.CostEstimate(
            flops=46_000_000_000, bytes_accessed=8 << 20, transcendentals=heads * rows * rows
        ),
        name="attn_bwd",
    )(qkv, qkv, qkv, o, do, lse)


def norm_parts(values):
    center = values - jnp.mean(values, axis=-1, keepdims=True)
    rstd = lax.rsqrt(jnp.mean(center * center, axis=-1, keepdims=True) + EPSILON)
    return center * rstd, rstd


def norm_back(hat, rstd, gain, grad):
    g = grad * gain
    return rstd * (
        g
        - jnp.mean(g, axis=-1, keepdims=True)
        - hat * jnp.mean(g * hat, axis=-1, keepdims=True)
    )


def gelu_parts(u):
    half = jnp.exp(-0.5 * u * u)
    t = 1.0 / (1.0 + (0.3275911 * 0.7071067811865476) * jnp.abs(u))
    poly = t * (
        0.254829592
        + t * (-0.284496736 + t * (1.421413741 + t * (-1.453152027 + t * 1.061405429)))
    )
    tail = 0.5 * poly * half
    cdf = jnp.where(u >= 0, 1.0 - tail, tail)
    return u * cdf, cdf + u * half * 0.3989422804014327


def make_body(mesh):
    dp_size, tp_size = mesh.shape["dp"], mesh.shape["tp"]
    dp_bits = [1 << b for b in range(dp_size.bit_length() - 1)]

    def swap(x, axis, bit):
        size = dp_size if axis == "dp" else tp_size
        return lax.ppermute(x, axis, [(i, i ^ bit) for i in range(size)])

    def core(x):
        return swap(x, "tp", 1)

    def across(x):
        return swap(x, "tp", 2)

    def diag(x):
        return swap(x, "tp", 3)

    def my_bit(bit):
        return (lax.axis_index("dp") & bit) != 0

    def fold_tp(parts, cast=BF16):
        got1 = core(parts[3].astype(cast))
        got0 = core(parts[1].astype(cast))
        mid = parts[2].astype(F32) + got1.astype(F32)
        own = parts[0].astype(F32) + got0.astype(F32)
        return own + across(mid.astype(cast)).astype(F32)

    def dp_sum(x, bits):
        for bit in bits:
            n = x.shape[0] // 2
            lo, hi = x[:n], x[n:]
            mine = my_bit(bit)
            send = jnp.where(mine, lo, hi).astype(BF16)
            keep = jnp.where(mine, hi, lo).astype(F32)
            x = keep + swap(send, "dp", bit).astype(F32)
        x = x.astype(BF16)
        for bit in reversed(bits):
            got = swap(x, "dp", bit)
            mine = my_bit(bit)
            x = jnp.concatenate([jnp.where(mine, got, x), jnp.where(mine, x, got)], axis=0)
        return x

    def dp_sum_halves(x):
        n = x.shape[0] // 2
        order = list(dp_bits)
        if n % dp_size:
            return dp_sum(x, order).astype(F32)
        other = [order[1], order[0]] + order[2:]
        return jnp.concatenate([dp_sum(x[:n], order), dp_sum(x[n:], other)], axis=0).astype(F32)

    def butterfly_dp(x):
        for bit in dp_bits:
            x = x + swap(x, "dp", bit)
        return x

    def butterfly_all(x):
        x = x + core(x)
        x = x + across(x)
        return butterfly_dp(x)

    def gather_tp(x):
        n = x.shape[0] // 2
        mine = my_bit(1)
        half = across(jnp.where(mine, x[n:], x[:n]))
        other = swap(half, "dp", 1)
        far = jnp.concatenate([jnp.where(mine, other, half), jnp.where(mine, half, other)], axis=0)
        return [x, core(x), far, core(far)]

    def body(
        tile_vectors,
        snapshot_horizon_slot,
        horizon_sample_tally,
        specialist_outlooks,
        early_layernorm_scale,
        early_layernorm_shift,
        horizon_vectors,
        triple_head_matrix,
        attending_matrix,
        attending_offset,
        later_layernorm_scale,
        later_layernorm_shift,
        widening_matrix,
        widening_offset,
        narrowing_matrix,
        narrowing_offset,
        router_matrix,
        router_offset,
        adjuster_matrix,
        adjuster_offset,
        combined_loss_slope,
    ):
        rows_dev, width = tile_vectors.shape
        heads = triple_head_matrix.shape[2] // HD
        rows_frame = rows_dev * tp_size
        fields = adjuster_matrix.shape[1]
        sites = combined_loss_slope.shape[1]
        scale_val = HD ** (-0.5)
        tp_index = lax.axis_index("tp")
        lead = snapshot_horizon_slot[0]
        embed = lax.dynamic_slice_in_dim(horizon_vectors, lead, 1, 0)
        row_scale = lax.rsqrt(
            lax.dynamic_slice_in_dim(horizon_sample_tally, lead, 1, 0).astype(F32)
        )[0]
        residual = tile_vectors.astype(F32)

        hat1, rstd1 = norm_parts(residual)
        attn_own = (hat1 * early_layernorm_scale + early_layernorm_shift + embed).astype(BF16)
        rows2 = across(attn_own)
        rows1 = core(attn_own)
        rows3 = core(rows2)
        rows2, rows3, triple_w, proj_w, wide_w, narrow_w = lax.optimization_barrier(
            (rows2, rows3, triple_head_matrix, attending_matrix, widening_matrix, narrowing_matrix)
        )
        attn_rows = jnp.concatenate([attn_own, rows1, rows2, rows3], axis=0)

        proj_all = gather_tp(proj_w)
        wide_all = gather_tp(wide_w)
        narrow_all = gather_tp(narrow_w)
        off2 = across(widening_offset)
        off_all = [widening_offset, core(widening_offset), off2, core(off2)]

        qkv = jnp.einsum(
            "sdh,td->sht", triple_w, attn_rows, preferred_element_type=F32
        ).astype(BF16)
        qkv = qkv.reshape(3, heads, HD, rows_frame)
        o_heads, lse = attn_fwd(qkv, scale_val, min(512, rows_frame))

        slope = combined_loss_slope.astype(F32)
        expert_dot = jnp.stack(
            [
                jnp.sum(specialist_outlooks[e].astype(F32) * slope, axis=1)
                for e in range(EXPERTS)
            ]
        )
        slope_sum = jnp.sum(slope, axis=1)

        o_flat = o_heads.reshape(heads * HD, rows_frame)
        ob = [o_flat[:, p * rows_dev : (p + 1) * rows_dev] for p in range(tp_size)]
        o_own = jnp.concatenate([ob[0], core(ob[1]), across(ob[2]), diag(ob[3])], axis=0)
        proj_cat = jnp.concatenate(proj_all, axis=0)
        x1 = residual + dot(o_own, proj_cat, ((0,), (0,))) + attending_offset
        hat2, rstd2 = norm_parts(x1)
        c_low = (hat2 * later_layernorm_scale + later_layernorm_shift).astype(BF16)
        acts, slopes = [], []
        for p in range(tp_size):
            m, d = gelu_parts(dot(c_low, wide_all[p]) + off_all[p])
            acts.append(m.astype(BF16))
            slopes.append(d)
        mlp = dot(acts[0], narrow_all[0])
        for p in range(1, tp_size):
            mlp = mlp + dot(acts[p], narrow_all[p])
        x2 = x1 + mlp + narrowing_offset
        h_low = x2.astype(BF16)
        logits = dot(router_matrix, h_low, ((0,), (1,))) + router_offset[:, None]
        corr = (dot(adjuster_matrix, h_low, ((0,), (1,))) + adjuster_offset[:, None]) * row_scale
        logits = logits.reshape(EXPERTS, fields, rows_dev)
        top = jnp.max(logits, axis=0, keepdims=True)
        raised = jnp.exp(logits - top)
        gates = raised / jnp.sum(raised, axis=0, keepdims=True)
        mixed = jnp.sum(gates * expert_dot, axis=0, keepdims=True)
        dlog = (gates * (expert_dot - mixed)).astype(BF16).reshape(EXPERTS * fields, rows_dev)
        dcorr = (slope_sum * row_scale).astype(BF16)

        head_grads = jnp.concatenate([dlog, dcorr], axis=0)
        head_w = jnp.concatenate([router_matrix, adjuster_matrix], axis=1)
        dx2 = dot(head_grads, head_w, ((0,), (1,)))
        dz = dx2.astype(BF16)
        d_narrow = [dot(acts[p], dz, ((0,), (0,))).astype(BF16) for p in range(tp_size)]
        dus = [
            (dot(dz, narrow_all[p], ((1,), (1,))) * slopes[p]).astype(BF16) for p in range(tp_size)
        ]
        d_wide = [dot(c_low, dus[p], ((0,), (0,))).astype(BF16) for p in range(tp_size)]
        dc = dot(dus[0], wide_all[0], ((1,), (1,)))
        for p in range(1, tp_size):
            dc = dc + dot(dus[p], wide_all[p], ((1,), (1,)))
        dx1 = dx2 + norm_back(hat2, rstd2, later_layernorm_scale, dc)
        dy = dx1.astype(BF16)
        do_all = dot(proj_cat, dy, ((1,), (1,))).astype(BF16)
        nh = heads * HD
        db = [do_all[p * nh : (p + 1) * nh] for p in range(tp_size)]
        do = jnp.concatenate([db[0], core(db[1]), across(db[2]), diag(db[3])], axis=1)
        do = do.reshape(heads, HD, rows_frame)
        dqt, dkt, dvt = attn_bwd(qkv, o_heads, do, lse, scale_val, min(512, rows_frame))

        blended = (corr)[:, None, :]
        for e in range(EXPERTS):
            blended = blended + gates[e][:, None, :] * specialist_outlooks[e].astype(F32)

        d_proj = dot(o_own, dy, ((1,), (0,))).astype(BF16)
        d_head = dot(h_low, head_grads, ((0,), (1,))).astype(BF16)
        d_head = jnp.pad(d_head, ((0, 0), (0, (-d_head.shape[1]) % 128)))
        dproj_parts = []
        for p in range(tp_size):
            head_blk = lax.dynamic_slice_in_dim(d_head, (tp_index ^ p) * nh, nh, 0)
            dproj_parts.append(
                jnp.concatenate([d_proj[p * nh : (p + 1) * nh], head_blk], axis=1)
            )

        narrow_sum = dp_sum_halves(fold_tp(d_narrow))
        wide_sum = dp_sum_halves(fold_tp(d_wide))
        proj_sum = dp_sum_halves(fold_tp(dproj_parts))
        proj_weight_grad = proj_sum[:, :width]
        head_own = proj_sum[:, width:].astype(BF16)
        h2 = across(head_own)
        head_parts = [head_own, core(head_own), h2, core(h2)]
        head_sum = jnp.zeros((width, head_own.shape[1]), BF16)
        for p in range(tp_size):
            head_sum = lax.dynamic_update_slice_in_dim(
                head_sum, head_parts[p], (tp_index ^ p) * nh, 0
            )
        head_sum = head_sum.astype(F32)
        gate_weight_grad = head_sum[:, : EXPERTS * fields]
        correct_weight_grad = head_sum[:, EXPERTS * fields : (EXPERTS + 1) * fields]

        head_bias = jnp.sum(head_grads.astype(F32), axis=1)
        head_bias = jnp.pad(head_bias, (0, width - head_bias.shape[0]))
        small = jnp.stack(
            [
                jnp.sum(dx2, axis=0),
                jnp.sum(dc * hat2, axis=0),
                jnp.sum(dc, axis=0),
                jnp.sum(dx1, axis=0),
                head_bias,
            ]
        )
        small = butterfly_all(small)
        in_parts = [jnp.sum(dus[p].astype(F32), axis=0) for p in range(tp_size)]
        in_bias_grad = butterfly_dp(fold_tp(in_parts, F32))

        dqkv = jnp.stack([dqt, dkt, dvt]).reshape(3, nh, rows_frame)
        d_qkv = jnp.einsum("td,sht->sdh", attn_rows, dqkv, preferred_element_type=F32)
        qkv_sum = dp_sum_halves(d_qkv.reshape(3 * width, nh)).reshape(3, width, nh)
        da_parts = [
            jnp.einsum(
                "sht,sdh->td",
                dqkv[:, :, p * rows_dev : (p + 1) * rows_dev],
                triple_w,
                preferred_element_type=F32,
            )
            for p in range(tp_size)
        ]
        da = fold_tp(da_parts)
        tokens_grad = dx1 + norm_back(hat1, rstd1, early_layernorm_scale, da)
        da_sum = jnp.sum(da, axis=0)
        last = jnp.stack([jnp.sum(da * hat1, axis=0), da_sum])
        last = last + core(last)
        last = last + across(last)
        leads = horizon_vectors.shape[0]
        onehot = (jnp.arange(leads, dtype=jnp.int32) == lead).astype(F32)
        table = jnp.concatenate([last, onehot[:, None] * last[1][None, :]], axis=0)
        table = butterfly_dp(table)

        return (
            blended,
            tokens_grad,
            table[0],
            table[1],
            table[2:],
            qkv_sum,
            proj_weight_grad,
            small[3],
            small[1],
            small[2],
            wide_sum,
            in_bias_grad,
            narrow_sum,
            small[0],
            gate_weight_grad,
            small[4, : EXPERTS * fields],
            correct_weight_grad,
            small[4, EXPERTS * fields : (EXPERTS + 1) * fields],
        )

    return body


def solution(mesh):
    return jax.shard_map(
        make_body(mesh),
        mesh=mesh,
        in_specs=(
            P(("dp", "tp"), None),
            P("dp"),
            P(),
            P(None, None, None, ("dp", "tp")),
            P(),
            P(),
            P(),
            P(None, None, "tp"),
            P("tp", None),
            P(),
            P(),
            P(),
            P(None, "tp"),
            P("tp"),
            P("tp", None),
            P(),
            P(),
            P(),
            P(),
            P(),
            P(None, None, ("dp", "tp")),
        ),
        out_specs=(
            P(None, None, ("dp", "tp")),
            P(("dp", "tp"), None),
            P(),
            P(),
            P(),
            P(None, None, "tp"),
            P("tp", None),
            P(),
            P(),
            P(),
            P(None, "tp"),
            P("tp"),
            P("tp", None),
            P(),
            P(),
            P(),
            P(),
            P(),
        ),
        check_vma=False,
    )
```

```python
import functools
import jax
import jax.numpy as jnp
from jax import lax
from jax.experimental import pallas as pl
from jax.experimental.pallas import tpu as pltpu
from jax.sharding import PartitionSpec as P

HD = 64
EXPERTS = 3
HEAD_ROWS = 80
EPSILON = 1e-05
F32 = jnp.float32
BF16 = jnp.bfloat16


def dot(a, b, dims=((1,), (0,))):
    return lax.dot_general(a, b, (dims, ((), ())), preferred_element_type=F32)


def fwd_kernel(q_ref, k_ref, v_ref, o_ref, lse_ref, ks, *, scale):
    @pl.when(pl.program_id(1) == 0)
    def _():
        ks[...] = k_ref[0, 0].T

    q = q_ref[0, 0] * jnp.bfloat16(scale)
    s = dot(ks[...], q)
    m = jnp.max(s, axis=0, keepdims=True)
    p = jnp.exp(s - m)
    l = jnp.sum(p, axis=0, keepdims=True)
    o = dot(v_ref[0, 0], p.astype(BF16))
    o_ref[0] = (o / l).astype(BF16)
    lse_ref[0] = m + jnp.log(l)


def attn_fwd(qkv, scale, bq):
    _, heads, _, rows = qkv.shape
    return pl.pallas_call(
        functools.partial(fwd_kernel, scale=scale),
        grid=(heads, rows // bq),
        in_specs=[
            pl.BlockSpec((1, 1, HD, bq), lambda h, i: (0, h, 0, i)),
            pl.BlockSpec((1, 1, HD, rows), lambda h, i: (1, h, 0, 0)),
            pl.BlockSpec((1, 1, HD, rows), lambda h, i: (2, h, 0, 0)),
        ],
        out_specs=[
            pl.BlockSpec((1, HD, bq), lambda h, i: (h, 0, i)),
            pl.BlockSpec((1, 1, bq), lambda h, i: (h, 0, i)),
        ],
        out_shape=[
            jax.ShapeDtypeStruct((heads, HD, rows), BF16),
            jax.ShapeDtypeStruct((heads, 1, rows), F32),
        ],
        scratch_shapes=[pltpu.VMEM((rows, HD), BF16)],
        compiler_params=pltpu.CompilerParams(vmem_limit_bytes=50 << 20),
        cost_estimate=pl.CostEstimate(
            flops=24_000_000_000, bytes_accessed=4 << 20, transcendentals=heads * rows * rows
        ),
        name="attn_fwd",
    )(qkv, qkv, qkv)


def partner(index, bit):
    return index + bit - 2 * bit * lax.rem(lax.div(index, bit), 2)


def rows_at(ref, start, size):
    return ref.at[pl.ds(pl.multiple_of(start, 16), size)]


def add_rows(dst, src, lead, dst_off, src_off, size):
    step = 48 if size % 48 == 0 else 32

    def one(r, carry):
        here = pl.ds(pl.multiple_of(dst_off + r * step, 16), step)
        there = pl.ds(pl.multiple_of(src_off + r * step, 16), step)
        got = src[there] if lead is None else src[lead, there]
        dst[here] = (dst[here].astype(F32) + got.astype(F32)).astype(BF16)
        return carry

    lax.fori_loop(0, size // step, one, 0)


def bwd_kernel(
    qkv_ref, o_ref, lse_ref, do_ref, rows_ref, wt_ref, tiles_ref, gain_ref, onehot_ref, small_ref,
    *rest, scale, chunks, dp_size, heads, tp_size, width
):
    n_src = tp_size * sum(1 for c in chunks if c["tp"] and c["part"] == 0)
    srcs = rest[:n_src]
    tok_ref, sum_ref, last_ref, head_ref = rest[n_src : n_src + 4]
    n_out = n_src + 4 + len(chunks)
    outs = rest[n_src + 4 : n_out]
    (
        ks, vs, dks, dvs, dos, dqkv, da_far, da_core, da_across,
        small_in, small_got, last_own, last_got, hg,
    ) = rest[n_out : n_out + 14]
    per = rest[n_out + 14 : -12]
    (
        send_sems, recv_sems, local_sems, do_send, do_recv, do_local, da_send, da_recv,
        vec_send, vec_recv, hg_send, hg_recv,
    ) = rest[-12:]
    i, h = pl.program_id(0), pl.program_id(1)
    steps = tp_size * heads
    step = i * heads + h
    dpi, tpi = lax.axis_index("dp"), lax.axis_index("tp")
    rows_dev = dos.shape[3]
    bits = [1 << b for b in range(dp_size.bit_length() - 1)]

    def remote(src, dst, ssem, rsem, axis, bit):
        dev = (partner(dpi, bit), tpi) if axis == "dp" else (dpi, partner_any(tpi, bit))
        return pltpu.make_async_remote_copy(
            src_ref=src, dst_ref=dst, send_sem=ssem, recv_sem=rsem,
            device_id=dev, device_id_type=pl.DeviceIdType.MESH,
        )

    def bit_of(bit):
        return lax.rem(lax.div(dpi, bit), 2)

    bufs, at = [], 0
    for c in chunks:
        n = 8 if c["tp"] else 5
        bufs.append(per[at : at + n])
        at += n

    class Chunk:
        def __init__(self, k):
            self.k, self.c = k, chunks[k]
            self.rows, self.order = self.c["rows"], self.c["order"]
            self.acc = bufs[k][0]
            self.halves = bufs[k][1:4]
            if self.c["tp"]:
                self.mid, self.got, self.got_far, self.got_x = bufs[k][4:8]
                self.fin = self.got
            else:
                self.fin = bufs[k][4]
            self.stages = []
            if self.c["tp"]:
                self.stages.append(("C", 0, None))
            size, seq, far = self.rows, [], self.c["tp"]
            for name in self.order:
                if name == "X":
                    far = False
                    self.stages.append(("X", size, list(seq)))
                else:
                    self.stages.append(("R", name, (list(seq), size, far)))
                    size //= 2
                    seq.append((name, size))
            for name in bits[3:]:
                self.stages.append(("B", name, (list(seq), size)))
            while seq:
                name, half = seq[-1]
                self.stages.append(("G", name, (list(seq), half)))
                seq.pop()

        def off(self, seq):
            total = 0
            for name, half in seq:
                total = total + bit_of(name) * half
            return total

        def copies(self, s):
            kind, name, info = self.stages[s]
            ss, rs = send_sems.at[self.k], recv_sems.at[self.k]
            if kind == "C":
                lo = self.c["part"] * self.rows
                blk = [r.at[pl.ds(lo, self.rows)] for r in self.c_src]
                return [
                    remote(blk[1], self.got, ss.at[0], rs.at[0], "tp", 1),
                    remote(blk[3], self.got_far, ss.at[1], rs.at[1], "tp", 1),
                    pltpu.make_async_copy(blk[0], self.acc, local_sems.at[self.k, 0]),
                    pltpu.make_async_copy(blk[2], self.mid, local_sems.at[self.k, 1]),
                ]
            if kind == "X":
                off = self.off(info)
                return [
                    remote(
                        rows_at(self.mid, off, name), rows_at(self.got_x, off, name),
                        ss.at[2], rs.at[2], "tp", 2,
                    )
                ]
            if kind == "R":
                seq, size, far = info
                half = size // 2
                off = self.off(seq) + (1 - bit_of(name)) * half
                slot = self.slot(s)
                out = [
                    remote(
                        rows_at(self.acc, off, half), self.halves[slot].at[0, pl.ds(0, half)],
                        ss.at[3 + s], rs.at[3 + s], "dp", name,
                    )
                ]
                if far:
                    out.append(
                        remote(
                            rows_at(self.mid, off, half),
                            self.halves[slot].at[1, pl.ds(0, half)],
                            ss.at[2 + 14], rs.at[2 + 14], "dp", name,
                        )
                    )
                return out
            if kind == "B":
                seq, size = info
                off = self.off(seq)
                slot = 2
                return [
                    remote(
                        rows_at(self.acc, off, size),
                        self.halves[slot].at[2 + bits.index(name) - 3, pl.ds(0, size)],
                        ss.at[3 + s], rs.at[3 + s], "dp", name,
                    )
                ]
            seq, half = info
            off = self.off(seq)
            here = rows_at(self.fin, off, half)
            return [remote(here, here, ss.at[3 + s], rs.at[3 + s], "dp", name)]

        def slot(self, s):
            return sum(1 for t in self.stages[:s] if t[0] == "R")

        def start(self, s):
            for cp in self.copies(s):
                cp.start()

        def finish(self, s):
            kind, name, info = self.stages[s]
            for cp in self.copies(s):
                cp.wait()
            if kind == "C":
                add_rows(self.acc, self.got, None, 0, 0, self.rows)
                add_rows(self.mid, self.got_far, None, 0, 0, self.rows)
            if kind == "X":
                off = self.off(info)
                add_rows(self.acc, self.got_x, None, off, off, name)
            if kind == "R":
                seq, size, far = info
                half = size // 2
                off = self.off(seq) + bit_of(name) * half
                got = self.halves[self.slot(s)]
                add_rows(self.acc, got, 0, off, 0, half)
                if far:
                    add_rows(self.mid, got, 1, off, 0, half)
            if kind == "B":
                seq, size = info
                add_rows(self.acc, self.halves[2], bits.index(name) - 1, self.off(seq), 0, size)

        def event(self, s):
            if s > 0:
                self.finish(s - 1)
            if s < len(self.stages):
                if self.stages[s][0] == "G" and self.stages[s - 1][0] != "G":
                    seq, size = self.stages[s][2]
                    here = pl.ds(pl.multiple_of(self.off(seq), 16), size)
                    self.fin[here] = self.acc[here]
                self.start(s)
            else:
                self.out_copy().start()

        def out_copy(self):
            return pltpu.make_async_copy(self.fin, outs[self.k], local_sems.at[self.k, 2])

        @property
        def n(self):
            return len(self.stages)

    work, at = [], 0
    for k, c in enumerate(chunks):
        ch = Chunk(k)
        if c["tp"]:
            if c["part"] == 0:
                at += tp_size
            ch.c_src = srcs[at - tp_size : at]
        work.append(ch)
    done = [0] * len(work)

    def go(k, upto=None):
        if done[k] <= work[k].n:
            work[k].event(done[k])
            done[k] += 1

    def turn(ks):
        for k in ks:
            go(k)

    ladder = [("tp", 1), ("tp", 2)] + [("dp", b) for b in bits]

    def small_copy(s):
        return remote(
            small_in, small_got.at[s], vec_send.at[0, s], vec_recv.at[0, s], *ladder[s]
        )

    def small_event(s):
        if s > 0:
            small_copy(s - 1).wait()
            got = small_got[s - 1]
            small_in[0:8] += got[0:8]
            if s == 1:
                small_in[8:9] += got[9:10]
                small_in[10:11] += got[11:12]
            elif s == 2:
                small_in[8:9] += got[10:11]
            else:
                small_in[8:9] += got[8:9]
        if s < len(ladder):
            small_copy(s).start()

    def do_copy(p):
        if p == 0:
            return pltpu.make_async_copy(do_ref.at[0], dos.at[0], do_local)
        return remote(do_ref.at[p], dos.at[p], do_send.at[p], do_recv.at[p], "tp", p)

    @pl.when(step == 0)
    def _():
        barrier = pltpu.get_barrier_semaphore()
        others = [("tp", 1), ("tp", 2), ("tp", 3)] + [("dp", b) for b in bits]
        for axis, bit in others:
            dev = (partner(dpi, bit), tpi) if axis == "dp" else (dpi, partner_any(tpi, bit))
            pl.semaphore_signal(
                barrier, inc=1, device_id=dev, device_id_type=pl.DeviceIdType.MESH
            )
        pl.semaphore_wait(barrier, len(others))
        for p in (2, 3, 1, 0):
            do_copy(p).start()
        for k in range(len(work)):
            if chunks[k]["tp"]:
                work[k].event(0)
        small_in[...] = small_ref[...]
        small_event(0)
        for hh in range(heads):
            ks[hh] = qkv_ref[1, hh].T
            vs[hh] = qkv_ref[2, hh].T
        dks[...] = jnp.zeros_like(dks)
        dvs[...] = jnp.zeros_like(dvs)

    for p in range(tp_size):

        @pl.when(step == p * heads)
        def _():
            do_copy(p).wait()

    lanes = pl.ds(pl.multiple_of(i * rows_dev, rows_dev), rows_dev)
    qt = qkv_ref[0, h, :, lanes] * jnp.bfloat16(scale)
    dot_t = dos[i, h]
    dsum = jnp.sum(
        dot_t.astype(F32) * o_ref[h, :, lanes].astype(F32), axis=0, keepdims=True
    )
    s = dot(ks[h], qt)
    p = jnp.exp(s - lse_ref[h, :, lanes])
    dp = dot(vs[h], dot_t)
    ds = (p * (dp - dsum)).astype(BF16)
    dqkv[0, h, :, lanes] = (dot(qkv_ref[1, h], ds) * scale).astype(BF16)
    dvs[h] += dot(p.astype(BF16), dot_t.T)
    dks[h] += dot(ds, qt.T)

    n_tp = [k for k in range(len(work)) if chunks[k]["tp"]]
    for k in n_tp:
        done[k] = 1
    small_done = [1]
    for st in range(steps):

        @pl.when(step == st)
        def _():
            if st < len(PLAN_STEPS):
                turn(PLAN_STEPS[st])
            if small_done[0] <= len(ladder):
                small_event(small_done[0])
                small_done[0] += 1

    @pl.when(step == steps - 1)
    def _():
        for hh in range(heads):
            dqkv[1, hh] = dks[hh].astype(BF16).T
            dqkv[2, hh] = dvs[hh].astype(BF16).T

        blk = 128

        def da_rows(p, store):
            def one(r, carry):
                lane = pl.ds(pl.multiple_of(p * rows_dev + r * blk, blk), blk)
                lhs = dqkv[:, :, :, lane].reshape(3 * heads * HD, blk)
                here = pl.ds(pl.multiple_of(r * blk, blk), blk)
                store(here, dot(lhs, wt_ref[...], ((0,), (0,))))
                return carry

            lax.fori_loop(0, rows_dev // blk, one, 0)

        def keep(slot):
            def store(here, val):
                da_far[slot, here] = val.astype(BF16)

            return store

        core3 = remote(da_far.at[0], da_core.at[0], da_send.at[0], da_recv.at[0], "tp", 1)
        core1 = remote(da_far.at[1], da_core.at[1], da_send.at[1], da_recv.at[1], "tp", 1)
        far = remote(da_far.at[2], da_across, da_send.at[2], da_recv.at[2], "tp", 2)
        da_rows(3, keep(0))
        core3.start()
        turn(PLAN_TAIL[0])
        da_rows(1, keep(1))
        core1.start()
        turn(PLAN_TAIL[1])
        core3.wait()

        def store2(here, val):
            da_far[2, here] = (val + da_core[0, here].astype(F32)).astype(BF16)

        da_rows(2, store2)
        far.start()
        turn(PLAN_TAIL[2])
        kq = [k for k in range(len(work)) if not chunks[k]["tp"]]
        nh = heads * HD
        spots = [(k, r) for k in kq for r in range(0, chunks[k]["rows"], nh)]
        for sec in range(3):
            k, r = spots[sec]
            lhs = dqkv[sec].reshape(nh, tp_size * rows_dev)
            work[k].acc[r : r + nh] = dot(lhs, rows_ref[...]).astype(BF16)
        k, r = spots[2]
        rest_rows = chunks[k]["rows"] - r - nh
        work[k].acc[r + nh :] = jnp.zeros((rest_rows, width), BF16)
        turn(kq)
        turn(PLAN_TAIL[3])
        core1.wait()

        def store0(here, val):
            tok_ref[here] = val + da_core[1, here].astype(F32)

        da_rows(0, store0)
        turn(PLAN_TAIL[4])
        turn(PLAN_WAIT)
        far.wait()
        last_own[...] = jnp.zeros_like(last_own)

        def norm_rows(r, carry):
            here = pl.ds(pl.multiple_of(r * blk, blk), blk)
            da = tok_ref[here] + da_across[here].astype(F32)
            hat, rstd = norm_parts(tiles_ref[here].astype(F32))
            tok_ref[here] = norm_back(hat, rstd, gain_ref[...], da)
            last_own[0:1] += jnp.sum(da * hat, axis=0, keepdims=True)
            last_own[1:2] += jnp.sum(da, axis=0, keepdims=True)
            return carry

        lax.fori_loop(0, rows_dev // blk, norm_rows, 0)

        def last_copy(s):
            if s < 2:
                return remote(
                    last_own.at[pl.ds(0, 8)], last_got.at[s, pl.ds(0, 8)],
                    vec_send.at[1, s], vec_recv.at[1, s], *ladder[s],
                )
            return remote(
                last_own, last_got.at[s], vec_send.at[1, s], vec_recv.at[1, s], *ladder[s]
            )

        last_copy(0).start()
        for st in range(len(ladder)):
            if st < len(PLAN_LAST):
                turn(PLAN_LAST[st])
            last_copy(st).wait()
            if st < 2:
                last_own[0:8] += last_got[st, 0:8]
                if st == 1:
                    last_own[8:] = onehot_ref[...] * last_own[1:2]
            else:
                last_own[...] += last_got[st]
            if st + 1 < len(ladder):
                last_copy(st + 1).start()
        while small_done[0] <= len(ladder):
            small_event(small_done[0])
            small_done[0] += 1
        turn(PLAN_LAST[-1])
        turn(PLAN_END)
        while any(done[k] <= work[k].n for k in range(len(work))):
            turn(range(len(work)))
        last_ref[...] = last_own[...]
        sum_ref[...] = small_in[...]
        kp = [k for k in n_tp if chunks[k].get("head")][0]
        nh, hr = chunks[kp]["head"]
        mine = work[kp].fin.at[pl.ds(nh, hr)]
        cps = [
            remote(mine, hg.at[p - 1], hg_send.at[p - 1], hg_recv.at[p - 1], "tp", p)
            for p in range(1, tp_size)
        ]
        for cp in cps:
            cp.start()
        head_out = [
            pltpu.make_async_copy(
                mine, rows_at(head_ref, tpi * hr, hr), do_local
            )
        ]
        head_out[0].start()
        for p, cp in enumerate(cps):
            cp.wait()
            out = pltpu.make_async_copy(
                hg.at[p], rows_at(head_ref, partner_any(tpi, p + 1) * hr, hr),
                local_sems.at[p, 3],
            )
            out.start()
            head_out.append(out)
        for out in head_out:
            out.wait()
        for ch in work:
            ch.out_copy().wait()


def partner_any(index, mask):
    if mask & 1:
        index = partner(index, 1)
    if mask & 2:
        index = partner(index, 2)
    return index


PLAN_STEPS = ((0, 1, 2), (3,), (4,), (), (0, 1, 2), (), (), (1,), (3, 4), (1,), (0,), (1, 2, 4))
PLAN_TAIL = ((0,), (), (1, 2, 3, 4), (0,), (1, 3))
PLAN_WAIT = (2, 6, 4, 5, 1)
PLAN_LAST = ((0,), (3, 5), (2, 6), (0, 4), (2, 3, 5), (0, 4, 6))
PLAN_END = (3, 2, 5, 4, 6, 5, 3, 6, 5, 6)


def attn_bwd(qkv, o, lse, do, rows, wt, tiles, gain, onehot, small, parts, mesh, scale):
    _, heads, _, frame = qkv.shape
    rows_dev, width = tiles.shape
    tp_size, dp_size = mesh.shape["tp"], mesh.shape["dp"]
    nbits = dp_size.bit_length() - 1
    half = width // 2
    ph_rows = parts[2][0].shape[0]
    chunks = [
        dict(tp=True, rows=half, part=0, order=[1, "X", 2, 4]),
        dict(tp=True, rows=half, part=1, order=["X", 1, 2, 4]),
        dict(tp=True, rows=half, part=0, order=[2, "X", 1, 4]),
        dict(tp=True, rows=half, part=1, order=[2, "X", 1, 4]),
        dict(tp=True, rows=ph_rows, part=0, order=["X", 1, 2, 4], head=(heads * HD, HEAD_ROWS)),
        dict(tp=False, rows=half, order=[2, 1, 4]),
        dict(tp=False, rows=256, order=[1, 2, 4]),
    ]
    n_k = len(chunks)
    scratch = [
        pltpu.VMEM((heads, frame, HD), BF16),
        pltpu.VMEM((heads, frame, HD), BF16),
        pltpu.VMEM((heads, frame, HD), F32),
        pltpu.VMEM((heads, frame, HD), F32),
        pltpu.VMEM((tp_size, heads, HD, rows_dev), BF16),
        pltpu.VMEM((3, heads, HD, frame), BF16),
        pltpu.VMEM((3, rows_dev, width), BF16),
        pltpu.VMEM((2, rows_dev, width), BF16),
        pltpu.VMEM((rows_dev, width), BF16),
        pltpu.VMEM((16, width), F32),
        pltpu.VMEM((2 + nbits, 16, width), F32),
        pltpu.VMEM((8 + onehot.shape[0], width), F32),
        pltpu.VMEM((2 + nbits, 8 + onehot.shape[0], width), F32),
        pltpu.VMEM((tp_size - 1, HEAD_ROWS, width), BF16),
    ]
    for c in chunks:
        r = c["rows"]
        scratch.append(pltpu.VMEM((r, width), BF16))
        scratch.append(pltpu.VMEM((2, r // 2, width), BF16))
        scratch.append(pltpu.VMEM((2, r // 4, width), BF16))
        scratch.append(pltpu.VMEM((2 + max(nbits - 3, 0), r // 8, width), BF16))
        if c["tp"]:
            scratch += [pltpu.VMEM((r, width), BF16)] * 4
        else:
            scratch.append(pltpu.VMEM((r, width), BF16))
    scratch += [
        pltpu.SemaphoreType.DMA((n_k, 17)),
        pltpu.SemaphoreType.DMA((n_k, 17)),
        pltpu.SemaphoreType.DMA((n_k, 4)),
        pltpu.SemaphoreType.DMA((tp_size,)),
        pltpu.SemaphoreType.DMA((tp_size,)),
        pltpu.SemaphoreType.DMA,
        pltpu.SemaphoreType.DMA((3,)),
        pltpu.SemaphoreType.DMA((3,)),
        pltpu.SemaphoreType.DMA((2, 2 + nbits)),
        pltpu.SemaphoreType.DMA((2, 2 + nbits)),
        pltpu.SemaphoreType.DMA((tp_size - 1,)),
        pltpu.SemaphoreType.DMA((tp_size - 1,)),
    ]
    any_spec = pl.BlockSpec(memory_space=pl.ANY)
    vmem = pl.BlockSpec(memory_space=pltpu.VMEM)
    flat = [x for group in parts for x in group]
    return pl.pallas_call(
        functools.partial(
            bwd_kernel, scale=scale, chunks=chunks, dp_size=dp_size, heads=heads,
            tp_size=tp_size, width=width,
        ),
        grid=(tp_size, heads),
        in_specs=[vmem, vmem, vmem, any_spec] + [vmem] * 6 + [any_spec] * len(flat),
        out_specs=[vmem, vmem, vmem, any_spec] + [any_spec] * n_k,
        out_shape=[
            jax.ShapeDtypeStruct((rows_dev, width), F32),
            jax.ShapeDtypeStruct((16, width), F32),
            jax.ShapeDtypeStruct((8 + onehot.shape[0], width), F32),
            jax.ShapeDtypeStruct((tp_size * HEAD_ROWS, width), BF16),
        ]
        + [jax.ShapeDtypeStruct((c["rows"], width), BF16) for c in chunks],
        scratch_shapes=scratch,
        compiler_params=pltpu.CompilerParams(
            vmem_limit_bytes=60 << 20, collective_id=1, has_side_effects=True
        ),
        cost_estimate=pl.CostEstimate(
            flops=60_000_000_000, bytes_accessed=30 << 20, transcendentals=heads * frame * frame
        ),
        name="attn_bwd",
    )(qkv, o, lse, do, rows, wt, tiles, gain, onehot, small, *flat)


def norm_parts(values):
    center = values - jnp.mean(values, axis=-1, keepdims=True)
    rstd = lax.rsqrt(jnp.mean(center * center, axis=-1, keepdims=True) + EPSILON)
    return center * rstd, rstd


def norm_back(hat, rstd, gain, grad):
    g = grad * gain
    return rstd * (
        g
        - jnp.mean(g, axis=-1, keepdims=True)
        - hat * jnp.mean(g * hat, axis=-1, keepdims=True)
    )


def gelu_parts(u):
    half = jnp.exp(-0.5 * u * u)
    t = 1.0 / (1.0 + (0.3275911 * 0.7071067811865476) * jnp.abs(u))
    poly = t * (
        0.254829592
        + t * (-0.284496736 + t * (1.421413741 + t * (-1.453152027 + t * 1.061405429)))
    )
    tail = 0.5 * poly * half
    cdf = jnp.where(u >= 0, 1.0 - tail, tail)
    return u * cdf, cdf + u * half * 0.3989422804014327


def make_body(mesh):
    dp_size, tp_size = mesh.shape["dp"], mesh.shape["tp"]

    def swap(x, axis, bit):
        size = dp_size if axis == "dp" else tp_size
        return lax.ppermute(x, axis, [(i, i ^ bit) for i in range(size)])

    def core(x):
        return swap(x, "tp", 1)

    def across(x):
        return swap(x, "tp", 2)

    def diag(x):
        return swap(x, "tp", 3)

    def my_bit(bit):
        return (lax.axis_index("dp") & bit) != 0

    def gather_tp(x):
        n = x.shape[0] // 2
        mine = my_bit(1)
        half = across(jnp.where(mine, x[n:], x[:n]))
        other = swap(half, "dp", 1)
        far = jnp.concatenate([jnp.where(mine, other, half), jnp.where(mine, half, other)], axis=0)
        return [x, core(x), far, core(far)]

    def body(
        tile_vectors,
        snapshot_horizon_slot,
        horizon_sample_tally,
        specialist_outlooks,
        early_layernorm_scale,
        early_layernorm_shift,
        horizon_vectors,
        triple_head_matrix,
        attending_matrix,
        attending_offset,
        later_layernorm_scale,
        later_layernorm_shift,
        widening_matrix,
        widening_offset,
        narrowing_matrix,
        narrowing_offset,
        router_matrix,
        router_offset,
        adjuster_matrix,
        adjuster_offset,
        combined_loss_slope,
    ):
        rows_dev, width = tile_vectors.shape
        heads = triple_head_matrix.shape[2] // HD
        rows_frame = rows_dev * tp_size
        fields = adjuster_matrix.shape[1]
        sites = combined_loss_slope.shape[1]
        scale_val = HD ** (-0.5)
        tp_index = lax.axis_index("tp")
        lead = snapshot_horizon_slot[0]
        embed = lax.dynamic_slice_in_dim(horizon_vectors, lead, 1, 0)
        row_scale = lax.rsqrt(
            lax.dynamic_slice_in_dim(horizon_sample_tally, lead, 1, 0).astype(F32)
        )[0]
        residual = tile_vectors.astype(F32)

        hat1, rstd1 = norm_parts(residual)
        attn_own = (hat1 * early_layernorm_scale + early_layernorm_shift + embed).astype(BF16)
        rows2 = across(attn_own)
        rows1 = core(attn_own)
        rows3 = core(rows2)
        rows2, rows3, triple_w, proj_w, wide_w, narrow_w = lax.optimization_barrier(
            (rows2, rows3, triple_head_matrix, attending_matrix, widening_matrix, narrowing_matrix)
        )
        attn_rows = jnp.concatenate([attn_own, rows1, rows2, rows3], axis=0)

        proj_all = gather_tp(proj_w)
        wide_all = gather_tp(wide_w)
        narrow_all = gather_tp(narrow_w)
        off2 = across(widening_offset)
        off_all = [widening_offset, core(widening_offset), off2, core(off2)]

        qkv = jnp.einsum(
            "sdh,td->sht", triple_w, attn_rows, preferred_element_type=F32
        ).astype(BF16)
        qkv = qkv.reshape(3, heads, HD, rows_frame)
        o_heads, lse = attn_fwd(qkv, scale_val, min(512, rows_frame))

        slope = combined_loss_slope.astype(F32)
        expert_dot = jnp.stack(
            [
                jnp.sum(specialist_outlooks[e].astype(F32) * slope, axis=1)
                for e in range(EXPERTS)
            ]
        )
        slope_sum = jnp.sum(slope, axis=1)

        o_flat = o_heads.reshape(heads * HD, rows_frame)
        ob = [o_flat[:, p * rows_dev : (p + 1) * rows_dev] for p in range(tp_size)]
        o_own = jnp.concatenate([ob[0], core(ob[1]), across(ob[2]), diag(ob[3])], axis=0)
        proj_cat = jnp.concatenate(proj_all, axis=0)
        x1 = residual + dot(o_own, proj_cat, ((0,), (0,))) + attending_offset
        hat2, rstd2 = norm_parts(x1)
        c_low = (hat2 * later_layernorm_scale + later_layernorm_shift).astype(BF16)
        acts, slopes = [], []
        for p in range(tp_size):
            m, d = gelu_parts(dot(c_low, wide_all[p]) + off_all[p])
            acts.append(m.astype(BF16))
            slopes.append(d)
        mlp = dot(acts[0], narrow_all[0])
        for p in range(1, tp_size):
            mlp = mlp + dot(acts[p], narrow_all[p])
        x2 = x1 + mlp + narrowing_offset
        h_low = x2.astype(BF16)
        logits = dot(router_matrix, h_low, ((0,), (1,))) + router_offset[:, None]
        corr = (dot(adjuster_matrix, h_low, ((0,), (1,))) + adjuster_offset[:, None]) * row_scale
        logits = logits.reshape(EXPERTS, fields, rows_dev)
        top = jnp.max(logits, axis=0, keepdims=True)
        raised = jnp.exp(logits - top)
        gates = raised / jnp.sum(raised, axis=0, keepdims=True)
        mixed = jnp.sum(gates * expert_dot, axis=0, keepdims=True)
        dlog = (gates * (expert_dot - mixed)).astype(BF16).reshape(EXPERTS * fields, rows_dev)
        dcorr = (slope_sum * row_scale).astype(BF16)

        head_grads = jnp.concatenate([dlog, dcorr], axis=0)
        head_w = jnp.concatenate([router_matrix, adjuster_matrix], axis=1)
        dx2 = dot(head_grads, head_w, ((0,), (1,)))
        dz = dx2.astype(BF16)
        d_narrow = [dot(acts[p], dz, ((0,), (0,))).astype(BF16) for p in range(tp_size)]
        dus = [
            (dot(dz, narrow_all[p], ((1,), (1,))) * slopes[p]).astype(BF16) for p in range(tp_size)
        ]
        d_wide = [dot(c_low, dus[p], ((0,), (0,))).astype(BF16) for p in range(tp_size)]
        dc = dot(dus[0], wide_all[0], ((1,), (1,)))
        for p in range(1, tp_size):
            dc = dc + dot(dus[p], wide_all[p], ((1,), (1,)))
        dx1 = dx2 + norm_back(hat2, rstd2, later_layernorm_scale, dc)
        dy = dx1.astype(BF16)
        do_all = dot(proj_cat, dy, ((1,), (1,))).astype(BF16)
        nh = heads * HD
        do_all = do_all.reshape(tp_size, heads, HD, rows_dev)
        blended = (corr)[:, None, :]
        for e in range(EXPERTS):
            blended = blended + gates[e][:, None, :] * specialist_outlooks[e].astype(F32)

        d_proj = dot(o_own, dy, ((1,), (0,))).astype(BF16)
        d_head = dot(head_grads, h_low).astype(BF16)
        d_head = jnp.pad(d_head, ((0, tp_size * HEAD_ROWS - d_head.shape[0]), (0, 0)))
        dproj_parts = []
        ph_rows = -(-(nh + HEAD_ROWS) // 128) * 128
        for p in range(tp_size):
            head_blk = lax.dynamic_slice_in_dim(d_head, (tp_index ^ p) * HEAD_ROWS, HEAD_ROWS, 0)
            dproj_parts.append(
                jnp.concatenate(
                    [
                        d_proj[p * nh : (p + 1) * nh],
                        head_blk,
                        jnp.zeros((ph_rows - nh - HEAD_ROWS, width), BF16),
                    ],
                    axis=0,
                )
            )

        head_bias = jnp.sum(head_grads.astype(F32), axis=1)
        head_bias = jnp.pad(head_bias, (0, width - head_bias.shape[0]))
        zero = jnp.zeros((width,), F32)
        small = jnp.stack(
            [
                jnp.sum(dx2, axis=0),
                jnp.sum(dc * hat2, axis=0),
                jnp.sum(dc, axis=0),
                jnp.sum(dx1, axis=0),
                head_bias,
                zero,
                zero,
                zero,
            ]
            + [jnp.sum(dus[p].astype(F32), axis=0) for p in range(tp_size)]
            + [zero] * 4
        )
        leads = horizon_vectors.shape[0]
        onehot = (jnp.arange(leads, dtype=jnp.int32) == lead).astype(F32)[:, None]
        w_t = jnp.transpose(triple_head_matrix, (0, 2, 1)).reshape(3 * nh, width)
        (token_part, small, table, head_sum, n0, n1, i0, i1, ph, q0, q1) = attn_bwd(
            qkv, o_heads, lse, do_all, attn_rows, w_t, tile_vectors,
            early_layernorm_scale[None, :], onehot, small,
            [d_narrow, d_wide, dproj_parts], mesh, scale_val,
        )
        tokens_grad = dx1 + token_part
        narrow_sum = jnp.concatenate([n0, n1], axis=0).astype(F32)
        wide_sum = jnp.concatenate([i0, i1], axis=0).astype(F32)
        proj_weight_grad = ph[:nh].astype(F32)
        head_sum = head_sum.T.astype(F32)
        gate_weight_grad = head_sum[:, : EXPERTS * fields]
        correct_weight_grad = head_sum[:, EXPERTS * fields : (EXPERTS + 1) * fields]
        q_all = jnp.concatenate([q0, q1], axis=0)[: 3 * nh]
        qkv_sum = jnp.transpose(q_all.reshape(3, nh, width), (0, 2, 1)).astype(F32)
        in_bias_grad = small[8]

        return (
            blended,
            tokens_grad,
            table[0],
            table[1],
            table[8:],
            qkv_sum,
            proj_weight_grad,
            small[3],
            small[1],
            small[2],
            wide_sum,
            in_bias_grad,
            narrow_sum,
            small[0],
            gate_weight_grad,
            small[4, : EXPERTS * fields],
            correct_weight_grad,
            small[4, EXPERTS * fields : (EXPERTS + 1) * fields],
        )

    return body


def solution(mesh):
    return jax.shard_map(
        make_body(mesh),
        mesh=mesh,
        in_specs=(
            P(("dp", "tp"), None),
            P("dp"),
            P(),
            P(None, None, None, ("dp", "tp")),
            P(),
            P(),
            P(),
            P(None, None, "tp"),
            P("tp", None),
            P(),
            P(),
            P(),
            P(None, "tp"),
            P("tp"),
            P("tp", None),
            P(),
            P(),
            P(),
            P(),
            P(),
            P(None, None, ("dp", "tp")),
        ),
        out_specs=(
            P(None, None, ("dp", "tp")),
            P(("dp", "tp"), None),
            P(),
            P(),
            P(),
            P(None, None, "tp"),
            P("tp", None),
            P(),
            P(),
            P(),
            P(None, "tp"),
            P("tp"),
            P("tp", None),
            P(),
            P(),
            P(),
            P(),
            P(),
        ),
        check_vma=False,
    )
```

```python
import functools
import jax
import jax.numpy as jnp
from jax import lax
from jax.experimental import pallas as pl
from jax.experimental.pallas import tpu as pltpu
from jax.sharding import PartitionSpec as P

HD = 64
EXPERTS = 3
HEAD_ROWS = 80
EPSILON = 1e-05
F32 = jnp.float32
BF16 = jnp.bfloat16


def dot(a, b, dims=((1,), (0,))):
    return lax.dot_general(a, b, (dims, ((), ())), preferred_element_type=F32)


def fwd_kernel(
    tiles_ref, gain_ref, shift_ref, wt_ref, proj_ref, wide_ref, narrow_ref, exp_ref, slope_ref,
    rows_out, qkv_ref, o_ref, lse_ref, own_out, dots_ref, proj_all, wide_all, narrow_all,
    rows_ref, own_ref, out_sem, ks, stream, stream_g, stream_sem, row_send, row_recv, o_send, o_recv, o_local,
    w_send, w_recv, *, scale, dp_size, tp_size, heads
):
    i, h = pl.program_id(0), pl.program_id(1)
    steps = tp_size * heads
    step = i * heads + h
    dpi, tpi = lax.axis_index("dp"), lax.axis_index("tp")
    rows_dev, width = tiles_ref.shape
    piece = rows_dev // 2
    mine = lax.rem(dpi, 2)

    def remote(src, dst, ssem, rsem, axis, bit):
        dev = (partner(dpi, bit), tpi) if axis == "dp" else (dpi, partner_any(tpi, bit))
        return pltpu.make_async_remote_copy(
            src_ref=src, dst_ref=dst, send_sem=ssem, recv_sem=rsem,
            device_id=dev, device_id_type=pl.DeviceIdType.MESH,
        )

    def row_copy(kind, c):
        a, b, bit = ((0, 1, 1), (0, 2, 2), (2, 3, 1))[kind]
        here = pl.ds(c * piece, piece)
        return remote(
            rows_ref.at[a, here], rows_ref.at[b, here],
            row_send.at[kind, c], row_recv.at[kind, c], "tp", bit,
        )

    parts = []
    for src, dst, cuts in ((proj_ref, proj_all, 1), (wide_ref, wide_all, 2), (narrow_ref, narrow_all, 2)):
        n = src.shape[0] // cuts
        for c in range(cuts):
            parts.append((src, dst, c * n, n // 2))

    def w_half(part, whose):
        return pl.ds(pl.multiple_of(part[2] + whose * part[3], 16), part[3])

    def w_far(n):
        src, dst, _, _ = parts[n]
        rows = w_half(parts[n], mine)
        return remote(
            src.at[rows], dst.at[1, rows], w_send.at[n, 0], w_recv.at[n, 0], "tp", 2
        )

    def w_side(n):
        dst = parts[n][1]
        rows = w_half(parts[n], mine)
        here = dst.at[1, rows]
        return remote(here, here, w_send.at[n, 1], w_recv.at[n, 1], "dp", 1)

    def w_fwd(n, second):
        dst = parts[n][1]
        rows = w_half(parts[n], 1 - mine if second else mine)
        k = 3 if second else 2
        return remote(
            dst.at[1, rows], dst.at[2, rows], w_send.at[n, k], w_recv.at[n, k], "tp", 1
        )

    def w_near(n):
        src, dst, lo, half = parts[n]
        rows = pl.ds(lo, 2 * half)
        return remote(src.at[rows], dst.at[0, rows], w_send.at[n, 4], w_recv.at[n, 4], "tp", 1)

    def o_copy(p):
        if p == 0:
            return pltpu.make_async_copy(o_ref.at[0], own_ref.at[0], o_local)
        return remote(o_ref.at[p], own_ref.at[p], o_send.at[p], o_recv.at[p], "tp", p)

    fields, sites = slope_ref.shape[0], slope_ref.shape[1]
    per = stream.shape[2]
    groups = fields // per
    depth = stream.shape[0]

    def stream_copies(g):
        slot = lax.rem(g, depth)
        at = pl.ds(g * per, per)
        return (
            pltpu.make_async_copy(
                exp_ref.at[:, at], stream.at[slot], stream_sem.at[slot, 0]
            ),
            pltpu.make_async_copy(
                slope_ref.at[at], stream_g.at[slot], stream_sem.at[slot, 1]
            ),
        )

    @pl.when(step == 0)
    def _():
        barrier = pltpu.get_barrier_semaphore()
        others = [("tp", 1), ("tp", 2), ("tp", 3), ("dp", 1)]
        for axis, bit in others:
            dev = (partner(dpi, bit), tpi) if axis == "dp" else (dpi, partner_any(tpi, bit))
            pl.semaphore_signal(
                barrier, inc=1, device_id=dev, device_id_type=pl.DeviceIdType.MESH
            )
        for g in range(min(depth - 1, groups)):
            for cp in stream_copies(g):
                cp.start()
        blk = 64

        def norm_rows(r, carry):
            here = pl.ds(pl.multiple_of(r * blk, blk), blk)
            hat, _ = norm_parts(tiles_ref[here].astype(F32))
            rows_ref[0, here] = (hat * gain_ref[...] + shift_ref[...]).astype(BF16)
            return carry

        half = piece // blk
        lax.fori_loop(0, half, norm_rows, 0)
        pl.semaphore_wait(barrier, len(others))
        row_copy(1, 0).start()
        lax.fori_loop(half, 2 * half, norm_rows, 0)
        row_copy(1, 1).start()
        row_copy(0, 0).start()
        row_copy(0, 1).start()

        def contract(g, carry):
            @pl.when(g + depth - 1 < groups)
            def _():
                for cp in stream_copies(g + depth - 1):
                    cp.start()

            for cp in stream_copies(g):
                cp.wait()
            slot = lax.rem(g, depth)
            for j in range(per):
                slope = stream_g[slot, j].astype(F32)
                for e in range(EXPERTS):
                    dots_ref[e, pl.ds(g * per + j, 1)] = jnp.sum(
                        stream[slot, e, j].astype(F32) * slope, axis=0, keepdims=True
                    )
                dots_ref[EXPERTS, pl.ds(g * per + j, 1)] = jnp.sum(slope, axis=0, keepdims=True)
            return carry

        dots_ref[...] = jnp.zeros_like(dots_ref)
        lax.fori_loop(0, groups, contract, 0)

        def project(p):
            lane = pl.ds(p * rows_dev, rows_dev)
            for s in range(3):
                part = dot(wt_ref[s], rows_ref[p], ((1,), (1,))).astype(BF16)
                qkv_ref[s, :, :, lane] = part.reshape(heads, HD, rows_dev)
            for hh in range(heads):
                ks[hh, lane] = qkv_ref[1, hh, :, lane].T

        project(0)
        for c in range(2):
            row_copy(0, c).wait()
        project(1)
        for c in range(2):
            row_copy(1, c).wait()
            row_copy(2, c).start()
        w_far(0).start()
        w_far(1).start()
        project(2)
        for c in range(2):
            row_copy(2, c).wait()
        for n in range(len(parts)):
            w_near(n).start()
        rows_copy = pltpu.make_async_copy(rows_ref, rows_out, out_sem.at[0])
        rows_copy.start()
        project(3)

    p = lax.rem(i + 2, tp_size)
    lanes = pl.ds(pl.multiple_of(p * rows_dev, rows_dev), rows_dev)
    q = qkv_ref[0, h, :, lanes] * jnp.bfloat16(scale)
    s = dot(ks[h], q)
    m = jnp.max(s, axis=0, keepdims=True)
    e = jnp.exp(s - m)
    l = jnp.sum(e, axis=0, keepdims=True)
    o_ref[p, h] = (dot(qkv_ref[2, h], e.astype(BF16)) / l).astype(BF16)
    lse_ref[p, h] = m + jnp.log(l)

    seq = {}

    def after(st, *what):
        seq.setdefault(min(st, steps - 1), []).extend(what)

    arrive = (1, 3, 6, 9, 11)
    side = (3, 7, 10, 11, 11)
    for n in range(len(parts)):
        after(arrive[n], ("far", n))
    for n in range(len(parts)):
        after(side[n], ("side", n))
    for st, what in seq.items():

        @pl.when(step == st)
        def _():
            for kind, n in what:
                if kind == "far":
                    w_far(n).wait()
                    if n + 2 < len(parts):
                        w_far(n + 2).start()
                    w_side(n).start()
                    w_fwd(n, False).start()
                else:
                    w_side(n).wait()
                    w_fwd(n, True).start()

    for k in range(tp_size):

        @pl.when(step == k * heads + heads - 1)
        def _():
            o_copy((k + 2) % tp_size).start()

    @pl.when(step == steps - 1)
    def _():
        for k in range(tp_size):
            o_copy(k).wait()
        own_copy = pltpu.make_async_copy(own_ref, own_out, out_sem.at[1])
        own_copy.start()
        for n in range(len(parts)):
            w_near(n).wait()
            w_fwd(n, False).wait()
            w_fwd(n, True).wait()
        own_copy.wait()
        pltpu.make_async_copy(rows_ref, rows_out, out_sem.at[0]).wait()


def attn_fwd(tiles, gain, shift, wt, proj, wide, narrow, experts, slope, mesh, scale):
    rows_dev, width = tiles.shape
    heads = proj.shape[0] // HD
    tp_size, dp_size = mesh.shape["tp"], mesh.shape["dp"]
    frame = tp_size * rows_dev
    fields, sites = slope.shape[0], slope.shape[1]
    per = 3 if fields % 3 == 0 else 1
    depth = 4
    any_spec = pl.BlockSpec(memory_space=pl.ANY)
    vmem = pl.BlockSpec(memory_space=pltpu.VMEM)
    return pl.pallas_call(
        functools.partial(
            fwd_kernel, scale=scale, dp_size=dp_size, tp_size=tp_size, heads=heads
        ),
        grid=(tp_size, heads),
        in_specs=[vmem] * 4 + [any_spec] * 5,
        out_specs=[any_spec] + [vmem] * 3 + [any_spec, vmem] + [any_spec] * 3,
        out_shape=[
            jax.ShapeDtypeStruct((tp_size, rows_dev, width), BF16),
            jax.ShapeDtypeStruct((3, heads, HD, frame), BF16),
            jax.ShapeDtypeStruct((tp_size, heads, HD, rows_dev), BF16),
            jax.ShapeDtypeStruct((tp_size, heads, 1, rows_dev), F32),
            jax.ShapeDtypeStruct((tp_size, heads, HD, rows_dev), BF16),
            jax.ShapeDtypeStruct((EXPERTS + 1, HEAD_ROWS, rows_dev), F32),
            jax.ShapeDtypeStruct((tp_size - 1,) + proj.shape, BF16),
            jax.ShapeDtypeStruct((tp_size - 1,) + wide.shape, BF16),
            jax.ShapeDtypeStruct((tp_size - 1,) + narrow.shape, BF16),
        ],
        scratch_shapes=[
            pltpu.VMEM((tp_size, rows_dev, width), BF16),
            pltpu.VMEM((tp_size, heads, HD, rows_dev), BF16),
            pltpu.SemaphoreType.DMA((2,)),
            pltpu.VMEM((heads, frame, HD), BF16),
            pltpu.VMEM((depth, EXPERTS, per, sites, rows_dev), BF16),
            pltpu.VMEM((depth, per, sites, rows_dev), BF16),
            pltpu.SemaphoreType.DMA((depth, 2)),
            pltpu.SemaphoreType.DMA((3, 2)),
            pltpu.SemaphoreType.DMA((3, 2)),
            pltpu.SemaphoreType.DMA((tp_size,)),
            pltpu.SemaphoreType.DMA((tp_size,)),
            pltpu.SemaphoreType.DMA,
            pltpu.SemaphoreType.DMA((5, 5)),
            pltpu.SemaphoreType.DMA((5, 5)),
        ],
        compiler_params=pltpu.CompilerParams(
            vmem_limit_bytes=56 << 20, collective_id=0, has_side_effects=True
        ),
        cost_estimate=pl.CostEstimate(
            flops=30_000_000_000, bytes_accessed=40 << 20, transcendentals=heads * frame * frame
        ),
        name="attn_fwd",
    )(tiles, gain, shift, wt, proj, wide, narrow, experts, slope)


def partner(index, bit):
    return index + bit - 2 * bit * lax.rem(lax.div(index, bit), 2)


def rows_at(ref, start, size):
    return ref.at[pl.ds(pl.multiple_of(start, 16), size)]


def add_rows(dst, src, lead, dst_off, src_off, size):
    step = 48 if size % 48 == 0 else 32

    def one(r, carry):
        here = pl.ds(pl.multiple_of(dst_off + r * step, 16), step)
        there = pl.ds(pl.multiple_of(src_off + r * step, 16), step)
        got = src[there] if lead is None else src[lead, there]
        dst[here] = (dst[here].astype(F32) + got.astype(F32)).astype(BF16)
        return carry

    lax.fori_loop(0, size // step, one, 0)


def bwd_kernel(
    qkv_ref, o_ref, lse_ref, do_ref, rows_ref, wt_ref, tiles_ref, gain_ref, onehot_ref, small_ref,
    *rest, scale, chunks, dp_size, heads, tp_size, width
):
    n_src = sum(1 for c in chunks if c["tp"] and c["part"] == 0)
    srcs = rest[:n_src]
    tok_ref, sum_ref, last_ref, head_ref = rest[n_src : n_src + 4]
    n_out = n_src + 4 + len(chunks)
    outs = rest[n_src + 4 : n_out]
    (
        ks, vs, dks, dvs, dos, dqkv, da_far, da_core, da_across,
        small_in, small_got, last_own, last_got, hg,
    ) = rest[n_out : n_out + 14]
    per = rest[n_out + 14 : -12]
    (
        send_sems, recv_sems, local_sems, do_send, do_recv, do_local, da_send, da_recv,
        vec_send, vec_recv, hg_send, hg_recv,
    ) = rest[-12:]
    i, h = pl.program_id(0), pl.program_id(1)
    steps = tp_size * heads
    step = i * heads + h
    dpi, tpi = lax.axis_index("dp"), lax.axis_index("tp")
    rows_dev = dos.shape[3]
    bits = [1 << b for b in range(dp_size.bit_length() - 1)]

    def remote(src, dst, ssem, rsem, axis, bit):
        dev = (partner(dpi, bit), tpi) if axis == "dp" else (dpi, partner_any(tpi, bit))
        return pltpu.make_async_remote_copy(
            src_ref=src, dst_ref=dst, send_sem=ssem, recv_sem=rsem,
            device_id=dev, device_id_type=pl.DeviceIdType.MESH,
        )

    def bit_of(bit):
        return lax.rem(lax.div(dpi, bit), 2)

    bufs, at = [], 0
    for c in chunks:
        n = 8 if c["tp"] else 5
        bufs.append(per[at : at + n])
        at += n

    class Chunk:
        def __init__(self, k):
            self.k, self.c = k, chunks[k]
            self.rows, self.order = self.c["rows"], self.c["order"]
            self.acc = bufs[k][0]
            self.halves = bufs[k][1:4]
            if self.c["tp"]:
                self.mid, self.got, self.got_far, self.got_x = bufs[k][4:8]
                self.fin = self.got
            else:
                self.fin = bufs[k][4]
            self.stages = []
            if self.c["tp"]:
                self.stages.append(("C", 0, None))
            size, seq, far = self.rows, [], self.c["tp"]
            for name in self.order:
                if name == "X":
                    far = False
                    self.stages.append(("X", size, list(seq)))
                else:
                    self.stages.append(("R", name, (list(seq), size, far)))
                    size //= 2
                    seq.append((name, size))
            for name in bits[3:]:
                self.stages.append(("B", name, (list(seq), size)))
            while seq:
                name, half = seq[-1]
                self.stages.append(("G", name, (list(seq), half)))
                seq.pop()

        def off(self, seq):
            total = 0
            for name, half in seq:
                total = total + bit_of(name) * half
            return total

        def copies(self, s):
            kind, name, info = self.stages[s]
            ss, rs = send_sems.at[self.k], recv_sems.at[self.k]
            if kind == "C":
                lo = self.c["part"] * self.rows
                blk = [self.c_src.at[p, pl.ds(lo, self.rows)] for p in range(tp_size)]
                return [
                    remote(blk[1], self.got, ss.at[0], rs.at[0], "tp", 1),
                    remote(blk[3], self.got_far, ss.at[1], rs.at[1], "tp", 1),
                    pltpu.make_async_copy(blk[0], self.acc, local_sems.at[self.k, 0]),
                    pltpu.make_async_copy(blk[2], self.mid, local_sems.at[self.k, 1]),
                ]
            if kind == "X":
                off = self.off(info)
                return [
                    remote(
                        rows_at(self.mid, off, name), rows_at(self.got_x, off, name),
                        ss.at[2], rs.at[2], "tp", 2,
                    )
                ]
            if kind == "R":
                seq, size, far = info
                half = size // 2
                off = self.off(seq) + (1 - bit_of(name)) * half
                slot = self.slot(s)
                out = [
                    remote(
                        rows_at(self.acc, off, half), self.halves[slot].at[0, pl.ds(0, half)],
                        ss.at[3 + s], rs.at[3 + s], "dp", name,
                    )
                ]
                if far:
                    out.append(
                        remote(
                            rows_at(self.mid, off, half),
                            self.halves[slot].at[1, pl.ds(0, half)],
                            ss.at[2 + 14], rs.at[2 + 14], "dp", name,
                        )
                    )
                return out
            if kind == "B":
                seq, size = info
                off = self.off(seq)
                slot = 2
                return [
                    remote(
                        rows_at(self.acc, off, size),
                        self.halves[slot].at[2 + bits.index(name) - 3, pl.ds(0, size)],
                        ss.at[3 + s], rs.at[3 + s], "dp", name,
                    )
                ]
            seq, half = info
            off = self.off(seq)
            here = rows_at(self.fin, off, half)
            return [remote(here, here, ss.at[3 + s], rs.at[3 + s], "dp", name)]

        def slot(self, s):
            return sum(1 for t in self.stages[:s] if t[0] == "R")

        def start(self, s):
            for cp in self.copies(s):
                cp.start()

        def finish(self, s):
            kind, name, info = self.stages[s]
            for cp in self.copies(s):
                cp.wait()
            if kind == "C":
                add_rows(self.acc, self.got, None, 0, 0, self.rows)
                add_rows(self.mid, self.got_far, None, 0, 0, self.rows)
            if kind == "X":
                off = self.off(info)
                add_rows(self.acc, self.got_x, None, off, off, name)
            if kind == "R":
                seq, size, far = info
                half = size // 2
                off = self.off(seq) + bit_of(name) * half
                got = self.halves[self.slot(s)]
                add_rows(self.acc, got, 0, off, 0, half)
                if far:
                    add_rows(self.mid, got, 1, off, 0, half)
            if kind == "B":
                seq, size = info
                add_rows(self.acc, self.halves[2], bits.index(name) - 1, self.off(seq), 0, size)

        def event(self, s):
            if s > 0:
                self.finish(s - 1)
            if s < len(self.stages):
                if self.stages[s][0] == "G" and self.stages[s - 1][0] != "G":
                    seq, size = self.stages[s][2]
                    here = pl.ds(pl.multiple_of(self.off(seq), 16), size)
                    self.fin[here] = self.acc[here]
                self.start(s)
            else:
                self.out_copy().start()

        def out_copy(self):
            return pltpu.make_async_copy(self.fin, outs[self.k], local_sems.at[self.k, 2])

        @property
        def n(self):
            return len(self.stages)

    work, at = [], 0
    for k, c in enumerate(chunks):
        ch = Chunk(k)
        if c["tp"]:
            if c["part"] == 0:
                at += 1
            ch.c_src = srcs[at - 1]
        work.append(ch)
    done = [0] * len(work)

    def go(k, upto=None):
        if done[k] <= work[k].n:
            work[k].event(done[k])
            done[k] += 1

    def turn(ks):
        for k in ks:
            go(k)

    ladder = [("tp", 1), ("tp", 2)] + [("dp", b) for b in bits]

    def small_copy(s):
        return remote(
            small_in, small_got.at[s], vec_send.at[0, s], vec_recv.at[0, s], *ladder[s]
        )

    def small_event(s):
        if s > 0:
            small_copy(s - 1).wait()
            got = small_got[s - 1]
            small_in[0:8] += got[0:8]
            if s == 1:
                small_in[8:9] += got[9:10]
                small_in[10:11] += got[11:12]
            elif s == 2:
                small_in[8:9] += got[10:11]
            else:
                small_in[8:9] += got[8:9]
        if s < len(ladder):
            small_copy(s).start()

    def do_copy(p):
        if p == 0:
            return pltpu.make_async_copy(do_ref.at[0], dos.at[0], do_local)
        return remote(do_ref.at[p], dos.at[p], do_send.at[p], do_recv.at[p], "tp", p)

    @pl.when(step == 0)
    def _():
        barrier = pltpu.get_barrier_semaphore()
        others = [("tp", 1), ("tp", 2), ("tp", 3)] + [("dp", b) for b in bits]
        for axis, bit in others:
            dev = (partner(dpi, bit), tpi) if axis == "dp" else (dpi, partner_any(tpi, bit))
            pl.semaphore_signal(
                barrier, inc=1, device_id=dev, device_id_type=pl.DeviceIdType.MESH
            )
        pl.semaphore_wait(barrier, len(others))
        for p in (2, 3, 1, 0):
            do_copy(p).start()
        for k in range(len(work)):
            if chunks[k]["tp"]:
                work[k].event(0)
        small_in[...] = small_ref[...]
        small_event(0)
        for hh in range(heads):
            ks[hh] = qkv_ref[1, hh].T
            vs[hh] = qkv_ref[2, hh].T
        dks[...] = jnp.zeros_like(dks)
        dvs[...] = jnp.zeros_like(dvs)

    for p in range(tp_size):

        @pl.when(step == p * heads)
        def _():
            do_copy(p).wait()

    lanes = pl.ds(pl.multiple_of(i * rows_dev, rows_dev), rows_dev)
    qt = qkv_ref[0, h, :, lanes] * jnp.bfloat16(scale)
    dot_t = dos[i, h]
    dsum = jnp.sum(
        dot_t.astype(F32) * o_ref[i, h].astype(F32), axis=0, keepdims=True
    )
    s = dot(ks[h], qt)
    p = jnp.exp(s - lse_ref[i, h])
    dp = dot(vs[h], dot_t)
    ds = (p * (dp - dsum)).astype(BF16)
    dqkv[0, h, :, lanes] = (dot(qkv_ref[1, h], ds) * scale).astype(BF16)
    dvs[h] += dot(p.astype(BF16), dot_t.T)
    dks[h] += dot(ds, qt.T)

    n_tp = [k for k in range(len(work)) if chunks[k]["tp"]]
    for k in n_tp:
        done[k] = 1
    small_done = [1]
    for st in range(steps):

        @pl.when(step == st)
        def _():
            if st < len(PLAN_STEPS):
                turn(PLAN_STEPS[st])
            if small_done[0] <= len(ladder):
                small_event(small_done[0])
                small_done[0] += 1

    @pl.when(step == steps - 1)
    def _():
        for hh in range(heads):
            dqkv[1, hh] = dks[hh].astype(BF16).T
            dqkv[2, hh] = dvs[hh].astype(BF16).T

        blk = 128

        def da_rows(p, store):
            def one(r, carry):
                lane = pl.ds(pl.multiple_of(p * rows_dev + r * blk, blk), blk)
                lhs = dqkv[:, :, :, lane].reshape(3 * heads * HD, blk)
                here = pl.ds(pl.multiple_of(r * blk, blk), blk)
                store(here, dot(lhs, wt_ref[...], ((0,), (0,))))
                return carry

            lax.fori_loop(0, rows_dev // blk, one, 0)

        def keep(slot):
            def store(here, val):
                da_far[slot, here] = val.astype(BF16)

            return store

        core3 = remote(da_far.at[0], da_core.at[0], da_send.at[0], da_recv.at[0], "tp", 1)
        core1 = remote(da_far.at[1], da_core.at[1], da_send.at[1], da_recv.at[1], "tp", 1)
        far = remote(da_far.at[2], da_across, da_send.at[2], da_recv.at[2], "tp", 2)
        da_rows(3, keep(0))
        core3.start()
        turn(PLAN_TAIL[0])
        da_rows(1, keep(1))
        core1.start()
        turn(PLAN_TAIL[1])
        core3.wait()

        def store2(here, val):
            da_far[2, here] = (val + da_core[0, here].astype(F32)).astype(BF16)

        da_rows(2, store2)
        far.start()
        turn(PLAN_TAIL[2])
        kq = [k for k in range(len(work)) if not chunks[k]["tp"]]
        nh = heads * HD
        spots = [(k, r) for k in kq for r in range(0, chunks[k]["rows"], nh)]
        for sec in range(3):
            k, r = spots[sec]
            lhs = dqkv[sec].reshape(nh, tp_size * rows_dev)
            work[k].acc[r : r + nh] = dot(lhs, rows_ref[...]).astype(BF16)
        k, r = spots[2]
        rest_rows = chunks[k]["rows"] - r - nh
        work[k].acc[r + nh :] = jnp.zeros((rest_rows, width), BF16)
        turn(kq)
        turn(PLAN_TAIL[3])
        core1.wait()

        def store0(here, val):
            tok_ref[here] = val + da_core[1, here].astype(F32)

        da_rows(0, store0)
        turn(PLAN_TAIL[4])
        turn(PLAN_WAIT)
        far.wait()
        last_own[...] = jnp.zeros_like(last_own)

        def norm_rows(r, carry):
            here = pl.ds(pl.multiple_of(r * blk, blk), blk)
            da = tok_ref[here] + da_across[here].astype(F32)
            hat, rstd = norm_parts(tiles_ref[here].astype(F32))
            tok_ref[here] = norm_back(hat, rstd, gain_ref[...], da)
            last_own[0:1] += jnp.sum(da * hat, axis=0, keepdims=True)
            last_own[1:2] += jnp.sum(da, axis=0, keepdims=True)
            return carry

        lax.fori_loop(0, rows_dev // blk, norm_rows, 0)

        def last_copy(s):
            if s < 2:
                return remote(
                    last_own.at[pl.ds(0, 8)], last_got.at[s, pl.ds(0, 8)],
                    vec_send.at[1, s], vec_recv.at[1, s], *ladder[s],
                )
            return remote(
                last_own, last_got.at[s], vec_send.at[1, s], vec_recv.at[1, s], *ladder[s]
            )

        last_copy(0).start()
        for st in range(len(ladder)):
            if st < len(PLAN_LAST):
                turn(PLAN_LAST[st])
            last_copy(st).wait()
            if st < 2:
                last_own[0:8] += last_got[st, 0:8]
                if st == 1:
                    last_own[8:] = onehot_ref[...] * last_own[1:2]
            else:
                last_own[...] += last_got[st]
            if st + 1 < len(ladder):
                last_copy(st + 1).start()
        while small_done[0] <= len(ladder):
            small_event(small_done[0])
            small_done[0] += 1
        turn(PLAN_LAST[-1])
        turn(PLAN_END)
        while any(done[k] <= work[k].n for k in range(len(work))):
            turn(range(len(work)))
        last_ref[...] = last_own[...]
        sum_ref[...] = small_in[...]
        kp = [k for k in n_tp if chunks[k].get("head")][0]
        nh, hr = chunks[kp]["head"]
        mine = work[kp].fin.at[pl.ds(nh, hr)]
        cps = [
            remote(mine, hg.at[p - 1], hg_send.at[p - 1], hg_recv.at[p - 1], "tp", p)
            for p in range(1, tp_size)
        ]
        for cp in cps:
            cp.start()
        head_out = [
            pltpu.make_async_copy(
                mine, rows_at(head_ref, tpi * hr, hr), do_local
            )
        ]
        head_out[0].start()
        for p, cp in enumerate(cps):
            cp.wait()
            out = pltpu.make_async_copy(
                hg.at[p], rows_at(head_ref, partner_any(tpi, p + 1) * hr, hr),
                local_sems.at[p, 3],
            )
            out.start()
            head_out.append(out)
        for out in head_out:
            out.wait()
        for ch in work:
            ch.out_copy().wait()


def partner_any(index, mask):
    if mask & 1:
        index = partner(index, 1)
    if mask & 2:
        index = partner(index, 2)
    return index


PLAN_STEPS = ((0, 1, 2), (3,), (4,), (), (0, 1, 2), (), (), (1,), (3, 4), (1,), (0,), (1, 2, 4))
PLAN_TAIL = ((0,), (), (1, 2, 3, 4), (0,), (1, 3))
PLAN_WAIT = (2, 6, 4, 5, 1)
PLAN_LAST = ((0,), (3, 5), (2, 6), (0, 4), (2, 3, 5), (0, 4, 6))
PLAN_END = (3, 2, 5, 4, 6, 5, 3, 6, 5, 6)


def attn_bwd(qkv, o, lse, do, rows, wt, tiles, gain, onehot, small, parts, mesh, scale):
    _, heads, _, frame = qkv.shape
    rows_dev, width = tiles.shape
    tp_size, dp_size = mesh.shape["tp"], mesh.shape["dp"]
    nbits = dp_size.bit_length() - 1
    half = width // 2
    ph_rows = parts[2].shape[1]
    chunks = [
        dict(tp=True, rows=half, part=0, order=[1, "X", 2, 4]),
        dict(tp=True, rows=half, part=1, order=["X", 1, 2, 4]),
        dict(tp=True, rows=half, part=0, order=[2, "X", 1, 4]),
        dict(tp=True, rows=half, part=1, order=[2, "X", 1, 4]),
        dict(tp=True, rows=ph_rows, part=0, order=["X", 1, 2, 4], head=(heads * HD, HEAD_ROWS)),
        dict(tp=False, rows=half, order=[2, 1, 4]),
        dict(tp=False, rows=256, order=[1, 2, 4]),
    ]
    n_k = len(chunks)
    scratch = [
        pltpu.VMEM((heads, frame, HD), BF16),
        pltpu.VMEM((heads, frame, HD), BF16),
        pltpu.VMEM((heads, frame, HD), F32),
        pltpu.VMEM((heads, frame, HD), F32),
        pltpu.VMEM((tp_size, heads, HD, rows_dev), BF16),
        pltpu.VMEM((3, heads, HD, frame), BF16),
        pltpu.VMEM((3, rows_dev, width), BF16),
        pltpu.VMEM((2, rows_dev, width), BF16),
        pltpu.VMEM((rows_dev, width), BF16),
        pltpu.VMEM((16, width), F32),
        pltpu.VMEM((2 + nbits, 16, width), F32),
        pltpu.VMEM((8 + onehot.shape[0], width), F32),
        pltpu.VMEM((2 + nbits, 8 + onehot.shape[0], width), F32),
        pltpu.VMEM((tp_size - 1, HEAD_ROWS, width), BF16),
    ]
    for c in chunks:
        r = c["rows"]
        scratch.append(pltpu.VMEM((r, width), BF16))
        scratch.append(pltpu.VMEM((2, r // 2, width), BF16))
        scratch.append(pltpu.VMEM((2, r // 4, width), BF16))
        scratch.append(pltpu.VMEM((2 + max(nbits - 3, 0), r // 8, width), BF16))
        if c["tp"]:
            scratch += [pltpu.VMEM((r, width), BF16)] * 4
        else:
            scratch.append(pltpu.VMEM((r, width), BF16))
    scratch += [
        pltpu.SemaphoreType.DMA((n_k, 17)),
        pltpu.SemaphoreType.DMA((n_k, 17)),
        pltpu.SemaphoreType.DMA((n_k, 4)),
        pltpu.SemaphoreType.DMA((tp_size,)),
        pltpu.SemaphoreType.DMA((tp_size,)),
        pltpu.SemaphoreType.DMA,
        pltpu.SemaphoreType.DMA((3,)),
        pltpu.SemaphoreType.DMA((3,)),
        pltpu.SemaphoreType.DMA((2, 2 + nbits)),
        pltpu.SemaphoreType.DMA((2, 2 + nbits)),
        pltpu.SemaphoreType.DMA((tp_size - 1,)),
        pltpu.SemaphoreType.DMA((tp_size - 1,)),
    ]
    any_spec = pl.BlockSpec(memory_space=pl.ANY)
    vmem = pl.BlockSpec(memory_space=pltpu.VMEM)
    return pl.pallas_call(
        functools.partial(
            bwd_kernel, scale=scale, chunks=chunks, dp_size=dp_size, heads=heads,
            tp_size=tp_size, width=width,
        ),
        grid=(tp_size, heads),
        in_specs=[vmem, vmem, vmem, any_spec] + [vmem] * 6 + [any_spec] * len(parts),
        out_specs=[vmem, vmem, vmem, any_spec] + [any_spec] * n_k,
        out_shape=[
            jax.ShapeDtypeStruct((rows_dev, width), F32),
            jax.ShapeDtypeStruct((16, width), F32),
            jax.ShapeDtypeStruct((8 + onehot.shape[0], width), F32),
            jax.ShapeDtypeStruct((tp_size * HEAD_ROWS, width), BF16),
        ]
        + [jax.ShapeDtypeStruct((c["rows"], width), BF16) for c in chunks],
        scratch_shapes=scratch,
        compiler_params=pltpu.CompilerParams(
            vmem_limit_bytes=60 << 20, collective_id=1, has_side_effects=True
        ),
        cost_estimate=pl.CostEstimate(
            flops=60_000_000_000, bytes_accessed=30 << 20, transcendentals=heads * frame * frame
        ),
        name="attn_bwd",
    )(qkv, o, lse, do, rows, wt, tiles, gain, onehot, small, *parts)


def mid_kernel(
    tiles_ref, o_ref, dots_ref, off_ref, vec_ref, hw_ref, hb_ref, scale_ref,
    pj_own, pj_far, wi_own, wi_far, na_own, na_far,
    dn_ref, dw_ref, ph_ref, do_ref, dx1_ref, small_ref, gates_ref, corr_ref,
    pj, wi, na, x1, hat, rstd, c_low, act, slope, h_low, hg, dx2, dz, du, dc, dy, hd, dn, dw, ph, dos,
    in_sem, out_sem, *, tp_size, heads
):
    tpi = lax.axis_index("tp")
    rows_dev, width = tiles_ref.shape
    nh = heads * HD
    half = rows_dev // 2
    blocks = [pl.ds(r * half, half) for r in range(2)]

    def loads(k, own, far, dst):
        out = []
        for p in range(tp_size):
            src = own if p == 0 else far.at[p - 1]
            n = src.shape[0]
            to = dst.at[pl.ds(p * n, n)] if len(dst.shape) == 2 else dst.at[p]
            out.append(pltpu.make_async_copy(src, to, in_sem.at[k, p]))
        return out

    load_pj = loads(0, pj_own, pj_far, pj)
    load_wi = loads(1, wi_own, wi_far, wi)
    load_na = loads(2, na_own, na_far, na)
    for cp in load_pj + load_wi + load_na:
        cp.start()
    small_ref[...] = jnp.zeros_like(small_ref)
    proj_bias, gain2, shift2, out_bias = (vec_ref[k : k + 1] for k in range(4))
    for cp in load_pj:
        cp.wait()
    for r in blocks:
        v = tiles_ref[r].astype(F32) + dot(o_ref[:, r], pj[...], ((0,), (0,))) + proj_bias
        x1[r] = v
        hv, rs = norm_parts(v)
        hat[r] = hv
        rstd[r] = rs
        c_low[r] = (hv * gain2 + shift2).astype(BF16)
    for p in range(tp_size):
        load_wi[p].wait()
        cols = pl.ds(p * width, width)
        for r in blocks:
            m, d = gelu_parts(dot(c_low[r], wi[p]) + off_ref[p : p + 1])
            act[r, cols] = m.astype(BF16)
            slope[r, cols] = d
    for cp in load_na:
        cp.wait()
    for r in blocks:
        h_low[r] = (x1[r] + dot(act[r], na[...]) + out_bias).astype(BF16)

    logits = dot(hw_ref[...], h_low[...], ((1,), (1,))) + hb_ref[...]
    row_scale = scale_ref[0:1, 0:1]
    lg = [logits[e * HEAD_ROWS : (e + 1) * HEAD_ROWS] for e in range(EXPERTS)]
    top = jnp.maximum(jnp.maximum(lg[0], lg[1]), lg[2])
    ex = [jnp.exp(v - top) for v in lg]
    inv = 1.0 / (ex[0] + ex[1] + ex[2])
    gt = [v * inv for v in ex]
    mixed = gt[0] * dots_ref[0] + gt[1] * dots_ref[1] + gt[2] * dots_ref[2]
    for e in range(EXPERTS):
        gates_ref[e] = gt[e]
        hg[e * HEAD_ROWS : (e + 1) * HEAD_ROWS] = (gt[e] * (dots_ref[e] - mixed)).astype(BF16)
    hg[EXPERTS * HEAD_ROWS :] = (dots_ref[EXPERTS] * row_scale).astype(BF16)
    corr_ref[...] = logits[EXPERTS * HEAD_ROWS :] * row_scale
    d2 = dot(hg[...], hw_ref[...], ((0,), (0,)))
    dx2[...] = d2
    dz[...] = d2.astype(BF16)
    small_ref[0:1] = jnp.sum(d2, axis=0, keepdims=True)
    ones = jnp.ones((8, rows_dev), BF16)
    small_ref[4:5, : tp_size * HEAD_ROWS] = dot(ones, hg[...], ((1,), (1,)))[0:1]

    def send_out(k, p, src, dst):
        cp = pltpu.make_async_copy(src, dst, out_sem.at[k, p])
        cp.start()
        return cp

    outs = []
    for p in range(tp_size):
        cols = pl.ds(p * width, width)
        dn[p] = dot(act[:, cols], dz[...], ((0,), (0,))).astype(BF16)
        outs.append(send_out(0, p, dn.at[p], dn_ref.at[p]))
    for p in range(tp_size):
        cols = pl.ds(p * width, width)
        for r in blocks:
            v = dot(dz[r], na[cols], ((1,), (1,))) * slope[r, cols]
            low = v.astype(BF16)
            du[p, r] = low
            small_ref[8 + p : 9 + p] += jnp.sum(low.astype(F32), axis=0, keepdims=True)
    for p in range(tp_size):
        dw[p] = dot(c_low[...], du[p], ((0,), (0,))).astype(BF16)
        outs.append(send_out(1, p, dw.at[p], dw_ref.at[p]))
    for r in blocks:
        g = dot(du[0, r], wi[0], ((1,), (1,)))
        for p in range(1, tp_size):
            g = g + dot(du[p, r], wi[p], ((1,), (1,)))
        hv = hat[r]
        d1 = dx2[r] + norm_back(hv, rstd[r], gain2, g)
        dx1_ref[r] = d1
        dy[r] = d1.astype(BF16)
        small_ref[1:2] += jnp.sum(g * hv, axis=0, keepdims=True)
        small_ref[2:3] += jnp.sum(g, axis=0, keepdims=True)
        small_ref[3:4] += jnp.sum(d1, axis=0, keepdims=True)
    dos[...] = dot(pj[...], dy[...], ((1,), (1,))).astype(BF16).reshape(dos.shape)
    outs.append(send_out(2, 0, dos, do_ref))
    dp = dot(o_ref[...], dy[...]).astype(BF16)
    hd[...] = dot(hg[...], h_low[...]).astype(BF16)
    for p in range(tp_size):
        ph[p, 0:nh] = dp[p * nh : (p + 1) * nh]
        at = pl.ds(pl.multiple_of(partner_any(tpi, p) * HEAD_ROWS, 16), HEAD_ROWS)
        ph[p, nh : nh + HEAD_ROWS] = hd[at]
        ph[p, nh + HEAD_ROWS :] = jnp.zeros((ph.shape[1] - nh - HEAD_ROWS, width), BF16)
        outs.append(send_out(3, p, ph.at[p], ph_ref.at[p]))
    for cp in outs:
        cp.wait()


def mid(tiles, o_own, dots, off, vec, hw, hb, row_scale, weights, mesh, heads):
    rows_dev, width = tiles.shape
    tp_size = mesh.shape["tp"]
    nh = heads * HD
    ph_rows = -(-(nh + HEAD_ROWS) // 128) * 128
    n_head = hw.shape[0]
    any_spec = pl.BlockSpec(memory_space=pl.ANY)
    vmem = pl.BlockSpec(memory_space=pltpu.VMEM)
    big = (tp_size, width, width)
    return pl.pallas_call(
        functools.partial(mid_kernel, tp_size=tp_size, heads=heads),
        in_specs=[vmem] * 8 + [any_spec] * 6,
        out_specs=[any_spec] * 4 + [vmem] * 4,
        out_shape=[
            jax.ShapeDtypeStruct(big, BF16),
            jax.ShapeDtypeStruct(big, BF16),
            jax.ShapeDtypeStruct((tp_size, ph_rows, width), BF16),
            jax.ShapeDtypeStruct((tp_size, heads, HD, rows_dev), BF16),
            jax.ShapeDtypeStruct((rows_dev, width), F32),
            jax.ShapeDtypeStruct((16, width), F32),
            jax.ShapeDtypeStruct((EXPERTS, HEAD_ROWS, rows_dev), F32),
            jax.ShapeDtypeStruct((HEAD_ROWS, rows_dev), F32),
        ],
        scratch_shapes=[
            pltpu.VMEM((tp_size * nh, width), BF16),
            pltpu.VMEM(big, BF16),
            pltpu.VMEM((tp_size * width, width), BF16),
            pltpu.VMEM((rows_dev, width), F32),
            pltpu.VMEM((rows_dev, width), F32),
            pltpu.VMEM((rows_dev, 1), F32),
            pltpu.VMEM((rows_dev, width), BF16),
            pltpu.VMEM((rows_dev, tp_size * width), BF16),
            pltpu.VMEM((rows_dev, tp_size * width), F32),
            pltpu.VMEM((rows_dev, width), BF16),
            pltpu.VMEM((n_head, rows_dev), BF16),
            pltpu.VMEM((rows_dev, width), F32),
            pltpu.VMEM((rows_dev, width), BF16),
            pltpu.VMEM((tp_size, rows_dev, width), BF16),
            pltpu.VMEM((8, width), F32),
            pltpu.VMEM((rows_dev, width), BF16),
            pltpu.VMEM((n_head, width), BF16),
            pltpu.VMEM(big, BF16),
            pltpu.VMEM(big, BF16),
            pltpu.VMEM((tp_size, ph_rows, width), BF16),
            pltpu.VMEM((tp_size, heads, HD, rows_dev), BF16),
            pltpu.SemaphoreType.DMA((3, tp_size)),
            pltpu.SemaphoreType.DMA((4, tp_size)),
        ],
        compiler_params=pltpu.CompilerParams(vmem_limit_bytes=60 << 20),
        cost_estimate=pl.CostEstimate(
            flops=18_000_000_000, bytes_accessed=30 << 20, transcendentals=2_000_000
        ),
        name="mid",
    )(tiles, o_own, dots, off, vec, hw, hb, row_scale, *weights)


def norm_parts(values):
    center = values - jnp.mean(values, axis=-1, keepdims=True)
    rstd = lax.rsqrt(jnp.mean(center * center, axis=-1, keepdims=True) + EPSILON)
    return center * rstd, rstd


def norm_back(hat, rstd, gain, grad):
    g = grad * gain
    return rstd * (
        g
        - jnp.mean(g, axis=-1, keepdims=True)
        - hat * jnp.mean(g * hat, axis=-1, keepdims=True)
    )


def gelu_parts(u):
    half = jnp.exp(-0.5 * u * u)
    t = 1.0 / (1.0 + (0.3275911 * 0.7071067811865476) * jnp.abs(u))
    poly = t * (
        0.254829592
        + t * (-0.284496736 + t * (1.421413741 + t * (-1.453152027 + t * 1.061405429)))
    )
    tail = 0.5 * poly * half
    cdf = jnp.where(u >= 0, 1.0 - tail, tail)
    return u * cdf, cdf + u * half * 0.3989422804014327


def make_body(mesh):
    dp_size, tp_size = mesh.shape["dp"], mesh.shape["tp"]

    def swap(x, axis, bit):
        size = dp_size if axis == "dp" else tp_size
        return lax.ppermute(x, axis, [(i, i ^ bit) for i in range(size)])

    def core(x):
        return swap(x, "tp", 1)

    def across(x):
        return swap(x, "tp", 2)

    def body(
        tile_vectors,
        snapshot_horizon_slot,
        horizon_sample_tally,
        specialist_outlooks,
        early_layernorm_scale,
        early_layernorm_shift,
        horizon_vectors,
        triple_head_matrix,
        attending_matrix,
        attending_offset,
        later_layernorm_scale,
        later_layernorm_shift,
        widening_matrix,
        widening_offset,
        narrowing_matrix,
        narrowing_offset,
        router_matrix,
        router_offset,
        adjuster_matrix,
        adjuster_offset,
        combined_loss_slope,
    ):
        rows_dev, width = tile_vectors.shape
        heads = triple_head_matrix.shape[2] // HD
        rows_frame = rows_dev * tp_size
        fields = adjuster_matrix.shape[1]
        sites = combined_loss_slope.shape[1]
        scale_val = HD ** (-0.5)
        tp_index = lax.axis_index("tp")
        lead = snapshot_horizon_slot[0]
        embed = lax.dynamic_slice_in_dim(horizon_vectors, lead, 1, 0)
        row_scale = lax.rsqrt(
            lax.dynamic_slice_in_dim(horizon_sample_tally, lead, 1, 0).astype(F32)
        )[0]
        nh = heads * HD
        w_t = jnp.transpose(triple_head_matrix, (0, 2, 1))
        (attn_rows, qkv, o_heads, lse, o_own, dots, proj_all, wide_all, narrow_all) = attn_fwd(
            tile_vectors,
            early_layernorm_scale[None, :],
            early_layernorm_shift[None, :] + embed,
            w_t,
            attending_matrix,
            widening_matrix,
            narrowing_matrix,
            specialist_outlooks,
            combined_loss_slope,
            mesh,
            scale_val,
        )
        off2 = across(widening_offset)
        off_all = jnp.stack([widening_offset, core(widening_offset), off2, core(off2)])

        def head_pad(x):
            x = x.reshape((EXPERTS + 1, fields) + x.shape[1:])
            x = jnp.pad(x, ((0, 0), (0, HEAD_ROWS - fields)) + ((0, 0),) * (x.ndim - 2))
            return x.reshape((-1,) + x.shape[2:])

        hw = head_pad(jnp.concatenate([router_matrix, adjuster_matrix], axis=1).T)
        hb = head_pad(jnp.concatenate([router_offset, adjuster_offset])[:, None])
        vec = jnp.stack(
            [attending_offset, later_layernorm_scale, later_layernorm_shift, narrowing_offset]
        )
        (d_narrow, d_wide, d_ph, do_all, dx1, small, gates, corr) = mid(
            tile_vectors,
            o_own.reshape(tp_size * nh, rows_dev),
            dots,
            off_all,
            vec,
            hw,
            hb,
            row_scale[None, None],
            [
                attending_matrix, proj_all, widening_matrix, wide_all,
                narrowing_matrix, narrow_all,
            ],
            mesh,
            heads,
        )
        gates = gates[:, :fields]
        corr = corr[:fields]

        blended = (corr)[:, None, :]
        for e in range(EXPERTS):
            blended = blended + gates[e][:, None, :] * specialist_outlooks[e].astype(F32)

        leads = horizon_vectors.shape[0]
        onehot = (jnp.arange(leads, dtype=jnp.int32) == lead).astype(F32)[:, None]
        (token_part, small, table, head_sum, n0, n1, i0, i1, ph, q0, q1) = attn_bwd(
            qkv, o_heads, lse, do_all, attn_rows.reshape(rows_frame, width), w_t.reshape(3 * nh, width), tile_vectors,
            early_layernorm_scale[None, :], onehot, small,
            [d_narrow, d_wide, d_ph], mesh, scale_val,
        )
        tokens_grad = dx1 + token_part
        narrow_sum = jnp.concatenate([n0, n1], axis=0).astype(F32)
        wide_sum = jnp.concatenate([i0, i1], axis=0).astype(F32)
        proj_weight_grad = ph[:nh].astype(F32)
        head_sum = head_sum.reshape(EXPERTS + 1, HEAD_ROWS, width)[:, :fields]
        gate_weight_grad = head_sum[:EXPERTS].reshape(EXPERTS * fields, width).T.astype(F32)
        correct_weight_grad = head_sum[EXPERTS].T.astype(F32)
        head_bias = small[4, : (EXPERTS + 1) * HEAD_ROWS].reshape(EXPERTS + 1, HEAD_ROWS)
        head_bias = head_bias[:, :fields]
        q_all = jnp.concatenate([q0, q1], axis=0)[: 3 * nh]
        qkv_sum = jnp.transpose(q_all.reshape(3, nh, width), (0, 2, 1)).astype(F32)
        in_bias_grad = small[8]

        return (
            blended,
            tokens_grad,
            table[0],
            table[1],
            table[8:],
            qkv_sum,
            proj_weight_grad,
            small[3],
            small[1],
            small[2],
            wide_sum,
            in_bias_grad,
            narrow_sum,
            small[0],
            gate_weight_grad,
            head_bias[:EXPERTS].reshape(EXPERTS * fields),
            correct_weight_grad,
            head_bias[EXPERTS],
        )

    return body


def solution(mesh):
    return jax.shard_map(
        make_body(mesh),
        mesh=mesh,
        in_specs=(
            P(("dp", "tp"), None),
            P("dp"),
            P(),
            P(None, None, None, ("dp", "tp")),
            P(),
            P(),
            P(),
            P(None, None, "tp"),
            P("tp", None),
            P(),
            P(),
            P(),
            P(None, "tp"),
            P("tp"),
            P("tp", None),
            P(),
            P(),
            P(),
            P(),
            P(),
            P(None, None, ("dp", "tp")),
        ),
        out_specs=(
            P(None, None, ("dp", "tp")),
            P(("dp", "tp"), None),
            P(),
            P(),
            P(),
            P(None, None, "tp"),
            P("tp", None),
            P(),
            P(),
            P(),
            P(None, "tp"),
            P("tp"),
            P("tp", None),
            P(),
            P(),
            P(),
            P(),
            P(),
        ),
        check_vma=False,
    )
```

```python
import functools
import jax
import jax.numpy as jnp
from jax import lax
from jax.experimental import pallas as pl
from jax.experimental.pallas import tpu as pltpu
from jax.sharding import PartitionSpec as P

HD = 64
EXPERTS = 3
HEAD_ROWS = 80
EPSILON = 1e-05
F32 = jnp.float32
BF16 = jnp.bfloat16


def dot(a, b, dims=((1,), (0,))):
    return lax.dot_general(a, b, (dims, ((), ())), preferred_element_type=F32)


def row_of(ref):
    return ref[...].reshape(1, ref.shape[0])


def fwd_kernel(
    lead_ref, tiles_ref, gain_ref, shift_ref, table_ref, off_ref, wt_ref, proj_ref, wide_ref,
    narrow_ref, exp_ref, slope_ref,
    rows_out, qkv_ref, o_ref, lse_ref, own_out, dots_ref, off_out, proj_all, wide_all, narrow_all,
    offs, off_send, off_recv, rows_ref, own_ref, out_sem, ks, stream, stream_g, stream_sem, row_send, row_recv, o_send, o_recv, o_local,
    w_send, w_recv, *, scale, dp_size, tp_size, heads
):
    i, h = pl.program_id(0), pl.program_id(1)
    steps = tp_size * heads
    step = i * heads + h
    dpi, tpi = lax.axis_index("dp"), lax.axis_index("tp")
    rows_dev, width = tiles_ref.shape
    piece = rows_dev // 2
    mine = lax.rem(dpi, 2)

    def remote(src, dst, ssem, rsem, axis, bit):
        dev = (partner(dpi, bit), tpi) if axis == "dp" else (dpi, partner_any(tpi, bit))
        return pltpu.make_async_remote_copy(
            src_ref=src, dst_ref=dst, send_sem=ssem, recv_sem=rsem,
            device_id=dev, device_id_type=pl.DeviceIdType.MESH,
        )

    def row_copy(kind, c):
        a, b, bit = ((0, 1, 1), (0, 2, 2), (2, 3, 1))[kind]
        here = pl.ds(c * piece, piece)
        return remote(
            rows_ref.at[a, here], rows_ref.at[b, here],
            row_send.at[kind, c], row_recv.at[kind, c], "tp", bit,
        )

    def off_copy(m):
        return remote(offs.at[0], offs.at[m], off_send.at[m], off_recv.at[m], "tp", m)

    parts = []
    for src, dst, cuts in ((proj_ref, proj_all, 1), (wide_ref, wide_all, 2), (narrow_ref, narrow_all, 2)):
        n = src.shape[0] // cuts
        for c in range(cuts):
            parts.append((src, dst, c * n, n // 2))

    def w_half(part, whose):
        return pl.ds(pl.multiple_of(part[2] + whose * part[3], 16), part[3])

    def w_far(n):
        src, dst, _, _ = parts[n]
        rows = w_half(parts[n], mine)
        return remote(
            src.at[rows], dst.at[1, rows], w_send.at[n, 0], w_recv.at[n, 0], "tp", 2
        )

    def w_side(n):
        dst = parts[n][1]
        rows = w_half(parts[n], mine)
        here = dst.at[1, rows]
        return remote(here, here, w_send.at[n, 1], w_recv.at[n, 1], "dp", 1)

    def w_fwd(n, second):
        dst = parts[n][1]
        rows = w_half(parts[n], 1 - mine if second else mine)
        k = 3 if second else 2
        return remote(
            dst.at[1, rows], dst.at[2, rows], w_send.at[n, k], w_recv.at[n, k], "tp", 1
        )

    def w_near(n):
        src, dst, lo, half = parts[n]
        rows = pl.ds(lo, 2 * half)
        return remote(src.at[rows], dst.at[0, rows], w_send.at[n, 4], w_recv.at[n, 4], "tp", 1)

    def o_copy(p):
        if p == 0:
            return pltpu.make_async_copy(o_ref.at[0], own_ref.at[0], o_local)
        return remote(o_ref.at[p], own_ref.at[p], o_send.at[p], o_recv.at[p], "tp", p)

    fields, sites = slope_ref.shape[0], slope_ref.shape[1]
    per = stream.shape[2]
    groups = fields // per
    depth = stream.shape[0]

    def stream_copies(g):
        slot = lax.rem(g, depth)
        at = pl.ds(g * per, per)
        return (
            pltpu.make_async_copy(
                exp_ref.at[:, at], stream.at[slot], stream_sem.at[slot, 0]
            ),
            pltpu.make_async_copy(
                slope_ref.at[at], stream_g.at[slot], stream_sem.at[slot, 1]
            ),
        )

    @pl.when(step == 0)
    def _():
        barrier = pltpu.get_barrier_semaphore()
        others = [("tp", 1), ("tp", 2), ("tp", 3), ("dp", 1)]
        for axis, bit in others:
            dev = (partner(dpi, bit), tpi) if axis == "dp" else (dpi, partner_any(tpi, bit))
            pl.semaphore_signal(
                barrier, inc=1, device_id=dev, device_id_type=pl.DeviceIdType.MESH
            )
        for g in range(min(depth - 1, groups)):
            for cp in stream_copies(g):
                cp.start()
        blk = 64
        gain = row_of(gain_ref)
        shift = row_of(shift_ref) + table_ref[pl.ds(lead_ref[0], 1)]
        offs[0, 0:1] = row_of(off_ref)

        def norm_rows(r, carry):
            here = pl.ds(pl.multiple_of(r * blk, blk), blk)
            hat, _ = norm_parts(tiles_ref[here].astype(F32))
            rows_ref[0, here] = (hat * gain + shift).astype(BF16)
            return carry

        half = piece // blk
        lax.fori_loop(0, half, norm_rows, 0)
        pl.semaphore_wait(barrier, len(others))
        row_copy(1, 0).start()
        lax.fori_loop(half, 2 * half, norm_rows, 0)
        row_copy(1, 1).start()
        row_copy(0, 0).start()
        row_copy(0, 1).start()
        for m in range(1, tp_size):
            off_copy(m).start()

        def contract(g, carry):
            @pl.when(g + depth - 1 < groups)
            def _():
                for cp in stream_copies(g + depth - 1):
                    cp.start()

            for cp in stream_copies(g):
                cp.wait()
            slot = lax.rem(g, depth)
            for j in range(per):
                slope = stream_g[slot, j].astype(F32)
                for e in range(EXPERTS):
                    dots_ref[e, pl.ds(g * per + j, 1)] = jnp.sum(
                        stream[slot, e, j].astype(F32) * slope, axis=0, keepdims=True
                    )
                dots_ref[EXPERTS, pl.ds(g * per + j, 1)] = jnp.sum(slope, axis=0, keepdims=True)
            return carry

        dots_ref[...] = jnp.zeros_like(dots_ref)
        lax.fori_loop(0, groups, contract, 0)

        def project(p):
            lane = pl.ds(p * rows_dev, rows_dev)
            for s in range(3):
                part = dot(wt_ref[s], rows_ref[p], ((1,), (1,))).astype(BF16)
                qkv_ref[s, :, :, lane] = part.reshape(heads, HD, rows_dev)
            for hh in range(heads):
                ks[hh, lane] = qkv_ref[1, hh, :, lane].T

        project(0)
        for c in range(2):
            row_copy(0, c).wait()
        project(1)
        for c in range(2):
            row_copy(1, c).wait()
            row_copy(2, c).start()
        w_far(0).start()
        w_far(1).start()
        project(2)
        for c in range(2):
            row_copy(2, c).wait()
        for n in range(len(parts)):
            w_near(n).start()
        rows_copy = pltpu.make_async_copy(rows_ref, rows_out, out_sem.at[0])
        rows_copy.start()
        project(3)

    p = lax.rem(i + 2, tp_size)
    lanes = pl.ds(pl.multiple_of(p * rows_dev, rows_dev), rows_dev)
    q = qkv_ref[0, h, :, lanes] * jnp.bfloat16(scale)
    s = dot(ks[h], q)
    m = jnp.max(s, axis=0, keepdims=True)
    e = jnp.exp(s - m)
    l = jnp.sum(e, axis=0, keepdims=True)
    o_ref[p, h] = (dot(qkv_ref[2, h], e.astype(BF16)) / l).astype(BF16)
    lse_ref[p, h] = m + jnp.log(l)

    seq = {}

    def after(st, *what):
        seq.setdefault(min(st, steps - 1), []).extend(what)

    arrive = (1, 3, 6, 9, 11)
    side = (3, 7, 10, 11, 11)
    for n in range(len(parts)):
        after(arrive[n], ("far", n))
    for n in range(len(parts)):
        after(side[n], ("side", n))
    for st, what in seq.items():

        @pl.when(step == st)
        def _():
            for kind, n in what:
                if kind == "far":
                    w_far(n).wait()
                    if n + 2 < len(parts):
                        w_far(n + 2).start()
                    w_side(n).start()
                    w_fwd(n, False).start()
                else:
                    w_side(n).wait()
                    w_fwd(n, True).start()

    for k in range(tp_size):

        @pl.when(step == k * heads + heads - 1)
        def _():
            o_copy((k + 2) % tp_size).start()

    @pl.when(step == steps - 1)
    def _():
        for k in range(tp_size):
            o_copy(k).wait()
        for m in range(1, tp_size):
            off_copy(m).wait()
        off_out[...] = offs[...]
        own_copy = pltpu.make_async_copy(own_ref, own_out, out_sem.at[1])
        own_copy.start()
        for n in range(len(parts)):
            w_near(n).wait()
            w_fwd(n, False).wait()
            w_fwd(n, True).wait()
        own_copy.wait()
        pltpu.make_async_copy(rows_ref, rows_out, out_sem.at[0]).wait()


def attn_fwd(
    lead, tiles, gain, shift, table, off, wt, proj, wide, narrow, experts, slope, mesh, scale
):
    rows_dev, width = tiles.shape
    heads = proj.shape[0] // HD
    tp_size, dp_size = mesh.shape["tp"], mesh.shape["dp"]
    frame = tp_size * rows_dev
    fields, sites = slope.shape[0], slope.shape[1]
    per = 3 if fields % 3 == 0 else 1
    depth = 4
    any_spec = pl.BlockSpec(memory_space=pl.ANY)
    vmem = pl.BlockSpec(memory_space=pltpu.VMEM)
    return pl.pallas_call(
        functools.partial(
            fwd_kernel, scale=scale, dp_size=dp_size, tp_size=tp_size, heads=heads
        ),
        grid=(tp_size, heads),
        in_specs=[pl.BlockSpec(memory_space=pltpu.SMEM)] + [vmem] * 6 + [any_spec] * 5,
        out_specs=[any_spec] + [vmem] * 3 + [any_spec, vmem, vmem] + [any_spec] * 3,
        out_shape=[
            jax.ShapeDtypeStruct((tp_size, rows_dev, width), BF16),
            jax.ShapeDtypeStruct((3, heads, HD, frame), BF16),
            jax.ShapeDtypeStruct((tp_size, heads, HD, rows_dev), BF16),
            jax.ShapeDtypeStruct((tp_size, heads, 1, rows_dev), F32),
            jax.ShapeDtypeStruct((tp_size, heads, HD, rows_dev), BF16),
            jax.ShapeDtypeStruct((EXPERTS + 1, HEAD_ROWS, rows_dev), F32),
            jax.ShapeDtypeStruct((tp_size, 8, width), F32),
            jax.ShapeDtypeStruct((tp_size - 1,) + proj.shape, BF16),
            jax.ShapeDtypeStruct((tp_size - 1,) + wide.shape, BF16),
            jax.ShapeDtypeStruct((tp_size - 1,) + narrow.shape, BF16),
        ],
        scratch_shapes=[
            pltpu.VMEM((tp_size, 8, width), F32),
            pltpu.SemaphoreType.DMA((tp_size,)),
            pltpu.SemaphoreType.DMA((tp_size,)),
            pltpu.VMEM((tp_size, rows_dev, width), BF16),
            pltpu.VMEM((tp_size, heads, HD, rows_dev), BF16),
            pltpu.SemaphoreType.DMA((2,)),
            pltpu.VMEM((heads, frame, HD), BF16),
            pltpu.VMEM((depth, EXPERTS, per, sites, rows_dev), BF16),
            pltpu.VMEM((depth, per, sites, rows_dev), BF16),
            pltpu.SemaphoreType.DMA((depth, 2)),
            pltpu.SemaphoreType.DMA((3, 2)),
            pltpu.SemaphoreType.DMA((3, 2)),
            pltpu.SemaphoreType.DMA((tp_size,)),
            pltpu.SemaphoreType.DMA((tp_size,)),
            pltpu.SemaphoreType.DMA,
            pltpu.SemaphoreType.DMA((5, 5)),
            pltpu.SemaphoreType.DMA((5, 5)),
        ],
        compiler_params=pltpu.CompilerParams(
            vmem_limit_bytes=56 << 20, collective_id=0, has_side_effects=True
        ),
        cost_estimate=pl.CostEstimate(
            flops=30_000_000_000, bytes_accessed=40 << 20, transcendentals=heads * frame * frame
        ),
        name="attn_fwd",
    )(lead, tiles, gain, shift, table, off, wt, proj, wide, narrow, experts, slope)


def partner(index, bit):
    return index + bit - 2 * bit * lax.rem(lax.div(index, bit), 2)


def rows_at(ref, start, size):
    return ref.at[pl.ds(pl.multiple_of(start, 16), size)]


def add_rows(dst, src, lead, dst_off, src_off, size):
    step = 48 if size % 48 == 0 else 32

    def one(r, carry):
        here = pl.ds(pl.multiple_of(dst_off + r * step, 16), step)
        there = pl.ds(pl.multiple_of(src_off + r * step, 16), step)
        got = src[there] if lead is None else src[lead, there]
        dst[here] = (dst[here].astype(F32) + got.astype(F32)).astype(BF16)
        return carry

    lax.fori_loop(0, size // step, one, 0)


def bwd_kernel(
    qkv_ref, o_ref, lse_ref, do_ref, rows_ref, wt_ref, tiles_ref, gain_ref, onehot_ref, small_ref,
    *rest, scale, chunks, dp_size, heads, tp_size, width
):
    n_src = sum(1 for c in chunks if c["tp"] and c["part"] == 0)
    srcs = rest[:n_src]
    tok_ref, sum_ref, last_ref, head_ref = rest[n_src : n_src + 4]
    n_out = n_src + 4 + 4
    outs = rest[n_src + 4 : n_out]
    (
        ks, vs, dks, dvs, dos, dqkv, da_far, da_core, da_across,
        small_in, small_got, last_tp, last_dp, hg,
    ) = rest[n_out : n_out + 14]
    per = rest[n_out + 14 : -12]
    (
        send_sems, recv_sems, local_sems, do_send, do_recv, do_local, da_send, da_recv,
        vec_send, vec_recv, hg_send, hg_recv,
    ) = rest[-12:]
    h, i = pl.program_id(0), pl.program_id(1)
    steps = tp_size * heads
    step = h * tp_size + i
    dpi, tpi = lax.axis_index("dp"), lax.axis_index("tp")
    rows_dev = dos.shape[3]
    bits = [1 << b for b in range(dp_size.bit_length() - 1)]

    def remote(src, dst, ssem, rsem, axis, bit):
        dev = (partner_any(dpi, bit), tpi) if axis == "dp" else (dpi, partner_any(tpi, bit))
        return pltpu.make_async_remote_copy(
            src_ref=src, dst_ref=dst, send_sem=ssem, recv_sem=rsem,
            device_id=dev, device_id_type=pl.DeviceIdType.MESH,
        )

    def bit_of(bit):
        return lax.rem(lax.div(dpi, bit), 2)

    bufs, at = [], 0
    for c in chunks:
        n = 8 if c["tp"] else 5
        bufs.append(per[at : at + n])
        at += n

    class Chunk:
        def __init__(self, k):
            self.k, self.c = k, chunks[k]
            self.rows, self.order = self.c["rows"], self.c["order"]
            self.acc = bufs[k][0]
            self.halves = bufs[k][1:4]
            if self.c["tp"]:
                self.mid, self.got, self.got_far, self.got_x = bufs[k][4:8]
                self.fin = self.got
            else:
                self.fin = bufs[k][4]
            self.stages = []
            if self.c["tp"]:
                self.stages.append(("C", 0, None))
            size, seq, far = self.rows, [], self.c["tp"]
            for name in self.order:
                if name == "X":
                    far = False
                    self.stages.append(("X", size, list(seq)))
                else:
                    self.stages.append(("R", name, (list(seq), size, far)))
                    size //= 2
                    seq.append((name, size))
            for name in bits[3:]:
                self.stages.append(("B", name, (list(seq), size)))
            while seq:
                name, half = seq[-1]
                self.stages.append(("G", name, (list(seq), half)))
                seq.pop()

        def off(self, seq):
            total = 0
            for name, half in seq:
                total = total + bit_of(name) * half
            return total

        def copies(self, s):
            kind, name, info = self.stages[s]
            ss, rs = send_sems.at[self.k], recv_sems.at[self.k]
            if kind == "C":
                lo = self.c["part"] * self.rows
                blk = [self.c_src.at[p, pl.ds(lo, self.rows)] for p in range(tp_size)]
                return [
                    remote(blk[1], self.got, ss.at[0], rs.at[0], "tp", 1),
                    remote(blk[3], self.got_far, ss.at[1], rs.at[1], "tp", 1),
                    pltpu.make_async_copy(blk[0], self.acc, local_sems.at[self.k, 0]),
                    pltpu.make_async_copy(blk[2], self.mid, local_sems.at[self.k, 1]),
                ]
            if kind == "X":
                off = self.off(info)
                return [
                    remote(
                        rows_at(self.mid, off, name), rows_at(self.got_x, off, name),
                        ss.at[2], rs.at[2], "tp", 2,
                    )
                ]
            if kind == "R":
                seq, size, far = info
                half = size // 2
                off = self.off(seq) + (1 - bit_of(name)) * half
                slot = self.slot(s)
                out = [
                    remote(
                        rows_at(self.acc, off, half), self.halves[slot].at[0, pl.ds(0, half)],
                        ss.at[3 + s], rs.at[3 + s], "dp", name,
                    )
                ]
                if far:
                    out.append(
                        remote(
                            rows_at(self.mid, off, half),
                            self.halves[slot].at[1, pl.ds(0, half)],
                            ss.at[2 + 14], rs.at[2 + 14], "dp", name,
                        )
                    )
                return out
            if kind == "B":
                seq, size = info
                off = self.off(seq)
                slot = 2
                return [
                    remote(
                        rows_at(self.acc, off, size),
                        self.halves[slot].at[2 + bits.index(name) - 3, pl.ds(0, size)],
                        ss.at[3 + s], rs.at[3 + s], "dp", name,
                    )
                ]
            seq, half = info
            off = self.off(seq)
            here = rows_at(self.fin, off, half)
            return [remote(here, here, ss.at[3 + s], rs.at[3 + s], "dp", name)]

        def slot(self, s):
            return sum(1 for t in self.stages[:s] if t[0] == "R")

        def start(self, s):
            for cp in self.copies(s):
                cp.start()

        def finish(self, s):
            kind, name, info = self.stages[s]
            for cp in self.copies(s):
                cp.wait()
            if kind == "C":
                add_rows(self.acc, self.got, None, 0, 0, self.rows)
                add_rows(self.mid, self.got_far, None, 0, 0, self.rows)
            if kind == "X":
                off = self.off(info)
                add_rows(self.acc, self.got_x, None, off, off, name)
            if kind == "R":
                seq, size, far = info
                half = size // 2
                off = self.off(seq) + bit_of(name) * half
                got = self.halves[self.slot(s)]
                add_rows(self.acc, got, 0, off, 0, half)
                if far:
                    add_rows(self.mid, got, 1, off, 0, half)
            if kind == "B":
                seq, size = info
                add_rows(self.acc, self.halves[2], bits.index(name) - 1, self.off(seq), 0, size)

        def event(self, s):
            if s > 0:
                self.finish(s - 1)
            if s < len(self.stages):
                if self.stages[s][0] == "G" and self.stages[s - 1][0] != "G":
                    seq, size = self.stages[s][2]
                    here = pl.ds(pl.multiple_of(self.off(seq), 16), size)
                    self.fin[here] = self.acc[here]
                self.start(s)
            else:
                self.out_copy().start()
                if self.c.get("head"):
                    head_start(self)

        def out_copy(self):
            return pltpu.make_async_copy(
                self.fin, outs[self.c["out"][0]].at[pl.ds(self.c["out"][1], self.rows)],
                local_sems.at[self.k, 2],
            )

        @property
        def n(self):
            return len(self.stages)

    head_nh, hr = [c["head"] for c in chunks if c.get("head")][0]
    head_chunk = []

    def head_remote(ch, p):
        mine = ch.fin.at[pl.ds(head_nh, hr)]
        return remote(mine, hg.at[p - 1], hg_send.at[p - 1], hg_recv.at[p - 1], "tp", p)

    def head_local(ch):
        mine = ch.fin.at[pl.ds(head_nh, hr)]
        return pltpu.make_async_copy(mine, rows_at(head_ref, tpi * hr, hr), local_sems.at[0, 3])

    def head_start(ch):
        head_chunk.append(ch)
        for p in range(1, tp_size):
            head_remote(ch, p).start()
        head_local(ch).start()

    work, at = [], 0
    for k, c in enumerate(chunks):
        ch = Chunk(k)
        if c["tp"]:
            if c["part"] == 0:
                at += 1
            ch.c_src = srcs[at - 1]
        work.append(ch)
    done = [0] * len(work)

    def go(k, upto=None):
        if done[k] <= work[k].n:
            work[k].event(done[k])
            done[k] += 1

    def turn(ks):
        for k in ks:
            go(k)

    ladder = [("tp", 1), ("tp", 2)] + [("dp", b) for b in bits]

    def small_copy(s):
        return remote(
            small_in, small_got.at[s], vec_send.at[0, s], vec_recv.at[0, s], *ladder[s]
        )

    def small_event(s):
        if s > 0:
            small_copy(s - 1).wait()
            got = small_got[s - 1]
            small_in[0:8] += got[0:8]
            if s == 1:
                small_in[8:9] += got[9:10]
                small_in[10:11] += got[11:12]
            elif s == 2:
                small_in[8:9] += got[10:11]
            else:
                small_in[8:9] += got[8:9]
        if s < len(ladder):
            small_copy(s).start()

    def do_copy(p):
        if p == 0:
            return pltpu.make_async_copy(do_ref.at[0], dos.at[0], do_local)
        return remote(do_ref.at[p], dos.at[p], do_send.at[p], do_recv.at[p], "tp", p)

    @pl.when(step == 0)
    def _():
        barrier = pltpu.get_barrier_semaphore()
        others = [("tp", m) for m in range(1, tp_size)] + [("dp", m) for m in range(1, dp_size)]
        for axis, bit in others:
            dev = (partner_any(dpi, bit), tpi) if axis == "dp" else (dpi, partner_any(tpi, bit))
            pl.semaphore_signal(
                barrier, inc=1, device_id=dev, device_id_type=pl.DeviceIdType.MESH
            )
        pl.semaphore_wait(barrier, len(others))
        for p in (2, 3, 1, 0):
            do_copy(p).start()
        turn(PLAN_FIRST)
        small_in[...] = small_ref[...]
        small_event(0)

    for p in range(tp_size):

        @pl.when(step == p)
        def _():
            do_copy(p).wait()

    @pl.when(i == 0)
    def _():
        ks[...] = qkv_ref[1, h].T
        vs[...] = qkv_ref[2, h].T
        dks[...] = jnp.zeros_like(dks)
        dvs[...] = jnp.zeros_like(dvs)

    lanes = pl.ds(pl.multiple_of(i * rows_dev, rows_dev), rows_dev)
    qt = qkv_ref[0, h, :, lanes] * jnp.bfloat16(scale)
    dot_t = dos[i, h]
    dsum = jnp.sum(
        dot_t.astype(F32) * o_ref[i, h].astype(F32), axis=0, keepdims=True
    )
    s = dot(ks[...], qt)
    p = jnp.exp(s - lse_ref[i, h])
    dp = dot(vs[...], dot_t)
    ds = (p * (dp - dsum)).astype(BF16)
    dqkv[0, h, :, lanes] = (dot(qkv_ref[1, h], ds) * scale).astype(BF16)
    dvs[...] += dot(p.astype(BF16), dot_t.T)
    dks[...] += dot(ds, qt.T)

    @pl.when(i == tp_size - 1)
    def _():
        dqkv[1, h] = dks[...].astype(BF16).T
        dqkv[2, h] = dvs[...].astype(BF16).T

    qk = 3 * HD
    due = {}
    spot = 0
    for k in range(len(work)):
        if not chunks[k]["tp"]:
            n = min(chunks[k]["rows"] // qk, heads - spot)
            due[k] = (spot, n)
            spot += n

    def weight_grad(k):
        first, n = due[k]
        for sec in range(3):
            lhs = dqkv[sec, first : first + n].reshape(n * HD, tp_size * rows_dev)
            work[k].acc[sec * n * HD : (sec + 1) * n * HD] = dot(lhs, rows_ref[...]).astype(BF16)
        spare = chunks[k]["rows"] - n * qk
        if spare:
            work[k].acc[n * qk :] = jnp.zeros((spare, width), BF16)
        go(k)

    early = [k for k in due if sum(due[k]) < heads]
    small_done = [1]
    for st in range(steps):

        @pl.when(step == st)
        def _():
            for k in early:
                if st == sum(due[k]) * tp_size - 1:
                    weight_grad(k)
            if st < len(PLAN_STEPS):
                turn(PLAN_STEPS[st])
            if small_done[0] <= len(ladder):
                small_event(small_done[0])
                small_done[0] += 1

    @pl.when(step == steps - 1)
    def _():
        blk = 128

        def da_rows(p, store):
            def one(r, carry):
                lane = pl.ds(pl.multiple_of(p * rows_dev + r * blk, blk), blk)
                lhs = dqkv[:, :, :, lane].reshape(3 * heads * HD, blk)
                here = pl.ds(pl.multiple_of(r * blk, blk), blk)
                store(here, dot(lhs, wt_ref[...], ((0,), (0,))))
                return carry

            lax.fori_loop(0, rows_dev // blk, one, 0)

        def keep(slot):
            def store(here, val):
                da_far[slot, here] = val.astype(BF16)

            return store

        core3 = remote(da_far.at[0], da_core.at[0], da_send.at[0], da_recv.at[0], "tp", 1)
        core1 = remote(da_far.at[1], da_core.at[1], da_send.at[1], da_recv.at[1], "tp", 1)
        far = remote(da_far.at[2], da_across, da_send.at[2], da_recv.at[2], "tp", 2)
        da_rows(3, keep(0))
        core3.start()
        turn(PLAN_TAIL[0])
        da_rows(1, keep(1))
        core1.start()
        turn(PLAN_TAIL[1])
        core3.wait()

        def store2(here, val):
            da_far[2, here] = (val + da_core[0, here].astype(F32)).astype(BF16)

        da_rows(2, store2)
        far.start()
        turn(PLAN_TAIL[2])
        for k in due:
            if k not in early:
                weight_grad(k)
        turn(PLAN_TAIL[3])
        core1.wait()

        def store0(here, val):
            tok_ref[here] = val + da_core[1, here].astype(F32)

        da_rows(0, store0)
        turn(PLAN_TAIL[4])
        turn(PLAN_WAIT)
        far.wait()
        last_tp[tpi] = jnp.zeros((8, width), F32)

        def norm_rows(r, carry):
            here = pl.ds(pl.multiple_of(r * blk, blk), blk)
            da = tok_ref[here] + da_across[here].astype(F32)
            hat, rstd = norm_parts(tiles_ref[here].astype(F32))
            tok_ref[here] = norm_back(hat, rstd, row_of(gain_ref), da)
            last_tp[tpi, 0:1] += jnp.sum(da * hat, axis=0, keepdims=True)
            last_tp[tpi, 1:2] += jnp.sum(da, axis=0, keepdims=True)
            return carry

        lax.fori_loop(0, rows_dev // blk, norm_rows, 0)

        def last_copy(axis, m):
            buf, me = (last_tp, tpi) if axis == "tp" else (last_dp, dpi)
            at = 0 if axis == "tp" else tp_size
            return remote(
                buf.at[me], buf.at[me], vec_send.at[1, at + m], vec_recv.at[1, at + m], axis, m
            )

        for m in range(1, tp_size):
            last_copy("tp", m).start()
        turn(PLAN_LAST[0])
        for m in range(1, tp_size):
            last_copy("tp", m).wait()
        total = last_tp[0]
        for k in range(1, tp_size):
            total = total + last_tp[k]
        last_dp[dpi] = total
        last_dp[dpi, 2:3] = onehot_ref[...]
        for m in range(1, dp_size):
            last_copy("dp", m).start()
        turn(PLAN_LAST[1])
        for m in range(1, dp_size):
            last_copy("dp", m).wait()

        last_ref[0:1] = jnp.sum(last_dp[:, 0, :], axis=0, keepdims=True)
        shares = last_dp[:, 1, :]
        last_ref[1:2] = jnp.sum(shares, axis=0, keepdims=True)
        leads = last_ref.shape[0] - 8
        hot = last_dp[:, 2, 0:128]
        for k in range(leads):
            last_ref[8 + k : 9 + k] = jnp.sum(hot[:, k : k + 1] * shares, axis=0, keepdims=True)
        turn(PLAN_LAST[2])
        while small_done[0] <= len(ladder):
            small_event(small_done[0])
            small_done[0] += 1
        turn(PLAN_END)
        while any(done[k] <= work[k].n for k in range(len(work))):
            turn(range(len(work)))
        sum_ref[...] = small_in[...]
        head_out = [head_local(head_chunk[0])]
        for p in range(1, tp_size):
            head_remote(head_chunk[0], p).wait()
            out = pltpu.make_async_copy(
                hg.at[p - 1], rows_at(head_ref, partner_any(tpi, p) * hr, hr),
                local_sems.at[p, 3],
            )
            out.start()
            head_out.append(out)
        for out in head_out:
            out.wait()
        for ch in work:
            ch.out_copy().wait()


def partner_any(index, mask):
    bit = 1
    while bit <= mask:
        if mask & bit:
            index = partner(index, bit)
        bit *= 2
    return index


PLAN_FIRST = (4, 2)
PLAN_STEPS = ((0, 1), (4, 2, 0, 1, 3), (), (3,), (4, 2), (), (), (4,), (2, 0, 1, 4), (5, 3, 2), (4,), (2, 5),)
PLAN_TAIL = ((), (4, 0), (), (3,), (2,),)
PLAN_WAIT = (5, 4, 0, 6, 5, 1, 4, 3, 2, 0)
PLAN_LAST = ((1, 6), (2, 5, 3), (6,),)
PLAN_END = (1, 3, 0, 6, 5, 1, 0, 3, 1, 6, 3, 0, 1, 6)


ORDERS = (
    (2, "X", 1, 4),
    (2, "X", 1, 4),
    (1, "X", 2, 4),
    ("X", 1, 2, 4),
    ("X", 1, 2, 4),
    (1, 2, 4),
    (1, 4, 2),
)


def attn_bwd(qkv, o, lse, do, rows, wt, tiles, gain, onehot, leads, small, parts, mesh, scale):
    _, heads, _, frame = qkv.shape
    rows_dev, width = tiles.shape
    tp_size, dp_size = mesh.shape["tp"], mesh.shape["dp"]
    nbits = dp_size.bit_length() - 1
    half = width // 2
    ph_rows = parts[2].shape[1]
    chunks = [
        dict(tp=True, rows=half, part=0, order=ORDERS[0], out=(0, 0)),
        dict(tp=True, rows=half, part=1, order=ORDERS[1], out=(0, half)),
        dict(tp=True, rows=half, part=0, order=ORDERS[2], out=(1, 0)),
        dict(tp=True, rows=half, part=1, order=ORDERS[3], out=(1, half)),
        dict(tp=True, rows=ph_rows, part=0, order=ORDERS[4], out=(2, 0), head=(heads * HD, HEAD_ROWS)),
        dict(tp=False, rows=half, order=ORDERS[5], out=(3, 0)),
        dict(tp=False, rows=256, order=ORDERS[6], out=(3, half)),
    ]
    n_k = len(chunks)
    scratch = [
        pltpu.VMEM((frame, HD), BF16),
        pltpu.VMEM((frame, HD), BF16),
        pltpu.VMEM((frame, HD), F32),
        pltpu.VMEM((frame, HD), F32),
        pltpu.VMEM((tp_size, heads, HD, rows_dev), BF16),
        pltpu.VMEM((3, heads, HD, frame), BF16),
        pltpu.VMEM((3, rows_dev, width), BF16),
        pltpu.VMEM((2, rows_dev, width), BF16),
        pltpu.VMEM((rows_dev, width), BF16),
        pltpu.VMEM((16, width), F32),
        pltpu.VMEM((2 + nbits, 16, width), F32),
        pltpu.VMEM((tp_size, 8, width), F32),
        pltpu.VMEM((dp_size, 8, width), F32),
        pltpu.VMEM((tp_size - 1, HEAD_ROWS, width), BF16),
    ]
    for c in chunks:
        r = c["rows"]
        scratch.append(pltpu.VMEM((r, width), BF16))
        scratch.append(pltpu.VMEM((2, r // 2, width), BF16))
        scratch.append(pltpu.VMEM((2, r // 4, width), BF16))
        scratch.append(pltpu.VMEM((2 + max(nbits - 3, 0), r // 8, width), BF16))
        if c["tp"]:
            scratch += [pltpu.VMEM((r, width), BF16)] * 4
        else:
            scratch.append(pltpu.VMEM((r, width), BF16))
    scratch += [
        pltpu.SemaphoreType.DMA((n_k, 17)),
        pltpu.SemaphoreType.DMA((n_k, 17)),
        pltpu.SemaphoreType.DMA((n_k, 4)),
        pltpu.SemaphoreType.DMA((tp_size,)),
        pltpu.SemaphoreType.DMA((tp_size,)),
        pltpu.SemaphoreType.DMA,
        pltpu.SemaphoreType.DMA((3,)),
        pltpu.SemaphoreType.DMA((3,)),
        pltpu.SemaphoreType.DMA((2, tp_size + dp_size)),
        pltpu.SemaphoreType.DMA((2, tp_size + dp_size)),
        pltpu.SemaphoreType.DMA((tp_size - 1,)),
        pltpu.SemaphoreType.DMA((tp_size - 1,)),
    ]
    any_spec = pl.BlockSpec(memory_space=pl.ANY)
    vmem = pl.BlockSpec(memory_space=pltpu.VMEM)
    return pl.pallas_call(
        functools.partial(
            bwd_kernel, scale=scale, chunks=chunks, dp_size=dp_size, heads=heads,
            tp_size=tp_size, width=width,
        ),
        grid=(heads, tp_size),
        in_specs=[vmem, vmem, vmem, any_spec] + [vmem] * 6 + [any_spec] * len(parts),
        out_specs=[vmem, vmem, vmem, any_spec] + [any_spec] * 4,
        out_shape=[
            jax.ShapeDtypeStruct((rows_dev, width), F32),
            jax.ShapeDtypeStruct((16, width), F32),
            jax.ShapeDtypeStruct((8 + leads, width), F32),
            jax.ShapeDtypeStruct((tp_size * HEAD_ROWS, width), BF16),
        ]
        + [
            jax.ShapeDtypeStruct((rows, width), BF16)
            for rows in (width, width, ph_rows, half + chunks[-1]["rows"])
        ],
        scratch_shapes=scratch,
        compiler_params=pltpu.CompilerParams(
            vmem_limit_bytes=60 << 20, collective_id=1, has_side_effects=True
        ),
        cost_estimate=pl.CostEstimate(
            flops=60_000_000_000, bytes_accessed=30 << 20, transcendentals=heads * frame * frame
        ),
        name="attn_bwd",
    )(qkv, o, lse, do, rows, wt, tiles, gain, onehot, small, *parts)


def mid_kernel(
    tiles_ref, o_ref, dots_ref, off_ref, pb_ref, g2_ref, s2_ref, nb_ref, hw_ref, hb_ref, scale_ref,
    pj_own, pj_far, wi_own, wi_far, na_own, na_far,
    dn_ref, dw_ref, ph_ref, do_ref, dx1_ref, small_ref, gates_ref, corr_ref,
    pj, wi, na, x1, hat, rstd, c_low, act, slope, h_low, hg, dx2, dz, du, dc, dy, hd, dn, dw, ph, dos,
    in_sem, out_sem, *, tp_size, heads
):
    tpi = lax.axis_index("tp")
    rows_dev, width = tiles_ref.shape
    nh = heads * HD
    half = rows_dev // 2
    blocks = [pl.ds(r * half, half) for r in range(2)]

    def loads(k, own, far, dst):
        out = []
        for p in range(tp_size):
            src = own if p == 0 else far.at[p - 1]
            n = src.shape[0]
            to = dst.at[pl.ds(p * n, n)] if len(dst.shape) == 2 else dst.at[p]
            out.append(pltpu.make_async_copy(src, to, in_sem.at[k, p]))
        return out

    load_pj = loads(0, pj_own, pj_far, pj)
    load_wi = loads(1, wi_own, wi_far, wi)
    load_na = loads(2, na_own, na_far, na)
    for cp in load_pj + load_wi + load_na:
        cp.start()
    small_ref[...] = jnp.zeros_like(small_ref)
    proj_bias, gain2, shift2, out_bias = (row_of(v) for v in (pb_ref, g2_ref, s2_ref, nb_ref))
    for cp in load_pj:
        cp.wait()
    for r in blocks:
        v = tiles_ref[r].astype(F32) + dot(o_ref[:, r], pj[...], ((0,), (0,))) + proj_bias
        x1[r] = v
        hv, rs = norm_parts(v)
        hat[r] = hv
        rstd[r] = rs
        c_low[r] = (hv * gain2 + shift2).astype(BF16)
    for p in range(tp_size):
        load_wi[p].wait()
        cols = pl.ds(p * width, width)
        for r in blocks:
            m, d = gelu_parts(dot(c_low[r], wi[p]) + off_ref[p, 0:1])
            act[r, cols] = m.astype(BF16)
            slope[r, cols] = d
    for cp in load_na:
        cp.wait()
    for r in blocks:
        h_low[r] = (x1[r] + dot(act[r], na[...]) + out_bias).astype(BF16)

    logits = dot(hw_ref[...], h_low[...], ((1,), (1,))) + hb_ref[...]
    row_scale = scale_ref[0:1, 0:1]
    lg = [logits[e * HEAD_ROWS : (e + 1) * HEAD_ROWS] for e in range(EXPERTS)]
    top = jnp.maximum(jnp.maximum(lg[0], lg[1]), lg[2])
    ex = [jnp.exp(v - top) for v in lg]
    inv = 1.0 / (ex[0] + ex[1] + ex[2])
    gt = [v * inv for v in ex]
    mixed = gt[0] * dots_ref[0] + gt[1] * dots_ref[1] + gt[2] * dots_ref[2]
    for e in range(EXPERTS):
        gates_ref[e] = gt[e]
        hg[e * HEAD_ROWS : (e + 1) * HEAD_ROWS] = (gt[e] * (dots_ref[e] - mixed)).astype(BF16)
    hg[EXPERTS * HEAD_ROWS :] = (dots_ref[EXPERTS] * row_scale).astype(BF16)
    corr_ref[...] = logits[EXPERTS * HEAD_ROWS :] * row_scale
    d2 = dot(hg[...], hw_ref[...], ((0,), (0,)))
    dx2[...] = d2
    dz[...] = d2.astype(BF16)
    small_ref[0:1] = jnp.sum(d2, axis=0, keepdims=True)
    ones = jnp.ones((8, rows_dev), BF16)
    small_ref[4:5, : tp_size * HEAD_ROWS] = dot(ones, hg[...], ((1,), (1,)))[0:1]

    def send_out(k, p, src, dst):
        cp = pltpu.make_async_copy(src, dst, out_sem.at[k, p])
        cp.start()
        return cp

    outs = []
    for p in range(tp_size):
        cols = pl.ds(p * width, width)
        dn[p] = dot(act[:, cols], dz[...], ((0,), (0,))).astype(BF16)
        outs.append(send_out(0, p, dn.at[p], dn_ref.at[p]))
    for p in range(tp_size):
        cols = pl.ds(p * width, width)
        for r in blocks:
            v = dot(dz[r], na[cols], ((1,), (1,))) * slope[r, cols]
            low = v.astype(BF16)
            du[p, r] = low
            small_ref[8 + p : 9 + p] += jnp.sum(low.astype(F32), axis=0, keepdims=True)
    for p in range(tp_size):
        dw[p] = dot(c_low[...], du[p], ((0,), (0,))).astype(BF16)
        outs.append(send_out(1, p, dw.at[p], dw_ref.at[p]))
    for r in blocks:
        g = dot(du[0, r], wi[0], ((1,), (1,)))
        for p in range(1, tp_size):
            g = g + dot(du[p, r], wi[p], ((1,), (1,)))
        hv = hat[r]
        d1 = dx2[r] + norm_back(hv, rstd[r], gain2, g)
        dx1_ref[r] = d1
        dy[r] = d1.astype(BF16)
        small_ref[1:2] += jnp.sum(g * hv, axis=0, keepdims=True)
        small_ref[2:3] += jnp.sum(g, axis=0, keepdims=True)
        small_ref[3:4] += jnp.sum(d1, axis=0, keepdims=True)
    dos[...] = dot(pj[...], dy[...], ((1,), (1,))).astype(BF16).reshape(dos.shape)
    outs.append(send_out(2, 0, dos, do_ref))
    dp = dot(o_ref[...], dy[...]).astype(BF16)
    hd[...] = dot(hg[...], h_low[...]).astype(BF16)
    for p in range(tp_size):
        ph[p, 0:nh] = dp[p * nh : (p + 1) * nh]
        at = pl.ds(pl.multiple_of(partner_any(tpi, p) * HEAD_ROWS, 16), HEAD_ROWS)
        ph[p, nh : nh + HEAD_ROWS] = hd[at]
        ph[p, nh + HEAD_ROWS :] = jnp.zeros((ph.shape[1] - nh - HEAD_ROWS, width), BF16)
        outs.append(send_out(3, p, ph.at[p], ph_ref.at[p]))
    for cp in outs:
        cp.wait()


def mid(tiles, o_own, dots, off, vecs, hw, hb, row_scale, weights, mesh, heads):
    rows_dev, width = tiles.shape
    tp_size = mesh.shape["tp"]
    nh = heads * HD
    ph_rows = -(-(nh + HEAD_ROWS) // 128) * 128
    n_head = hw.shape[0]
    any_spec = pl.BlockSpec(memory_space=pl.ANY)
    vmem = pl.BlockSpec(memory_space=pltpu.VMEM)
    big = (tp_size, width, width)
    return pl.pallas_call(
        functools.partial(mid_kernel, tp_size=tp_size, heads=heads),
        in_specs=[vmem] * 11 + [any_spec] * 6,
        out_specs=[any_spec] * 4 + [vmem] * 4,
        out_shape=[
            jax.ShapeDtypeStruct(big, BF16),
            jax.ShapeDtypeStruct(big, BF16),
            jax.ShapeDtypeStruct((tp_size, ph_rows, width), BF16),
            jax.ShapeDtypeStruct((tp_size, heads, HD, rows_dev), BF16),
            jax.ShapeDtypeStruct((rows_dev, width), F32),
            jax.ShapeDtypeStruct((16, width), F32),
            jax.ShapeDtypeStruct((EXPERTS, HEAD_ROWS, rows_dev), F32),
            jax.ShapeDtypeStruct((HEAD_ROWS, rows_dev), F32),
        ],
        scratch_shapes=[
            pltpu.VMEM((tp_size * nh, width), BF16),
            pltpu.VMEM(big, BF16),
            pltpu.VMEM((tp_size * width, width), BF16),
            pltpu.VMEM((rows_dev, width), F32),
            pltpu.VMEM((rows_dev, width), F32),
            pltpu.VMEM((rows_dev, 1), F32),
            pltpu.VMEM((rows_dev, width), BF16),
            pltpu.VMEM((rows_dev, tp_size * width), BF16),
            pltpu.VMEM((rows_dev, tp_size * width), F32),
            pltpu.VMEM((rows_dev, width), BF16),
            pltpu.VMEM((n_head, rows_dev), BF16),
            pltpu.VMEM((rows_dev, width), F32),
            pltpu.VMEM((rows_dev, width), BF16),
            pltpu.VMEM((tp_size, rows_dev, width), BF16),
            pltpu.VMEM((8, width), F32),
            pltpu.VMEM((rows_dev, width), BF16),
            pltpu.VMEM((n_head, width), BF16),
            pltpu.VMEM(big, BF16),
            pltpu.VMEM(big, BF16),
            pltpu.VMEM((tp_size, ph_rows, width), BF16),
            pltpu.VMEM((tp_size, heads, HD, rows_dev), BF16),
            pltpu.SemaphoreType.DMA((3, tp_size)),
            pltpu.SemaphoreType.DMA((4, tp_size)),
        ],
        compiler_params=pltpu.CompilerParams(vmem_limit_bytes=60 << 20),
        cost_estimate=pl.CostEstimate(
            flops=18_000_000_000, bytes_accessed=30 << 20, transcendentals=2_000_000
        ),
        name="mid",
    )(tiles, o_own, dots, off, *vecs, hw, hb, row_scale, *weights)


def finish_kernel(
    n_ref, i_ref, ph_ref, qa_ref, qb_ref, hd_ref, tok_ref, dx_ref, table_ref,
    no_ref, io_ref, po_ref, qo_ref, g_ref, c_ref, to_ref, lead_ref, *, fields
):
    no_ref[...] = n_ref[...].astype(F32)
    io_ref[...] = i_ref[...].astype(F32)
    po_ref[...] = ph_ref[...].astype(F32)
    na = qa_ref.shape[0]
    qo_ref[0, :na] = qa_ref[...].astype(F32)
    qo_ref[0, na:] = qb_ref[...].astype(F32)
    for e in range(EXPERTS):
        g_ref[e * fields : (e + 1) * fields] = hd_ref[pl.ds(e * HEAD_ROWS, HEAD_ROWS)].astype(F32)[
            :fields
        ]
    c_ref[...] = hd_ref[pl.ds(EXPERTS * HEAD_ROWS, HEAD_ROWS)].astype(F32)[:fields]
    to_ref[...] = tok_ref[...] + dx_ref[...]
    lead_ref[...] = table_ref[8:]


def finish(n, i, ph, q, hd, tok, dx1, table, heads, fields):
    width = n.shape[0]
    nh = heads * HD
    steps = 3
    rows = width // steps
    first = (width // 2) // (3 * HD) * HD
    second = nh - first
    base = 3 * first // second
    tok_rows = tok.shape[0] // 2
    leads = table.shape[0] - 8

    def by_row(r):
        return pl.BlockSpec((r, width), lambda g: (g, 0))

    token = pl.BlockSpec((tok_rows, width), lambda g: (jnp.minimum(g, 1), 0))
    return pl.pallas_call(
        functools.partial(finish_kernel, fields=fields),
        grid=(steps,),
        in_specs=[
            by_row(rows),
            by_row(rows),
            by_row(nh // steps),
            by_row(first),
            pl.BlockSpec((second, width), lambda g: (base + g, 0)),
            pl.BlockSpec((hd.shape[0], rows), lambda g: (0, g)),
            token,
            token,
            pl.BlockSpec(table.shape, lambda g: (0, 0)),
        ],
        out_specs=[
            by_row(rows),
            by_row(rows),
            by_row(nh // steps),
            pl.BlockSpec((1, nh, width), lambda g: (g, 0, 0)),
            pl.BlockSpec((EXPERTS * fields, rows), lambda g: (0, g)),
            pl.BlockSpec((fields, rows), lambda g: (0, g)),
            token,
            pl.BlockSpec((leads, width), lambda g: (0, 0)),
        ],
        out_shape=[
            jax.ShapeDtypeStruct((width, width), F32),
            jax.ShapeDtypeStruct((width, width), F32),
            jax.ShapeDtypeStruct((nh, width), F32),
            jax.ShapeDtypeStruct((3, nh, width), F32),
            jax.ShapeDtypeStruct((EXPERTS * fields, width), F32),
            jax.ShapeDtypeStruct((fields, width), F32),
            jax.ShapeDtypeStruct(tok.shape, F32),
            jax.ShapeDtypeStruct((leads, width), F32),
        ],
        name="finish",
    )(n, i, ph, q, q, hd, tok, dx1, table)


def norm_parts(values):
    center = values - jnp.mean(values, axis=-1, keepdims=True)
    rstd = lax.rsqrt(jnp.mean(center * center, axis=-1, keepdims=True) + EPSILON)
    return center * rstd, rstd


def norm_back(hat, rstd, gain, grad):
    g = grad * gain
    return rstd * (
        g
        - jnp.mean(g, axis=-1, keepdims=True)
        - hat * jnp.mean(g * hat, axis=-1, keepdims=True)
    )


def gelu_parts(u):
    half = jnp.exp(-0.5 * u * u)
    t = 1.0 / (1.0 + (0.3275911 * 0.7071067811865476) * jnp.abs(u))
    poly = t * (
        0.254829592
        + t * (-0.284496736 + t * (1.421413741 + t * (-1.453152027 + t * 1.061405429)))
    )
    tail = 0.5 * poly * half
    cdf = jnp.where(u >= 0, 1.0 - tail, tail)
    return u * cdf, cdf + u * half * 0.3989422804014327


def make_body(mesh):
    tp_size = mesh.shape["tp"]

    def body(
        tile_vectors,
        snapshot_horizon_slot,
        horizon_sample_tally,
        specialist_outlooks,
        early_layernorm_scale,
        early_layernorm_shift,
        horizon_vectors,
        triple_head_matrix,
        attending_matrix,
        attending_offset,
        later_layernorm_scale,
        later_layernorm_shift,
        widening_matrix,
        widening_offset,
        narrowing_matrix,
        narrowing_offset,
        router_matrix,
        router_offset,
        adjuster_matrix,
        adjuster_offset,
        combined_loss_slope,
    ):
        rows_dev, width = tile_vectors.shape
        heads = triple_head_matrix.shape[2] // HD
        rows_frame = rows_dev * tp_size
        fields = adjuster_matrix.shape[1]
        sites = combined_loss_slope.shape[1]
        scale_val = HD ** (-0.5)
        tp_index = lax.axis_index("tp")
        lead = snapshot_horizon_slot[0]
        row_scale = lax.rsqrt(
            lax.dynamic_slice_in_dim(horizon_sample_tally, lead, 1, 0).astype(F32)
        )[0]
        nh = heads * HD
        w_t = jnp.transpose(triple_head_matrix, (0, 2, 1))
        (attn_rows, qkv, o_heads, lse, o_own, dots, off_all, proj_all, wide_all, narrow_all) = attn_fwd(
            snapshot_horizon_slot,
            tile_vectors,
            early_layernorm_scale,
            early_layernorm_shift,
            horizon_vectors,
            widening_offset,
            w_t,
            attending_matrix,
            widening_matrix,
            narrowing_matrix,
            specialist_outlooks,
            combined_loss_slope,
            mesh,
            scale_val,
        )

        def head_pad(x):
            x = x.reshape((EXPERTS + 1, fields) + x.shape[1:])
            x = jnp.pad(x, ((0, 0), (0, HEAD_ROWS - fields)) + ((0, 0),) * (x.ndim - 2))
            return x.reshape((-1,) + x.shape[2:])

        hw = head_pad(jnp.concatenate([router_matrix, adjuster_matrix], axis=1).T)
        hb = head_pad(jnp.concatenate([router_offset, adjuster_offset])[:, None])
        vec = (attending_offset, later_layernorm_scale, later_layernorm_shift, narrowing_offset)
        (d_narrow, d_wide, d_ph, do_all, dx1, small, gates, corr) = mid(
            tile_vectors,
            o_own.reshape(tp_size * nh, rows_dev),
            dots,
            off_all,
            vec,
            hw,
            hb,
            row_scale[None, None],
            [
                attending_matrix, proj_all, widening_matrix, wide_all,
                narrowing_matrix, narrow_all,
            ],
            mesh,
            heads,
        )
        gates = gates[:, :fields]
        corr = corr[:fields]

        blended = (corr)[:, None, :]
        for e in range(EXPERTS):
            blended = blended + gates[e][:, None, :] * specialist_outlooks[e].astype(F32)

        leads = horizon_vectors.shape[0]
        onehot = (jnp.arange(width, dtype=jnp.int32) == lead).astype(F32)[None, :]
        (token_part, small, table, head_sum, n_low, i_low, ph, q_low) = attn_bwd(
            qkv, o_heads, lse, do_all, attn_rows.reshape(rows_frame, width), w_t.reshape(3 * nh, width), tile_vectors,
            early_layernorm_scale, onehot, leads, small,
            [d_narrow, d_wide, d_ph], mesh, scale_val,
        )
        (
            narrow_sum, wide_sum, proj_weight_grad, qkv_sum, gate_sum, correct_sum, tokens_grad,
            lead_sum,
        ) = finish(
            n_low, i_low, ph, q_low, head_sum, token_part, dx1, table, heads, fields
        )
        qkv_sum = jnp.transpose(qkv_sum, (0, 2, 1))
        gate_weight_grad = gate_sum.T
        correct_weight_grad = correct_sum.T
        head_bias = small[4, : (EXPERTS + 1) * HEAD_ROWS].reshape(EXPERTS + 1, HEAD_ROWS)
        head_bias = head_bias[:, :fields]
        in_bias_grad = small[8]

        return (
            blended,
            tokens_grad,
            table[0],
            table[1],
            lead_sum,
            qkv_sum,
            proj_weight_grad,
            small[3],
            small[1],
            small[2],
            wide_sum,
            in_bias_grad,
            narrow_sum,
            small[0],
            gate_weight_grad,
            head_bias[:EXPERTS].reshape(EXPERTS * fields),
            correct_weight_grad,
            head_bias[EXPERTS],
        )

    return body


def solution(mesh):
    return jax.shard_map(
        make_body(mesh),
        mesh=mesh,
        in_specs=(
            P(("dp", "tp"), None),
            P("dp"),
            P(),
            P(None, None, None, ("dp", "tp")),
            P(),
            P(),
            P(),
            P(None, None, "tp"),
            P("tp", None),
            P(),
            P(),
            P(),
            P(None, "tp"),
            P("tp"),
            P("tp", None),
            P(),
            P(),
            P(),
            P(),
            P(),
            P(None, None, ("dp", "tp")),
        ),
        out_specs=(
            P(None, None, ("dp", "tp")),
            P(("dp", "tp"), None),
            P(),
            P(),
            P(),
            P(None, None, "tp"),
            P("tp", None),
            P(),
            P(),
            P(),
            P(None, "tp"),
            P("tp"),
            P("tp", None),
            P(),
            P(),
            P(),
            P(),
            P(),
        ),
        check_vma=False,
    )
```

```python
import functools
import jax
import jax.numpy as jnp
from jax import lax
from jax.experimental import pallas as pl
from jax.experimental.pallas import tpu as pltpu
from jax.sharding import PartitionSpec as P

HD = 64
EXPERTS = 3
HEAD_ROWS = 80
MID_VMEM = 62 << 20
PRE_BIT = 2
EPSILON = 1e-05
F32 = jnp.float32
BF16 = jnp.bfloat16


def dot(a, b, dims=((1,), (0,))):
    return lax.dot_general(a, b, (dims, ((), ())), preferred_element_type=F32)


def row_of(ref):
    return ref[...].reshape(1, ref.shape[0])


W_FLIGHT = 2
W_PLAN = (
    (0, (("far", 0),)),
    (1, (("far", 1),)),
    (3, (("far", 2), (0, 0))),
    (4, ((0, 1),)),
    (5, ((0, 2),)),
    (6, (("far", 3),)),
    (7, ((1, 1),)),
    (9, (("far", 4),)),
    (10, ((1, 2), (0, 3), ("far", 5))),
    (11, ((0, 4), (0, 5))),
)


def fwd_kernel(
    lead_ref, tiles_ref, gain_ref, shift_ref, table_ref, off_ref, wt_ref, proj_ref, wide_ref,
    narrow_ref, exp_ref, slope_ref,
    rows_out, qkv_ref, o_ref, lse_ref, own_out, dots_ref, off_out, proj_all, wide_all, narrow_all,
    offs, off_send, off_recv, rows_ref, own_ref, out_sem, ks, stream, stream_g, stream_sem, row_send, row_recv, o_send, o_recv, o_local,
    w_send, w_recv, *, scale, dp_size, tp_size, heads
):
    i, h = pl.program_id(0), pl.program_id(1)
    steps = tp_size * heads
    step = i * heads + h
    dpi, tpi = lax.axis_index("dp"), lax.axis_index("tp")
    rows_dev, width = tiles_ref.shape
    piece = rows_dev // 2

    def remote(src, dst, ssem, rsem, axis, bit):
        dev = (partner(dpi, bit), tpi) if axis == "dp" else (dpi, partner_any(tpi, bit))
        return pltpu.make_async_remote_copy(
            src_ref=src, dst_ref=dst, send_sem=ssem, recv_sem=rsem,
            device_id=dev, device_id_type=pl.DeviceIdType.MESH,
        )

    def row_copy(kind, c):
        a, b, bit = ((0, 1, 1), (0, 2, 2), (2, 3, 1))[kind]
        here = pl.ds(c * piece, piece)
        return remote(
            rows_ref.at[a, here], rows_ref.at[b, here],
            row_send.at[kind, c], row_recv.at[kind, c], "tp", bit,
        )

    def off_copy(m):
        return remote(offs.at[0], offs.at[m], off_send.at[m], off_recv.at[m], "tp", m)

    parts = []
    for src, dst, cuts, share in (
        (proj_ref, proj_all, (1,), (1,)),
        (narrow_ref, narrow_all, (2, 2), (1, 2)),
        (wide_ref, wide_all, (2, 3, 6), (1,)),
    ):
        lo = 0
        for cut in cuts:
            n = src.shape[0] // cut
            parts.append((src, dst, lo, n, share))
            lo += n

    def w_rows(n, stage, theirs=False):
        _, _, lo, size, share = parts[n]
        size = size // (1 << len(share))
        for bit in share[:stage]:
            size *= 2
        at = lo
        step = size
        for k, bit in enumerate(share[stage:]):
            mine = lax.rem(lax.div(dpi, bit), 2)
            if theirs and k == 0:
                mine = 1 - mine
            at = at + mine * step
            step *= 2
        return pl.ds(pl.multiple_of(at, 16), size)

    def w_far(n):
        src, dst = parts[n][:2]
        rows = w_rows(n, 0)
        return remote(
            src.at[rows], dst.at[1, rows], w_send.at[n, 0], w_recv.at[n, 0], "tp", 2
        )

    def w_side(n, k):
        rows = w_rows(n, k)
        here = parts[n][1].at[1, rows]
        return remote(
            here, here, w_send.at[n, 1 + k], w_recv.at[n, 1 + k], "dp", parts[n][4][k]
        )

    def w_fwd(n, k):
        dst = parts[n][1]
        rows = w_rows(n, 0) if k == 0 else w_rows(n, k - 1, True)
        return remote(
            dst.at[1, rows], dst.at[2, rows], w_send.at[n, 3 + k], w_recv.at[n, 3 + k], "tp", 1
        )

    def w_near(n):
        src, dst, lo, size, _ = parts[n]
        rows = pl.ds(lo, size)
        return remote(src.at[rows], dst.at[0, rows], w_send.at[n, 6], w_recv.at[n, 6], "tp", 1)

    def o_copy(p):
        if p == 0:
            return pltpu.make_async_copy(o_ref.at[0], own_ref.at[0], o_local)
        return remote(o_ref.at[p], own_ref.at[p], o_send.at[p], o_recv.at[p], "tp", p)

    fields, sites = slope_ref.shape[0], slope_ref.shape[1]
    per = stream.shape[2]
    groups = fields // per
    depth = stream.shape[0]

    def stream_copies(g):
        slot = lax.rem(g, depth)
        at = pl.ds(g * per, per)
        return (
            pltpu.make_async_copy(
                exp_ref.at[:, at], stream.at[slot], stream_sem.at[slot, 0]
            ),
            pltpu.make_async_copy(
                slope_ref.at[at], stream_g.at[slot], stream_sem.at[slot, 1]
            ),
        )

    @pl.when(step == 0)
    def _():
        barrier = pltpu.get_barrier_semaphore()
        others = [("tp", 1), ("tp", 2), ("tp", 3), ("dp", 1), ("dp", 2)]
        for axis, bit in others:
            dev = (partner(dpi, bit), tpi) if axis == "dp" else (dpi, partner_any(tpi, bit))
            pl.semaphore_signal(
                barrier, inc=1, device_id=dev, device_id_type=pl.DeviceIdType.MESH
            )
        for g in range(min(depth - 1, groups)):
            for cp in stream_copies(g):
                cp.start()
        blk = 64
        gain = row_of(gain_ref)
        shift = row_of(shift_ref) + table_ref[pl.ds(lead_ref[0], 1)]
        offs[0, 0:1] = row_of(off_ref)

        def norm_rows(r, carry):
            here = pl.ds(pl.multiple_of(r * blk, blk), blk)
            hat, _ = norm_parts(tiles_ref[here].astype(F32))
            rows_ref[0, here] = (hat * gain + shift).astype(BF16)
            return carry

        half = piece // blk
        lax.fori_loop(0, half, norm_rows, 0)
        pl.semaphore_wait(barrier, len(others))
        row_copy(1, 0).start()
        lax.fori_loop(half, 2 * half, norm_rows, 0)
        row_copy(1, 1).start()
        row_copy(0, 0).start()
        row_copy(0, 1).start()
        for m in range(1, tp_size):
            off_copy(m).start()

        def contract(g, carry):
            @pl.when(g + depth - 1 < groups)
            def _():
                for cp in stream_copies(g + depth - 1):
                    cp.start()

            for cp in stream_copies(g):
                cp.wait()
            slot = lax.rem(g, depth)
            for j in range(per):
                slope = stream_g[slot, j].astype(F32)
                for e in range(EXPERTS):
                    dots_ref[e, pl.ds(g * per + j, 1)] = jnp.sum(
                        stream[slot, e, j].astype(F32) * slope, axis=0, keepdims=True
                    )
                dots_ref[EXPERTS, pl.ds(g * per + j, 1)] = jnp.sum(slope, axis=0, keepdims=True)
            return carry

        dots_ref[...] = jnp.zeros_like(dots_ref)
        lax.fori_loop(0, groups, contract, 0)

        def project(p):
            lane = pl.ds(p * rows_dev, rows_dev)
            for s in range(3):
                part = dot(wt_ref[s], rows_ref[p], ((1,), (1,))).astype(BF16)
                qkv_ref[s, :, :, lane] = part.reshape(heads, HD, rows_dev)
            for hh in range(heads):
                ks[hh, lane] = qkv_ref[1, hh, :, lane].T

        project(0)
        for c in range(2):
            row_copy(0, c).wait()
        project(1)
        for c in range(2):
            row_copy(1, c).wait()
            row_copy(2, c).start()
        for n in range(W_FLIGHT):
            w_far(n).start()
        project(2)
        for c in range(2):
            row_copy(2, c).wait()
        for n in range(len(parts)):
            w_near(n).start()
        rows_copy = pltpu.make_async_copy(rows_ref, rows_out, out_sem.at[0])
        rows_copy.start()
        project(3)

    p = lax.rem(i + 2, tp_size)
    lanes = pl.ds(pl.multiple_of(p * rows_dev, rows_dev), rows_dev)
    q = qkv_ref[0, h, :, lanes] * jnp.bfloat16(scale)
    s = dot(ks[h], q)
    m = jnp.max(s, axis=0, keepdims=True)
    e = jnp.exp(s - m)
    l = jnp.sum(e, axis=0, keepdims=True)
    o_ref[p, h] = (dot(qkv_ref[2, h], e.astype(BF16)) / l).astype(BF16)
    lse_ref[p, h] = m + jnp.log(l)

    seq = {}

    def after(st, *what):
        seq.setdefault(min(st, steps - 1), []).extend(what)

    for st, what in W_PLAN:
        after(st, *what)
    for st, what in seq.items():

        @pl.when(step == st)
        def _():
            for kind, n in what:
                if kind == "far":
                    w_far(n).wait()
                    if n + W_FLIGHT < len(parts):
                        w_far(n + W_FLIGHT).start()
                    w_side(n, 0).start()
                    w_fwd(n, 0).start()
                else:
                    w_side(n, kind).wait()
                    if kind + 1 < len(parts[n][4]):
                        w_side(n, kind + 1).start()
                    w_fwd(n, kind + 1).start()

    for k in range(tp_size):

        @pl.when(step == k * heads + heads - 1)
        def _():
            o_copy((k + 2) % tp_size).start()

    @pl.when(step == steps - 1)
    def _():
        for k in range(tp_size):
            o_copy(k).wait()
        for m in range(1, tp_size):
            off_copy(m).wait()
        off_out[...] = offs[...]
        own_copy = pltpu.make_async_copy(own_ref, own_out, out_sem.at[1])
        own_copy.start()
        for n in range(len(parts)):
            w_near(n).wait()
            for k in range(1 + len(parts[n][4])):
                w_fwd(n, k).wait()
        own_copy.wait()
        pltpu.make_async_copy(rows_ref, rows_out, out_sem.at[0]).wait()


def attn_fwd(
    lead, tiles, gain, shift, table, off, wt, proj, wide, narrow, experts, slope, mesh, scale
):
    rows_dev, width = tiles.shape
    heads = proj.shape[0] // HD
    tp_size, dp_size = mesh.shape["tp"], mesh.shape["dp"]
    frame = tp_size * rows_dev
    fields, sites = slope.shape[0], slope.shape[1]
    per = 3 if fields % 3 == 0 else 1
    depth = 4
    any_spec = pl.BlockSpec(memory_space=pl.ANY)
    vmem = pl.BlockSpec(memory_space=pltpu.VMEM)
    return pl.pallas_call(
        functools.partial(
            fwd_kernel, scale=scale, dp_size=dp_size, tp_size=tp_size, heads=heads
        ),
        grid=(tp_size, heads),
        in_specs=[pl.BlockSpec(memory_space=pltpu.SMEM)] + [vmem] * 6 + [any_spec] * 5,
        out_specs=[any_spec] + [vmem] * 3 + [any_spec, vmem, vmem] + [any_spec] * 3,
        out_shape=[
            jax.ShapeDtypeStruct((tp_size, rows_dev, width), BF16),
            jax.ShapeDtypeStruct((3, heads, HD, frame), BF16),
            jax.ShapeDtypeStruct((tp_size, heads, HD, rows_dev), BF16),
            jax.ShapeDtypeStruct((tp_size, heads, 1, rows_dev), F32),
            jax.ShapeDtypeStruct((tp_size, heads, HD, rows_dev), BF16),
            jax.ShapeDtypeStruct((EXPERTS + 1, HEAD_ROWS, rows_dev), F32),
            jax.ShapeDtypeStruct((tp_size, 8, width), F32),
            jax.ShapeDtypeStruct((tp_size - 1,) + proj.shape, BF16),
            jax.ShapeDtypeStruct((tp_size - 1,) + wide.shape, BF16),
            jax.ShapeDtypeStruct((tp_size - 1,) + narrow.shape, BF16),
        ],
        scratch_shapes=[
            pltpu.VMEM((tp_size, 8, width), F32),
            pltpu.SemaphoreType.DMA((tp_size,)),
            pltpu.SemaphoreType.DMA((tp_size,)),
            pltpu.VMEM((tp_size, rows_dev, width), BF16),
            pltpu.VMEM((tp_size, heads, HD, rows_dev), BF16),
            pltpu.SemaphoreType.DMA((2,)),
            pltpu.VMEM((heads, frame, HD), BF16),
            pltpu.VMEM((depth, EXPERTS, per, sites, rows_dev), BF16),
            pltpu.VMEM((depth, per, sites, rows_dev), BF16),
            pltpu.SemaphoreType.DMA((depth, 2)),
            pltpu.SemaphoreType.DMA((3, 2)),
            pltpu.SemaphoreType.DMA((3, 2)),
            pltpu.SemaphoreType.DMA((tp_size,)),
            pltpu.SemaphoreType.DMA((tp_size,)),
            pltpu.SemaphoreType.DMA,
            pltpu.SemaphoreType.DMA((6, 7)),
            pltpu.SemaphoreType.DMA((6, 7)),
        ],
        compiler_params=pltpu.CompilerParams(
            vmem_limit_bytes=56 << 20, collective_id=0, has_side_effects=True
        ),
        cost_estimate=pl.CostEstimate(
            flops=30_000_000_000, bytes_accessed=40 << 20, transcendentals=heads * frame * frame
        ),
        name="attn_fwd",
    )(lead, tiles, gain, shift, table, off, wt, proj, wide, narrow, experts, slope)


def partner(index, bit):
    return index + bit - 2 * bit * lax.rem(lax.div(index, bit), 2)


def rows_at(ref, start, size):
    return ref.at[pl.ds(pl.multiple_of(start, 16), size)]


def add_rows(dst, src, lead, dst_off, src_off, size):
    step = 48 if size % 48 == 0 else 32

    def one(r, carry):
        here = pl.ds(pl.multiple_of(dst_off + r * step, 16), step)
        there = pl.ds(pl.multiple_of(src_off + r * step, 16), step)
        got = src[there] if lead is None else src[lead, there]
        dst[here] = (dst[here].astype(F32) + got.astype(F32)).astype(BF16)
        return carry

    lax.fori_loop(0, size // step, one, 0)


def bwd_kernel(
    qkv_ref, o_ref, lse_ref, do_ref, rows_ref, wt_ref, tiles_ref, gain_ref, onehot_ref, small_ref,
    *rest, scale, chunks, dp_size, heads, tp_size, width
):
    n_src = sum(1 for c in chunks if c["tp"] and c["part"] == 0)
    srcs = rest[:n_src]
    tok_ref, sum_ref, last_ref, head_ref = rest[n_src : n_src + 4]
    n_out = n_src + 4 + 4
    outs = rest[n_src + 4 : n_out]
    (
        ks, vs, dks, dvs, dos, dqkv, da_far, da_core, da_across,
        small_in, small_got, last_tp, last_dp, hg,
    ) = rest[n_out : n_out + 14]
    per = rest[n_out + 14 : -12]
    (
        send_sems, recv_sems, local_sems, do_send, do_recv, do_local, da_send, da_recv,
        vec_send, vec_recv, hg_send, hg_recv,
    ) = rest[-12:]
    h, i = pl.program_id(0), pl.program_id(1)
    steps = tp_size * heads
    step = h * tp_size + i
    dpi, tpi = lax.axis_index("dp"), lax.axis_index("tp")
    rows_dev = dos.shape[3]
    bits = [1 << b for b in range(dp_size.bit_length() - 1)]

    def remote(src, dst, ssem, rsem, axis, bit):
        dev = (partner_any(dpi, bit), tpi) if axis == "dp" else (dpi, partner_any(tpi, bit))
        return pltpu.make_async_remote_copy(
            src_ref=src, dst_ref=dst, send_sem=ssem, recv_sem=rsem,
            device_id=dev, device_id_type=pl.DeviceIdType.MESH,
        )

    def bit_of(bit):
        return lax.rem(lax.div(dpi, bit), 2)

    bufs, at = [], 0
    for c in chunks:
        n = 7 if c["tp"] else 5
        bufs.append(per[at : at + n])
        at += n

    class Chunk:
        def __init__(self, k):
            self.k, self.c = k, chunks[k]
            self.rows, self.order = self.c["rows"], self.c["order"]
            self.acc = bufs[k][0]
            self.halves = bufs[k][1:4]
            if self.c["tp"]:
                self.mid, self.fin, self.got_x = bufs[k][4:7]
            else:
                self.fin = bufs[k][4]
            self.stages = []
            if self.c["tp"]:
                self.stages.append(("C", 0, None))
            size, seq, far = self.rows, [], self.c["tp"]
            for name in self.order:
                if name == "X":
                    far = False
                    self.stages.append(("X", size, list(seq)))
                else:
                    self.stages.append(("R", name, (list(seq), size, far)))
                    size //= 2
                    seq.append((name, size))
            for name in bits[3:]:
                self.stages.append(("B", name, (list(seq), size)))
            if self.c.get("pre"):
                self.stages.pop(1)
            while seq:
                name, half = seq[-1]
                self.stages.append(("G", name, (list(seq), half)))
                seq.pop()

        def off(self, seq):
            total = 0
            for name, half in seq:
                total = total + bit_of(name) * half
            return total

        def copies(self, s):
            kind, name, info = self.stages[s]
            ss, rs = send_sems.at[self.k], recv_sems.at[self.k]
            if kind == "C":
                lo = self.c["part"] * self.rows
                blk = [self.c_src.at[p, pl.ds(lo, self.rows)] for p in range(2)]
                return [
                    pltpu.make_async_copy(blk[0], self.acc, local_sems.at[self.k, 0]),
                    pltpu.make_async_copy(blk[1], self.mid, local_sems.at[self.k, 1]),
                ]
            if kind == "X":
                off = self.off(info)
                return [
                    remote(
                        rows_at(self.mid, off, name), rows_at(self.got_x, off, name),
                        ss.at[2], rs.at[2], "tp", 2,
                    )
                ]
            if kind == "R":
                seq, size, far = info
                half = size // 2
                off = self.off(seq) + (1 - bit_of(name)) * half
                slot = self.slot(s)
                out = [
                    remote(
                        rows_at(self.acc, off, half), self.halves[slot].at[0, pl.ds(0, half)],
                        ss.at[3 + s], rs.at[3 + s], "dp", name,
                    )
                ]
                if far:
                    out.append(
                        remote(
                            rows_at(self.mid, off, half),
                            self.halves[slot].at[1, pl.ds(0, half)],
                            ss.at[2 + 14], rs.at[2 + 14], "dp", name,
                        )
                    )
                return out
            if kind == "B":
                seq, size = info
                off = self.off(seq)
                slot = 2
                return [
                    remote(
                        rows_at(self.acc, off, size),
                        self.halves[slot].at[2 + bits.index(name) - 3, pl.ds(0, size)],
                        ss.at[3 + s], rs.at[3 + s], "dp", name,
                    )
                ]
            seq, half = info
            off = self.off(seq)
            here = rows_at(self.fin, off, half)
            return [remote(here, here, ss.at[3 + s], rs.at[3 + s], "dp", name)]

        def slot(self, s):
            return sum(1 for t in self.stages[:s] if t[0] == "R")

        def start(self, s):
            for cp in self.copies(s):
                cp.start()

        def finish(self, s):
            kind, name, info = self.stages[s]
            for cp in self.copies(s):
                cp.wait()
            if kind == "X":
                off = self.off(info)
                add_rows(self.acc, self.got_x, None, off, off, name)
            if kind == "R":
                seq, size, far = info
                half = size // 2
                off = self.off(seq) + bit_of(name) * half
                got = self.halves[self.slot(s)]
                add_rows(self.acc, got, 0, off, 0, half)
                if far:
                    add_rows(self.mid, got, 1, off, 0, half)
            if kind == "B":
                seq, size = info
                add_rows(self.acc, self.halves[2], bits.index(name) - 1, self.off(seq), 0, size)

        def event(self, s):
            if s > 0:
                self.finish(s - 1)
            if s < len(self.stages):
                if self.stages[s][0] == "G" and self.stages[s - 1][0] != "G":
                    seq, size = self.stages[s][2]
                    here = pl.ds(pl.multiple_of(self.off(seq), 16), size)
                    self.fin[here] = self.acc[here]
                self.start(s)
            else:
                self.out_copy().start()
                if self.c.get("head"):
                    head_start(self)

        def out_copy(self):
            return pltpu.make_async_copy(
                self.fin, outs[self.c["out"][0]].at[pl.ds(self.c["out"][1], self.rows)],
                local_sems.at[self.k, 2],
            )

        @property
        def n(self):
            return len(self.stages)

    head_nh, hr = [c["head"] for c in chunks if c.get("head")][0]
    head_chunk = []

    def head_remote(ch, p):
        mine = ch.fin.at[pl.ds(head_nh, hr)]
        return remote(mine, hg.at[p - 1], hg_send.at[p - 1], hg_recv.at[p - 1], "tp", p)

    def head_local(ch):
        mine = ch.fin.at[pl.ds(head_nh, hr)]
        return pltpu.make_async_copy(mine, rows_at(head_ref, tpi * hr, hr), local_sems.at[0, 3])

    def head_start(ch):
        head_chunk.append(ch)
        for p in range(1, tp_size):
            head_remote(ch, p).start()
        head_local(ch).start()

    work, at = [], 0
    for k, c in enumerate(chunks):
        ch = Chunk(k)
        if c["tp"]:
            if c["part"] == 0:
                at += 1
            ch.c_src = srcs[at - 1]
        work.append(ch)
    done = [0] * len(work)

    def go(k, upto=None):
        if done[k] <= work[k].n:
            work[k].event(done[k])
            done[k] += 1

    def turn(ks):
        for k in ks:
            go(k)

    ladder = [("tp", 1), ("tp", 2)] + [("dp", b) for b in bits]

    def small_copy(s):
        return remote(
            small_in, small_got.at[s], vec_send.at[0, s], vec_recv.at[0, s], *ladder[s]
        )

    def small_event(s):
        if s > 0:
            small_copy(s - 1).wait()
            got = small_got[s - 1]
            small_in[0:8] += got[0:8]
            if s == 1:
                small_in[8:9] += got[9:10]
                small_in[10:11] += got[11:12]
            elif s == 2:
                small_in[8:9] += got[10:11]
            else:
                small_in[8:9] += got[8:9]
        if s < len(ladder):
            small_copy(s).start()

    def do_copy(p):
        if p == 0:
            return pltpu.make_async_copy(do_ref.at[0], dos.at[0], do_local)
        return remote(do_ref.at[p], dos.at[p], do_send.at[p], do_recv.at[p], "tp", p)

    @pl.when(step == 0)
    def _():
        barrier = pltpu.get_barrier_semaphore()
        others = [("tp", m) for m in range(1, tp_size)] + [("dp", m) for m in range(1, dp_size)]
        for axis, bit in others:
            dev = (partner_any(dpi, bit), tpi) if axis == "dp" else (dpi, partner_any(tpi, bit))
            pl.semaphore_signal(
                barrier, inc=1, device_id=dev, device_id_type=pl.DeviceIdType.MESH
            )
        pl.semaphore_wait(barrier, len(others))
        for p in (2, 3, 1, 0):
            do_copy(p).start()
        turn(PLAN_FIRST)
        small_in[...] = small_ref[...]
        small_event(0)

    for p in range(tp_size):

        @pl.when(step == p)
        def _():
            do_copy(p).wait()

    @pl.when(i == 0)
    def _():
        ks[...] = qkv_ref[1, h].T
        vs[...] = qkv_ref[2, h].T
        dks[...] = jnp.zeros_like(dks)
        dvs[...] = jnp.zeros_like(dvs)

    lanes = pl.ds(pl.multiple_of(i * rows_dev, rows_dev), rows_dev)
    qt = qkv_ref[0, h, :, lanes] * jnp.bfloat16(scale)
    dot_t = dos[i, h]
    dsum = jnp.sum(
        dot_t.astype(F32) * o_ref[i, h].astype(F32), axis=0, keepdims=True
    )
    s = dot(ks[...], qt)
    p = jnp.exp(s - lse_ref[i, h])
    dp = dot(vs[...], dot_t)
    ds = (p * (dp - dsum)).astype(BF16)
    dqkv[0, h, :, lanes] = (dot(qkv_ref[1, h], ds) * scale).astype(BF16)
    dvs[...] += dot(p.astype(BF16), dot_t.T)
    dks[...] += dot(ds, qt.T)

    @pl.when(i == tp_size - 1)
    def _():
        dqkv[1, h] = dks[...].astype(BF16).T
        dqkv[2, h] = dvs[...].astype(BF16).T

    qk = 3 * HD
    due = {}
    spot = 0
    for k in range(len(work)):
        if not chunks[k]["tp"]:
            n = min(chunks[k]["rows"] // qk, heads - spot)
            due[k] = (spot, n)
            spot += n

    def weight_grad(k):
        first, n = due[k]
        for sec in range(3):
            lhs = dqkv[sec, first : first + n].reshape(n * HD, tp_size * rows_dev)
            work[k].acc[sec * n * HD : (sec + 1) * n * HD] = dot(lhs, rows_ref[...]).astype(BF16)
        spare = chunks[k]["rows"] - n * qk
        if spare:
            work[k].acc[n * qk :] = jnp.zeros((spare, width), BF16)
        go(k)

    early = [k for k in due if sum(due[k]) < heads]
    small_done = [1]
    for st in range(steps):

        @pl.when(step == st)
        def _():
            for k in early:
                if st == sum(due[k]) * tp_size - 1:
                    weight_grad(k)
            if st < len(PLAN_STEPS):
                turn(PLAN_STEPS[st])
            if small_done[0] <= len(ladder):
                small_event(small_done[0])
                small_done[0] += 1

    @pl.when(step == steps - 1)
    def _():
        blk = 128

        def da_rows(p, store):
            def one(r, carry):
                lane = pl.ds(pl.multiple_of(p * rows_dev + r * blk, blk), blk)
                lhs = dqkv[:, :, :, lane].reshape(3 * heads * HD, blk)
                here = pl.ds(pl.multiple_of(r * blk, blk), blk)
                store(here, dot(lhs, wt_ref[...], ((0,), (0,))))
                return carry

            lax.fori_loop(0, rows_dev // blk, one, 0)

        def keep(slot):
            def store(here, val):
                da_far[slot, here] = val.astype(BF16)

            return store

        core3 = remote(da_far.at[0], da_core.at[0], da_send.at[0], da_recv.at[0], "tp", 1)
        core1 = remote(da_far.at[1], da_core.at[1], da_send.at[1], da_recv.at[1], "tp", 1)
        far = remote(da_far.at[2], da_across, da_send.at[2], da_recv.at[2], "tp", 2)
        da_rows(3, keep(0))
        core3.start()
        turn(PLAN_TAIL[0])
        da_rows(1, keep(1))
        core1.start()
        turn(PLAN_TAIL[1])
        core3.wait()

        def store2(here, val):
            da_far[2, here] = (val + da_core[0, here].astype(F32)).astype(BF16)

        da_rows(2, store2)
        far.start()
        turn(PLAN_TAIL[2])
        for k in due:
            if k not in early:
                weight_grad(k)
        turn(PLAN_TAIL[3])
        core1.wait()

        def store0(here, val):
            tok_ref[here] = val + da_core[1, here].astype(F32)

        da_rows(0, store0)
        turn(PLAN_TAIL[4])
        turn(PLAN_WAIT)
        far.wait()
        last_tp[tpi] = jnp.zeros((8, width), F32)

        def norm_rows(r, carry):
            here = pl.ds(pl.multiple_of(r * blk, blk), blk)
            da = tok_ref[here] + da_across[here].astype(F32)
            hat, rstd = norm_parts(tiles_ref[here].astype(F32))
            tok_ref[here] = norm_back(hat, rstd, row_of(gain_ref), da)
            last_tp[tpi, 0:1] += jnp.sum(da * hat, axis=0, keepdims=True)
            last_tp[tpi, 1:2] += jnp.sum(da, axis=0, keepdims=True)
            return carry

        lax.fori_loop(0, rows_dev // blk, norm_rows, 0)

        def last_copy(axis, m):
            buf, me = (last_tp, tpi) if axis == "tp" else (last_dp, dpi)
            at = 0 if axis == "tp" else tp_size
            return remote(
                buf.at[me], buf.at[me], vec_send.at[1, at + m], vec_recv.at[1, at + m], axis, m
            )

        for m in range(1, tp_size):
            last_copy("tp", m).start()
        turn(PLAN_LAST[0])
        for m in range(1, tp_size):
            last_copy("tp", m).wait()
        total = last_tp[0]
        for k in range(1, tp_size):
            total = total + last_tp[k]
        last_dp[dpi] = total
        last_dp[dpi, 2:3] = onehot_ref[...]
        for m in range(1, dp_size):
            last_copy("dp", m).start()
        turn(PLAN_LAST[1])
        for m in range(1, dp_size):
            last_copy("dp", m).wait()

        last_ref[0:1] = jnp.sum(last_dp[:, 0, :], axis=0, keepdims=True)
        shares = last_dp[:, 1, :]
        last_ref[1:2] = jnp.sum(shares, axis=0, keepdims=True)
        leads = last_ref.shape[0] - 8
        hot = last_dp[:, 2, 0:128]
        for k in range(leads):
            last_ref[8 + k : 9 + k] = jnp.sum(hot[:, k : k + 1] * shares, axis=0, keepdims=True)
        turn(PLAN_LAST[2])
        while small_done[0] <= len(ladder):
            small_event(small_done[0])
            small_done[0] += 1
        turn(PLAN_END)
        while any(done[k] <= work[k].n for k in range(len(work))):
            turn(range(len(work)))
        sum_ref[...] = small_in[...]
        head_out = [head_local(head_chunk[0])]
        for p in range(1, tp_size):
            head_remote(head_chunk[0], p).wait()
            out = pltpu.make_async_copy(
                hg.at[p - 1], rows_at(head_ref, partner_any(tpi, p) * hr, hr),
                local_sems.at[p, 3],
            )
            out.start()
            head_out.append(out)
        for out in head_out:
            out.wait()
        for ch in work:
            ch.out_copy().wait()


def partner_any(index, mask):
    bit = 1
    while bit <= mask:
        if mask & bit:
            index = partner(index, bit)
        bit *= 2
    return index


PLAN_FIRST = (2, 0)
PLAN_STEPS = ((2, 0, 4, 1), (4, 1, 3), (3,), (0,), (2, 1), (0,), (1,), (0, 4, 1), (2,), (0, 3, 5, 4, 1), (2,), (),)
PLAN_TAIL = ((0,), (), (2,), (5,), (),)
PLAN_WAIT = (3, 4, 2, 6, 5, 0, 4, 1, 3)
PLAN_LAST = ((2,), (6, 5), (4, 3),)
PLAN_END = (2, 6, 4, 3, 5, 1, 6, 3, 6, 5, 4, 6, 3)

ORDERS = (
    ("X", 2, 1, 4),
    (2, "X", 1, 4),
    (1, "X", 2, 4),
    ("X", 2, 1, 4),
    (2, "X", 1, 4),
    (1, 2, 4),
    (1, 2, 4),
)


def attn_bwd(qkv, o, lse, do, rows, wt, tiles, gain, onehot, leads, small, parts, mesh, scale):
    _, heads, _, frame = qkv.shape
    rows_dev, width = tiles.shape
    tp_size, dp_size = mesh.shape["tp"], mesh.shape["dp"]
    nbits = dp_size.bit_length() - 1
    half = width // 2
    ph_rows = parts[2].shape[1]
    chunks = [
        dict(tp=True, rows=half, part=0, pre=True, order=ORDERS[0], out=(0, 0)),
        dict(tp=True, rows=half, part=1, pre=True, order=ORDERS[1], out=(0, half)),
        dict(tp=True, rows=half, part=0, order=ORDERS[2], out=(1, 0)),
        dict(tp=True, rows=half, part=1, order=ORDERS[3], out=(1, half)),
        dict(tp=True, rows=ph_rows, part=0, order=ORDERS[4], out=(2, 0), head=(heads * HD, HEAD_ROWS)),
        dict(tp=False, rows=half, order=ORDERS[5], out=(3, 0)),
        dict(tp=False, rows=256, order=ORDERS[6], out=(3, half)),
    ]
    n_k = len(chunks)
    scratch = [
        pltpu.VMEM((frame, HD), BF16),
        pltpu.VMEM((frame, HD), BF16),
        pltpu.VMEM((frame, HD), F32),
        pltpu.VMEM((frame, HD), F32),
        pltpu.VMEM((tp_size, heads, HD, rows_dev), BF16),
        pltpu.VMEM((3, heads, HD, frame), BF16),
        pltpu.VMEM((3, rows_dev, width), BF16),
        pltpu.VMEM((2, rows_dev, width), BF16),
        pltpu.VMEM((rows_dev, width), BF16),
        pltpu.VMEM((16, width), F32),
        pltpu.VMEM((2 + nbits, 16, width), F32),
        pltpu.VMEM((tp_size, 8, width), F32),
        pltpu.VMEM((dp_size, 8, width), F32),
        pltpu.VMEM((tp_size - 1, HEAD_ROWS, width), BF16),
    ]
    for c in chunks:
        r = c["rows"]
        scratch.append(pltpu.VMEM((r, width), BF16))
        scratch.append(pltpu.VMEM((2, r // 2, width), BF16))
        scratch.append(pltpu.VMEM((2, r // 4, width), BF16))
        scratch.append(pltpu.VMEM((2 + max(nbits - 3, 0), r // 8, width), BF16))
        if c["tp"]:
            scratch += [pltpu.VMEM((r, width), BF16)] * 3
        else:
            scratch.append(pltpu.VMEM((r, width), BF16))
    scratch += [
        pltpu.SemaphoreType.DMA((n_k, 17)),
        pltpu.SemaphoreType.DMA((n_k, 17)),
        pltpu.SemaphoreType.DMA((n_k, 4)),
        pltpu.SemaphoreType.DMA((tp_size,)),
        pltpu.SemaphoreType.DMA((tp_size,)),
        pltpu.SemaphoreType.DMA,
        pltpu.SemaphoreType.DMA((3,)),
        pltpu.SemaphoreType.DMA((3,)),
        pltpu.SemaphoreType.DMA((2, tp_size + dp_size)),
        pltpu.SemaphoreType.DMA((2, tp_size + dp_size)),
        pltpu.SemaphoreType.DMA((tp_size - 1,)),
        pltpu.SemaphoreType.DMA((tp_size - 1,)),
    ]
    any_spec = pl.BlockSpec(memory_space=pl.ANY)
    vmem = pl.BlockSpec(memory_space=pltpu.VMEM)
    return pl.pallas_call(
        functools.partial(
            bwd_kernel, scale=scale, chunks=chunks, dp_size=dp_size, heads=heads,
            tp_size=tp_size, width=width,
        ),
        grid=(heads, tp_size),
        in_specs=[vmem, vmem, vmem, any_spec] + [vmem] * 6 + [any_spec] * len(parts),
        out_specs=[vmem, vmem, vmem, any_spec] + [any_spec] * 4,
        out_shape=[
            jax.ShapeDtypeStruct((rows_dev, width), F32),
            jax.ShapeDtypeStruct((16, width), F32),
            jax.ShapeDtypeStruct((8 + leads, width), F32),
            jax.ShapeDtypeStruct((tp_size * HEAD_ROWS, width), BF16),
        ]
        + [
            jax.ShapeDtypeStruct((rows, width), BF16)
            for rows in (width, width, ph_rows, half + chunks[-1]["rows"])
        ],
        scratch_shapes=scratch,
        compiler_params=pltpu.CompilerParams(
            vmem_limit_bytes=60 << 20, collective_id=1, has_side_effects=True
        ),
        cost_estimate=pl.CostEstimate(
            flops=60_000_000_000, bytes_accessed=30 << 20, transcendentals=heads * frame * frame
        ),
        name="attn_bwd",
    )(qkv, o, lse, do, rows, wt, tiles, gain, onehot, small, *parts)


def mid_kernel(
    tiles_ref, o_ref, dots_ref, off_ref, pb_ref, g2_ref, s2_ref, nb_ref, hw_ref, hb_ref, scale_ref,
    pj_own, pj_far, wi_own, wi_far, na_own, na_far,
    dn_ref, dw_ref, ph_ref, do_ref, dx1_ref, small_ref, gates_ref, corr_ref,
    pj, wi, na, x1, hat, rstd, c_low, act, slope, h_low, hg, dx2, dz, du, dc, dy, hd, dn, dw, ph, dos,
    got_n, got_w, got_p, got_x, got_z, c_send, c_recv, x_send, x_recv, in_sem, out_sem, *, tp_size, heads
):
    dpi = lax.axis_index("dp")
    tpi = lax.axis_index("tp")
    rows_dev, width = tiles_ref.shape
    nh = heads * HD
    half = rows_dev // 2
    blocks = [pl.ds(r * half, half) for r in range(2)]

    def loads(k, own, far, dst):
        out = []
        for p in range(tp_size):
            src = own if p == 0 else far.at[p - 1]
            n = src.shape[0]
            to = dst.at[pl.ds(p * n, n)] if len(dst.shape) == 2 else dst.at[p]
            out.append(pltpu.make_async_copy(src, to, in_sem.at[k, p]))
        return out

    load_pj = loads(0, pj_own, pj_far, pj)
    load_wi = loads(1, wi_own, wi_far, wi)
    load_na = loads(2, na_own, na_far, na)
    for cp in load_pj + load_wi + load_na:
        cp.start()
    other = (dpi, partner(tpi, 1))
    side = (partner(dpi, PRE_BIT), tpi)
    far = (dpi, partner(tpi, 2))
    barrier = pltpu.get_barrier_semaphore()
    for dev in (other, side, far):
        pl.semaphore_signal(
            barrier, inc=1, device_id=dev, device_id_type=pl.DeviceIdType.MESH
        )
    mine = lax.rem(lax.div(dpi, PRE_BIT), 2)
    top_rows, quarter = width // 2, width // 4

    def far_copy():
        return pltpu.make_async_remote_copy(
            src_ref=dn.at[2, pl.ds(0, top_rows)], dst_ref=got_x,
            send_sem=x_send.at[0], recv_sem=x_recv.at[0],
            device_id=far, device_id_type=pl.DeviceIdType.MESH,
        )

    def side_copy(j):
        rows = pl.ds(pl.multiple_of(top_rows + (1 - mine) * quarter, 16), quarter)
        return pltpu.make_async_remote_copy(
            src_ref=dn.at[2 * j, rows], dst_ref=got_z.at[j],
            send_sem=x_send.at[1 + j], recv_sem=x_recv.at[1 + j],
            device_id=side, device_id_type=pl.DeviceIdType.MESH,
        )

    def core_copy(k, j, src, got):
        return pltpu.make_async_remote_copy(
            src_ref=src.at[2 * j + 1], dst_ref=got.at[j],
            send_sem=c_send.at[k, j], recv_sem=c_recv.at[k, j],
            device_id=other, device_id_type=pl.DeviceIdType.MESH,
        )

    small_ref[...] = jnp.zeros_like(small_ref)
    proj_bias, gain2, shift2, out_bias = (row_of(v) for v in (pb_ref, g2_ref, s2_ref, nb_ref))
    for cp in load_pj:
        cp.wait()
    for r in blocks:
        v = tiles_ref[r].astype(F32) + dot(o_ref[:, r], pj[...], ((0,), (0,))) + proj_bias
        x1[r] = v
        hv, rs = norm_parts(v)
        hat[r] = hv
        rstd[r] = rs
        c_low[r] = (hv * gain2 + shift2).astype(BF16)
    for p in range(tp_size):
        load_wi[p].wait()
        cols = pl.ds(p * width, width)
        for r in blocks:
            m, d = gelu_parts(dot(c_low[r], wi[p]) + off_ref[p, 0:1])
            act[r, cols] = m.astype(BF16)
            slope[r, cols] = d.astype(BF16)
    for cp in load_na:
        cp.wait()
    for r in blocks:
        h_low[r] = (x1[r] + dot(act[r], na[...]) + out_bias).astype(BF16)

    logits = dot(hw_ref[...], h_low[...], ((1,), (1,))) + hb_ref[...]
    row_scale = scale_ref[0:1, 0:1]
    lg = [logits[e * HEAD_ROWS : (e + 1) * HEAD_ROWS] for e in range(EXPERTS)]
    top = jnp.maximum(jnp.maximum(lg[0], lg[1]), lg[2])
    ex = [jnp.exp(v - top) for v in lg]
    inv = 1.0 / (ex[0] + ex[1] + ex[2])
    gt = [v * inv for v in ex]
    mixed = gt[0] * dots_ref[0] + gt[1] * dots_ref[1] + gt[2] * dots_ref[2]
    for e in range(EXPERTS):
        gates_ref[e] = gt[e]
        hg[e * HEAD_ROWS : (e + 1) * HEAD_ROWS] = (gt[e] * (dots_ref[e] - mixed)).astype(BF16)
    hg[EXPERTS * HEAD_ROWS :] = (dots_ref[EXPERTS] * row_scale).astype(BF16)
    corr_ref[...] = logits[EXPERTS * HEAD_ROWS :] * row_scale
    d2 = dot(hg[...], hw_ref[...], ((0,), (0,)))
    dx2[...] = d2
    dz[...] = d2.astype(BF16)
    small_ref[0:1] = jnp.sum(d2, axis=0, keepdims=True)
    ones = jnp.ones((8, rows_dev), BF16)
    small_ref[4:5, : tp_size * HEAD_ROWS] = dot(ones, hg[...], ((1,), (1,)))[0:1]

    def send_out(k, p, src, dst):
        cp = pltpu.make_async_copy(src, dst, out_sem.at[k, p])
        cp.start()
        return cp

    outs = []
    pairs = range(tp_size // 2)

    def narrow_dot(p):
        return dot(act[:, p * width : (p + 1) * width], dz[...], ((0,), (0,)))

    def wide_dot(p):
        return dot(c_low[...], du[p], ((0,), (0,)))

    pl.semaphore_wait(barrier, 3)
    for j in (1, 0):
        dn[2 * j + 1] = narrow_dot(2 * j + 1).astype(BF16)
        core_copy(0, j, dn, got_n).start()
    def hidden_grad(p):
        cols = pl.ds(p * width, width)
        for r in blocks:
            v = dot(dz[r], na[cols], ((1,), (1,))) * slope[r, cols].astype(F32)
            low = v.astype(BF16)
            du[p, r] = low
            small_ref[8 + p : 9 + p] += jnp.sum(low.astype(F32), axis=0, keepdims=True)
    hidden_grad(1)
    hidden_grad(3)
    for j in (1, 0):
        core_copy(0, j, dn, got_n).wait()
        dn[2 * j] = (narrow_dot(2 * j) + got_n[j].astype(F32)).astype(BF16)
        if j == 1:
            far_copy().start()
        side_copy(j).start()
    hidden_grad(0)
    hidden_grad(2)
    for j in pairs:
        dw[2 * j + 1] = wide_dot(2 * j + 1).astype(BF16)
        core_copy(1, j, dw, got_w).start()
    for r in blocks:
        g = dot(du[0, r], wi[0], ((1,), (1,)))
        for p in range(1, tp_size):
            g = g + dot(du[p, r], wi[p], ((1,), (1,)))
        hv = hat[r]
        d1 = dx2[r] + norm_back(hv, rstd[r], gain2, g)
        dx1_ref[r] = d1
        dy[r] = d1.astype(BF16)
        small_ref[1:2] += jnp.sum(g * hv, axis=0, keepdims=True)
        small_ref[2:3] += jnp.sum(g, axis=0, keepdims=True)
        small_ref[3:4] += jnp.sum(d1, axis=0, keepdims=True)
    dos[...] = dot(pj[...], dy[...], ((1,), (1,))).astype(BF16).reshape(dos.shape)
    outs.append(send_out(2, 0, dos, do_ref))
    dp = dot(o_ref[...], dy[...]).astype(BF16)
    hd[...] = dot(hg[...], h_low[...]).astype(BF16)
    for p in range(tp_size):
        ph[p, 0:nh] = dp[p * nh : (p + 1) * nh]
        at = pl.ds(pl.multiple_of(partner_any(tpi, p) * HEAD_ROWS, 16), HEAD_ROWS)
        ph[p, nh : nh + HEAD_ROWS] = hd[at]
        ph[p, nh + HEAD_ROWS :] = jnp.zeros((ph.shape[1] - nh - HEAD_ROWS, width), BF16)
    for j in pairs:
        core_copy(2, j, ph, got_p).start()
    for j in pairs:
        core_copy(1, j, dw, got_w).wait()
        dw[2 * j] = (wide_dot(2 * j) + got_w[j].astype(F32)).astype(BF16)
        outs.append(send_out(1, j, dw.at[2 * j], dw_ref.at[j]))
    for j in pairs:
        core_copy(2, j, ph, got_p).wait()
        ph[2 * j] = (ph[2 * j].astype(F32) + got_p[j].astype(F32)).astype(BF16)
        outs.append(send_out(3, j, ph.at[2 * j], ph_ref.at[j]))
    far_copy().wait()
    add_rows(dn.at[0], got_x, None, 0, 0, top_rows)
    for j in (1, 0):
        side_copy(j).wait()
        add_rows(dn.at[2 * j], got_z, j, top_rows + mine * quarter, 0, quarter)
        outs.append(send_out(0, j, dn.at[2 * j], dn_ref.at[j]))
    for cp in outs:
        cp.wait()


def mid(tiles, o_own, dots, off, vecs, hw, hb, row_scale, weights, mesh, heads):
    rows_dev, width = tiles.shape
    tp_size = mesh.shape["tp"]
    nh = heads * HD
    ph_rows = -(-(nh + HEAD_ROWS) // 128) * 128
    n_head = hw.shape[0]
    any_spec = pl.BlockSpec(memory_space=pl.ANY)
    vmem = pl.BlockSpec(memory_space=pltpu.VMEM)
    big = (tp_size, width, width)
    pair = (tp_size // 2,)
    return pl.pallas_call(
        functools.partial(mid_kernel, tp_size=tp_size, heads=heads),
        in_specs=[vmem] * 11 + [any_spec] * 6,
        out_specs=[any_spec] * 4 + [vmem] * 4,
        out_shape=[
            jax.ShapeDtypeStruct(pair + (width, width), BF16),
            jax.ShapeDtypeStruct(pair + (width, width), BF16),
            jax.ShapeDtypeStruct(pair + (ph_rows, width), BF16),
            jax.ShapeDtypeStruct((tp_size, heads, HD, rows_dev), BF16),
            jax.ShapeDtypeStruct((rows_dev, width), F32),
            jax.ShapeDtypeStruct((16, width), F32),
            jax.ShapeDtypeStruct((EXPERTS, HEAD_ROWS, rows_dev), F32),
            jax.ShapeDtypeStruct((HEAD_ROWS, rows_dev), F32),
        ],
        scratch_shapes=[
            pltpu.VMEM((tp_size * nh, width), BF16),
            pltpu.VMEM(big, BF16),
            pltpu.VMEM((tp_size * width, width), BF16),
            pltpu.VMEM((rows_dev, width), F32),
            pltpu.VMEM((rows_dev, width), F32),
            pltpu.VMEM((rows_dev, 1), F32),
            pltpu.VMEM((rows_dev, width), BF16),
            pltpu.VMEM((rows_dev, tp_size * width), BF16),
            pltpu.VMEM((rows_dev, tp_size * width), BF16),
            pltpu.VMEM((rows_dev, width), BF16),
            pltpu.VMEM((n_head, rows_dev), BF16),
            pltpu.VMEM((rows_dev, width), F32),
            pltpu.VMEM((rows_dev, width), BF16),
            pltpu.VMEM((tp_size, rows_dev, width), BF16),
            pltpu.VMEM((8, width), F32),
            pltpu.VMEM((rows_dev, width), BF16),
            pltpu.VMEM((n_head, width), BF16),
            pltpu.VMEM(big, BF16),
            pltpu.VMEM(big, BF16),
            pltpu.VMEM((tp_size, ph_rows, width), BF16),
            pltpu.VMEM((tp_size, heads, HD, rows_dev), BF16),
            pltpu.VMEM(pair + (width, width), BF16),
            pltpu.VMEM(pair + (width, width), BF16),
            pltpu.VMEM(pair + (ph_rows, width), BF16),
            pltpu.VMEM((width // 2, width), BF16),
            pltpu.VMEM(pair + (width // 4, width), BF16),
            pltpu.SemaphoreType.DMA((3, tp_size // 2)),
            pltpu.SemaphoreType.DMA((3, tp_size // 2)),
            pltpu.SemaphoreType.DMA((3,)),
            pltpu.SemaphoreType.DMA((3,)),
            pltpu.SemaphoreType.DMA((3, tp_size)),
            pltpu.SemaphoreType.DMA((4, tp_size)),
        ],
        compiler_params=pltpu.CompilerParams(
            vmem_limit_bytes=MID_VMEM, collective_id=2, has_side_effects=True
        ),
        cost_estimate=pl.CostEstimate(
            flops=18_000_000_000, bytes_accessed=30 << 20, transcendentals=2_000_000
        ),
        name="mid",
    )(tiles, o_own, dots, off, *vecs, hw, hb, row_scale, *weights)


def finish_kernel(
    n_ref, i_ref, ph_ref, qa_ref, qb_ref, hd_ref, tok_ref, dx_ref, table_ref,
    no_ref, io_ref, po_ref, qo_ref, g_ref, c_ref, to_ref, lead_ref, *, fields
):
    no_ref[...] = n_ref[...].astype(F32)
    io_ref[...] = i_ref[...].astype(F32)
    po_ref[...] = ph_ref[...].astype(F32)
    na = qa_ref.shape[0]
    qo_ref[0, :na] = qa_ref[...].astype(F32)
    qo_ref[0, na:] = qb_ref[...].astype(F32)
    for e in range(EXPERTS):
        g_ref[e * fields : (e + 1) * fields] = hd_ref[pl.ds(e * HEAD_ROWS, HEAD_ROWS)].astype(F32)[
            :fields
        ]
    c_ref[...] = hd_ref[pl.ds(EXPERTS * HEAD_ROWS, HEAD_ROWS)].astype(F32)[:fields]
    to_ref[...] = tok_ref[...] + dx_ref[...]
    lead_ref[...] = table_ref[8:]


def finish(n, i, ph, q, hd, tok, dx1, table, heads, fields):
    width = n.shape[0]
    nh = heads * HD
    steps = 3
    rows = width // steps
    first = (width // 2) // (3 * HD) * HD
    second = nh - first
    base = 3 * first // second
    tok_rows = tok.shape[0] // 2
    leads = table.shape[0] - 8

    def by_row(r):
        return pl.BlockSpec((r, width), lambda g: (g, 0))

    token = pl.BlockSpec((tok_rows, width), lambda g: (jnp.minimum(g, 1), 0))
    return pl.pallas_call(
        functools.partial(finish_kernel, fields=fields),
        grid=(steps,),
        in_specs=[
            by_row(rows),
            by_row(rows),
            by_row(nh // steps),
            by_row(first),
            pl.BlockSpec((second, width), lambda g: (base + g, 0)),
            pl.BlockSpec((hd.shape[0], rows), lambda g: (0, g)),
            token,
            token,
            pl.BlockSpec(table.shape, lambda g: (0, 0)),
        ],
        out_specs=[
            by_row(rows),
            by_row(rows),
            by_row(nh // steps),
            pl.BlockSpec((1, nh, width), lambda g: (g, 0, 0)),
            pl.BlockSpec((EXPERTS * fields, rows), lambda g: (0, g)),
            pl.BlockSpec((fields, rows), lambda g: (0, g)),
            token,
            pl.BlockSpec((leads, width), lambda g: (0, 0)),
        ],
        out_shape=[
            jax.ShapeDtypeStruct((width, width), F32),
            jax.ShapeDtypeStruct((width, width), F32),
            jax.ShapeDtypeStruct((nh, width), F32),
            jax.ShapeDtypeStruct((3, nh, width), F32),
            jax.ShapeDtypeStruct((EXPERTS * fields, width), F32),
            jax.ShapeDtypeStruct((fields, width), F32),
            jax.ShapeDtypeStruct(tok.shape, F32),
            jax.ShapeDtypeStruct((leads, width), F32),
        ],
        name="finish",
    )(n, i, ph, q, q, hd, tok, dx1, table)


def norm_parts(values):
    center = values - jnp.mean(values, axis=-1, keepdims=True)
    rstd = lax.rsqrt(jnp.mean(center * center, axis=-1, keepdims=True) + EPSILON)
    return center * rstd, rstd


def norm_back(hat, rstd, gain, grad):
    g = grad * gain
    return rstd * (
        g
        - jnp.mean(g, axis=-1, keepdims=True)
        - hat * jnp.mean(g * hat, axis=-1, keepdims=True)
    )


def gelu_parts(u):
    half = jnp.exp(-0.5 * u * u)
    t = 1.0 / (1.0 + (0.3275911 * 0.7071067811865476) * jnp.abs(u))
    poly = t * (
        0.254829592
        + t * (-0.284496736 + t * (1.421413741 + t * (-1.453152027 + t * 1.061405429)))
    )
    tail = 0.5 * poly * half
    cdf = jnp.where(u >= 0, 1.0 - tail, tail)
    return u * cdf, cdf + u * half * 0.3989422804014327


def make_body(mesh):
    tp_size = mesh.shape["tp"]

    def body(
        tile_vectors,
        snapshot_horizon_slot,
        horizon_sample_tally,
        specialist_outlooks,
        early_layernorm_scale,
        early_layernorm_shift,
        horizon_vectors,
        triple_head_matrix,
        attending_matrix,
        attending_offset,
        later_layernorm_scale,
        later_layernorm_shift,
        widening_matrix,
        widening_offset,
        narrowing_matrix,
        narrowing_offset,
        router_matrix,
        router_offset,
        adjuster_matrix,
        adjuster_offset,
        combined_loss_slope,
    ):
        rows_dev, width = tile_vectors.shape
        heads = triple_head_matrix.shape[2] // HD
        rows_frame = rows_dev * tp_size
        fields = adjuster_matrix.shape[1]
        sites = combined_loss_slope.shape[1]
        scale_val = HD ** (-0.5)
        tp_index = lax.axis_index("tp")
        lead = snapshot_horizon_slot[0]
        row_scale = lax.rsqrt(
            lax.dynamic_slice_in_dim(horizon_sample_tally, lead, 1, 0).astype(F32)
        )[0]
        nh = heads * HD
        w_t = jnp.transpose(triple_head_matrix, (0, 2, 1))
        (attn_rows, qkv, o_heads, lse, o_own, dots, off_all, proj_all, wide_all, narrow_all) = attn_fwd(
            snapshot_horizon_slot,
            tile_vectors,
            early_layernorm_scale,
            early_layernorm_shift,
            horizon_vectors,
            widening_offset,
            w_t,
            attending_matrix,
            widening_matrix,
            narrowing_matrix,
            specialist_outlooks,
            combined_loss_slope,
            mesh,
            scale_val,
        )

        def head_pad(x):
            x = x.reshape((EXPERTS + 1, fields) + x.shape[1:])
            x = jnp.pad(x, ((0, 0), (0, HEAD_ROWS - fields)) + ((0, 0),) * (x.ndim - 2))
            return x.reshape((-1,) + x.shape[2:])

        hw = head_pad(jnp.concatenate([router_matrix, adjuster_matrix], axis=1).T)
        hb = head_pad(jnp.concatenate([router_offset, adjuster_offset])[:, None])
        vec = (attending_offset, later_layernorm_scale, later_layernorm_shift, narrowing_offset)
        (d_narrow, d_wide, d_ph, do_all, dx1, small, gates, corr) = mid(
            tile_vectors,
            o_own.reshape(tp_size * nh, rows_dev),
            dots,
            off_all,
            vec,
            hw,
            hb,
            row_scale[None, None],
            [
                attending_matrix, proj_all, widening_matrix, wide_all,
                narrowing_matrix, narrow_all,
            ],
            mesh,
            heads,
        )
        gates = gates[:, :fields]
        corr = corr[:fields]

        blended = (corr)[:, None, :]
        for e in range(EXPERTS):
            blended = blended + gates[e][:, None, :] * specialist_outlooks[e].astype(F32)

        leads = horizon_vectors.shape[0]
        onehot = (jnp.arange(width, dtype=jnp.int32) == lead).astype(F32)[None, :]
        (token_part, small, table, head_sum, n_low, i_low, ph, q_low) = attn_bwd(
            qkv, o_heads, lse, do_all, attn_rows.reshape(rows_frame, width), w_t.reshape(3 * nh, width), tile_vectors,
            early_layernorm_scale, onehot, leads, small,
            [d_narrow, d_wide, d_ph], mesh, scale_val,
        )
        (
            narrow_sum, wide_sum, proj_weight_grad, qkv_sum, gate_sum, correct_sum, tokens_grad,
            lead_sum,
        ) = finish(
            n_low, i_low, ph, q_low, head_sum, token_part, dx1, table, heads, fields
        )
        qkv_sum = jnp.transpose(qkv_sum, (0, 2, 1))
        gate_weight_grad = gate_sum.T
        correct_weight_grad = correct_sum.T
        head_bias = small[4, : (EXPERTS + 1) * HEAD_ROWS].reshape(EXPERTS + 1, HEAD_ROWS)
        head_bias = head_bias[:, :fields]
        in_bias_grad = small[8]

        return (
            blended,
            tokens_grad,
            table[0],
            table[1],
            lead_sum,
            qkv_sum,
            proj_weight_grad,
            small[3],
            small[1],
            small[2],
            wide_sum,
            in_bias_grad,
            narrow_sum,
            small[0],
            gate_weight_grad,
            head_bias[:EXPERTS].reshape(EXPERTS * fields),
            correct_weight_grad,
            head_bias[EXPERTS],
        )

    return body


def solution(mesh):
    return jax.shard_map(
        make_body(mesh),
        mesh=mesh,
        in_specs=(
            P(("dp", "tp"), None),
            P("dp"),
            P(),
            P(None, None, None, ("dp", "tp")),
            P(),
            P(),
            P(),
            P(None, None, "tp"),
            P("tp", None),
            P(),
            P(),
            P(),
            P(None, "tp"),
            P("tp"),
            P("tp", None),
            P(),
            P(),
            P(),
            P(),
            P(),
            P(None, None, ("dp", "tp")),
        ),
        out_specs=(
            P(None, None, ("dp", "tp")),
            P(("dp", "tp"), None),
            P(),
            P(),
            P(),
            P(None, None, "tp"),
            P("tp", None),
            P(),
            P(),
            P(),
            P(None, "tp"),
            P("tp"),
            P("tp", None),
            P(),
            P(),
            P(),
            P(),
            P(),
        ),
        check_vma=False,
    )
```

```python
import functools
import jax
import jax.numpy as jnp
from jax import lax
from jax.experimental import pallas as pl
from jax.experimental.pallas import tpu as pltpu
from jax.sharding import PartitionSpec as P

HD = 64
EXPERTS = 3
HEAD_ROWS = 80
MID_VMEM = 62 << 20
PRE_BIT = 2
EPSILON = 1e-05
F32 = jnp.float32
BF16 = jnp.bfloat16


def dot(a, b, dims=((1,), (0,))):
    return lax.dot_general(a, b, (dims, ((), ())), preferred_element_type=F32)


def row_of(ref):
    return ref[...].reshape(1, ref.shape[0])


W_FLIGHT = 6
W_PLAN = (
    (0, (("far", 0),)),
    (1, (("far", 1),)),
    (3, (("far", 2), (0, 0))),
    (4, ((0, 1),)),
    (5, ((0, 2),)),
    (6, (("far", 3),)),
    (7, ((1, 1),)),
    (9, (("far", 4),)),
    (10, ((1, 2), (0, 3), ("far", 5))),
    (11, ((0, 4), (0, 5))),
)


def fwd_kernel(
    lead_ref, tiles_ref, gain_ref, shift_ref, table_ref, off_ref, wt_ref, proj_ref, wide_ref,
    narrow_ref, exp_ref, slope_ref,
    rows_out, qkv_ref, o_ref, lse_ref, own_out, dots_ref, off_out, proj_all, wide_all, narrow_all,
    offs, off_send, off_recv, rows_ref, own_ref, out_sem, ks, stream, stream_g, stream_sem, row_send, row_recv, o_send, o_recv, o_local,
    w_send, w_recv, *, scale, dp_size, tp_size, heads
):
    i, h = pl.program_id(0), pl.program_id(1)
    steps = tp_size * heads
    step = i * heads + h
    dpi, tpi = lax.axis_index("dp"), lax.axis_index("tp")
    rows_dev, width = tiles_ref.shape
    piece = rows_dev // 2

    def remote(src, dst, ssem, rsem, axis, bit):
        dev = (partner(dpi, bit), tpi) if axis == "dp" else (dpi, partner_any(tpi, bit))
        return pltpu.make_async_remote_copy(
            src_ref=src, dst_ref=dst, send_sem=ssem, recv_sem=rsem,
            device_id=dev, device_id_type=pl.DeviceIdType.MESH,
        )

    def row_copy(kind, c):
        a, b, bit = ((0, 1, 1), (0, 2, 2), (2, 3, 1))[kind]
        here = pl.ds(c * piece, piece)
        return remote(
            rows_ref.at[a, here], rows_ref.at[b, here],
            row_send.at[kind, c], row_recv.at[kind, c], "tp", bit,
        )

    def off_copy(m):
        return remote(offs.at[0], offs.at[m], off_send.at[m], off_recv.at[m], "tp", m)

    parts = []
    for src, dst, cuts, share in (
        (proj_ref, proj_all, (1,), (1,)),
        (narrow_ref, narrow_all, (2, 2), (1, 2)),
        (wide_ref, wide_all, (2, 3, 6), (1,)),
    ):
        lo = 0
        for cut in cuts:
            n = src.shape[0] // cut
            parts.append((src, dst, lo, n, share))
            lo += n

    def w_rows(n, stage, theirs=False):
        _, _, lo, size, share = parts[n]
        size = size // (1 << len(share))
        for bit in share[:stage]:
            size *= 2
        at = lo
        step = size
        for k, bit in enumerate(share[stage:]):
            mine = lax.rem(lax.div(dpi, bit), 2)
            if theirs and k == 0:
                mine = 1 - mine
            at = at + mine * step
            step *= 2
        return pl.ds(pl.multiple_of(at, 16), size)

    def w_far(n):
        src, dst = parts[n][:2]
        rows = w_rows(n, 0)
        return remote(
            src.at[rows], dst.at[1, rows], w_send.at[n, 0], w_recv.at[n, 0], "tp", 2
        )

    def w_side(n, k):
        rows = w_rows(n, k)
        here = parts[n][1].at[1, rows]
        return remote(
            here, here, w_send.at[n, 1 + k], w_recv.at[n, 1 + k], "dp", parts[n][4][k]
        )

    def w_fwd(n, k):
        dst = parts[n][1]
        rows = w_rows(n, 0) if k == 0 else w_rows(n, k - 1, True)
        return remote(
            dst.at[1, rows], dst.at[2, rows], w_send.at[n, 3 + k], w_recv.at[n, 3 + k], "tp", 1
        )

    def w_near(n):
        src, dst, lo, size, _ = parts[n]
        rows = pl.ds(lo, size)
        return remote(src.at[rows], dst.at[0, rows], w_send.at[n, 6], w_recv.at[n, 6], "tp", 1)

    def o_copy(p):
        if p == 0:
            return pltpu.make_async_copy(o_ref.at[0], own_ref.at[0], o_local)
        return remote(o_ref.at[p], own_ref.at[p], o_send.at[p], o_recv.at[p], "tp", p)

    fields, sites = slope_ref.shape[0], slope_ref.shape[1]
    per = stream.shape[2]
    groups = fields // per
    depth = stream.shape[0]

    def stream_copies(g):
        slot = lax.rem(g, depth)
        at = pl.ds(g * per, per)
        return (
            pltpu.make_async_copy(
                exp_ref.at[:, at], stream.at[slot], stream_sem.at[slot, 0]
            ),
            pltpu.make_async_copy(
                slope_ref.at[at], stream_g.at[slot], stream_sem.at[slot, 1]
            ),
        )

    @pl.when(step == 0)
    def _():
        barrier = pltpu.get_barrier_semaphore()
        others = [("tp", 1), ("tp", 2), ("tp", 3), ("dp", 1), ("dp", 2)]
        for axis, bit in others:
            dev = (partner(dpi, bit), tpi) if axis == "dp" else (dpi, partner_any(tpi, bit))
            pl.semaphore_signal(
                barrier, inc=1, device_id=dev, device_id_type=pl.DeviceIdType.MESH
            )
        for g in range(min(depth - 1, groups)):
            for cp in stream_copies(g):
                cp.start()
        blk = 64
        gain = row_of(gain_ref)
        shift = row_of(shift_ref) + table_ref[pl.ds(lead_ref[0], 1)]
        offs[0, 0:1] = row_of(off_ref)

        def norm_rows(r, carry):
            here = pl.ds(pl.multiple_of(r * blk, blk), blk)
            hat, _ = norm_parts(tiles_ref[here].astype(F32))
            rows_ref[0, here] = (hat * gain + shift).astype(BF16)
            return carry

        half = piece // blk
        lax.fori_loop(0, half, norm_rows, 0)
        pl.semaphore_wait(barrier, len(others))
        row_copy(1, 0).start()
        lax.fori_loop(half, 2 * half, norm_rows, 0)
        row_copy(1, 1).start()
        row_copy(0, 0).start()
        row_copy(0, 1).start()
        for m in range(1, tp_size):
            off_copy(m).start()
        for n in range(W_FLIGHT):
            w_far(n).start()

        def contract(g, carry):
            @pl.when(g + depth - 1 < groups)
            def _():
                for cp in stream_copies(g + depth - 1):
                    cp.start()

            for cp in stream_copies(g):
                cp.wait()
            slot = lax.rem(g, depth)
            for j in range(per):
                slope = stream_g[slot, j].astype(F32)
                for e in range(EXPERTS):
                    dots_ref[e, pl.ds(g * per + j, 1)] = jnp.sum(
                        stream[slot, e, j].astype(F32) * slope, axis=0, keepdims=True
                    )
                dots_ref[EXPERTS, pl.ds(g * per + j, 1)] = jnp.sum(slope, axis=0, keepdims=True)
            return carry

        dots_ref[...] = jnp.zeros_like(dots_ref)
        lax.fori_loop(0, groups, contract, 0)

        def project(p):
            lane = pl.ds(p * rows_dev, rows_dev)
            for s in range(3):
                part = dot(wt_ref[s], rows_ref[p], ((1,), (1,))).astype(BF16)
                qkv_ref[s, :, :, lane] = part.reshape(heads, HD, rows_dev)
            for hh in range(heads):
                ks[hh, lane] = qkv_ref[1, hh, :, lane].T

        project(0)
        for c in range(2):
            row_copy(0, c).wait()
        project(1)
        for c in range(2):
            row_copy(1, c).wait()
            row_copy(2, c).start()
        project(2)
        for c in range(2):
            row_copy(2, c).wait()
        for n in range(len(parts)):
            w_near(n).start()
        rows_copy = pltpu.make_async_copy(rows_ref, rows_out, out_sem.at[0])
        rows_copy.start()
        project(3)

    p = lax.rem(i + 2, tp_size)
    lanes = pl.ds(pl.multiple_of(p * rows_dev, rows_dev), rows_dev)
    q = qkv_ref[0, h, :, lanes] * jnp.bfloat16(scale)
    s = dot(ks[h], q)
    m = jnp.max(s, axis=0, keepdims=True)
    e = jnp.exp(s - m)
    l = jnp.sum(e, axis=0, keepdims=True)
    o_ref[p, h] = (dot(qkv_ref[2, h], e.astype(BF16)) / l).astype(BF16)
    lse_ref[p, h] = m + jnp.log(l)

    seq = {}

    def after(st, *what):
        seq.setdefault(min(st, steps - 1), []).extend(what)

    for st, what in W_PLAN:
        after(st, *what)
    for st, what in seq.items():

        @pl.when(step == st)
        def _():
            for kind, n in what:
                if kind == "far":
                    w_far(n).wait()
                    if n + W_FLIGHT < len(parts):
                        w_far(n + W_FLIGHT).start()
                    w_side(n, 0).start()
                    w_fwd(n, 0).start()
                else:
                    w_side(n, kind).wait()
                    if kind + 1 < len(parts[n][4]):
                        w_side(n, kind + 1).start()
                    w_fwd(n, kind + 1).start()

    for k in range(tp_size):

        @pl.when(step == k * heads + heads - 1)
        def _():
            o_copy((k + 2) % tp_size).start()

    @pl.when(step == steps - 1)
    def _():
        for k in range(tp_size):
            o_copy(k).wait()
        for m in range(1, tp_size):
            off_copy(m).wait()
        off_out[...] = offs[...]
        own_copy = pltpu.make_async_copy(own_ref, own_out, out_sem.at[1])
        own_copy.start()
        for n in range(len(parts)):
            w_near(n).wait()
            for k in range(1 + len(parts[n][4])):
                w_fwd(n, k).wait()
        own_copy.wait()
        pltpu.make_async_copy(rows_ref, rows_out, out_sem.at[0]).wait()


def attn_fwd(
    lead, tiles, gain, shift, table, off, wt, proj, wide, narrow, experts, slope, mesh, scale
):
    rows_dev, width = tiles.shape
    heads = proj.shape[0] // HD
    tp_size, dp_size = mesh.shape["tp"], mesh.shape["dp"]
    frame = tp_size * rows_dev
    fields, sites = slope.shape[0], slope.shape[1]
    per = 3 if fields % 3 == 0 else 1
    depth = 4
    any_spec = pl.BlockSpec(memory_space=pl.ANY)
    vmem = pl.BlockSpec(memory_space=pltpu.VMEM)
    return pl.pallas_call(
        functools.partial(
            fwd_kernel, scale=scale, dp_size=dp_size, tp_size=tp_size, heads=heads
        ),
        grid=(tp_size, heads),
        in_specs=[pl.BlockSpec(memory_space=pltpu.SMEM)] + [vmem] * 6 + [any_spec] * 5,
        out_specs=[any_spec] + [vmem] * 3 + [any_spec, vmem, vmem] + [any_spec] * 3,
        out_shape=[
            jax.ShapeDtypeStruct((tp_size, rows_dev, width), BF16),
            jax.ShapeDtypeStruct((3, heads, HD, frame), BF16),
            jax.ShapeDtypeStruct((tp_size, heads, HD, rows_dev), BF16),
            jax.ShapeDtypeStruct((tp_size, heads, 1, rows_dev), F32),
            jax.ShapeDtypeStruct((tp_size, heads, HD, rows_dev), BF16),
            jax.ShapeDtypeStruct((EXPERTS + 1, HEAD_ROWS, rows_dev), F32),
            jax.ShapeDtypeStruct((tp_size, 8, width), F32),
            jax.ShapeDtypeStruct((tp_size - 1,) + proj.shape, BF16),
            jax.ShapeDtypeStruct((tp_size - 1,) + wide.shape, BF16),
            jax.ShapeDtypeStruct((tp_size - 1,) + narrow.shape, BF16),
        ],
        scratch_shapes=[
            pltpu.VMEM((tp_size, 8, width), F32),
            pltpu.SemaphoreType.DMA((tp_size,)),
            pltpu.SemaphoreType.DMA((tp_size,)),
            pltpu.VMEM((tp_size, rows_dev, width), BF16),
            pltpu.VMEM((tp_size, heads, HD, rows_dev), BF16),
            pltpu.SemaphoreType.DMA((2,)),
            pltpu.VMEM((heads, frame, HD), BF16),
            pltpu.VMEM((depth, EXPERTS, per, sites, rows_dev), BF16),
            pltpu.VMEM((depth, per, sites, rows_dev), BF16),
            pltpu.SemaphoreType.DMA((depth, 2)),
            pltpu.SemaphoreType.DMA((3, 2)),
            pltpu.SemaphoreType.DMA((3, 2)),
            pltpu.SemaphoreType.DMA((tp_size,)),
            pltpu.SemaphoreType.DMA((tp_size,)),
            pltpu.SemaphoreType.DMA,
            pltpu.SemaphoreType.DMA((6, 7)),
            pltpu.SemaphoreType.DMA((6, 7)),
        ],
        compiler_params=pltpu.CompilerParams(
            vmem_limit_bytes=56 << 20, collective_id=0, has_side_effects=True
        ),
        cost_estimate=pl.CostEstimate(
            flops=30_000_000_000, bytes_accessed=40 << 20, transcendentals=heads * frame * frame
        ),
        name="attn_fwd",
    )(lead, tiles, gain, shift, table, off, wt, proj, wide, narrow, experts, slope)


def partner(index, bit):
    return index + bit - 2 * bit * lax.rem(lax.div(index, bit), 2)


def rows_at(ref, start, size):
    return ref.at[pl.ds(pl.multiple_of(start, 16), size)]


def add_rows(dst, src, lead, dst_off, src_off, size):
    step = 48 if size % 48 == 0 else 32

    def one(r, carry):
        here = pl.ds(pl.multiple_of(dst_off + r * step, 16), step)
        there = pl.ds(pl.multiple_of(src_off + r * step, 16), step)
        got = src[there] if lead is None else src[lead, there]
        dst[here] = (dst[here].astype(F32) + got.astype(F32)).astype(BF16)
        return carry

    lax.fori_loop(0, size // step, one, 0)


def bwd_kernel(
    qkv_ref, o_ref, lse_ref, do_ref, rows_ref, wt_ref, tiles_ref, gain_ref, onehot_ref, small_ref,
    *rest, scale, chunks, dp_size, heads, tp_size, width
):
    n_src = sum(1 for c in chunks if c["tp"] and c["part"] == 0)
    srcs = rest[:n_src]
    tok_ref, sum_ref, last_ref, head_ref = rest[n_src : n_src + 4]
    n_out = n_src + 4 + 4
    outs = rest[n_src + 4 : n_out]
    (
        ks, vs, dks, dvs, dos, dqkv, da_far, da_core, da_across,
        small_in, small_got, last_tp, last_dp, hg,
    ) = rest[n_out : n_out + 14]
    per = rest[n_out + 14 : -12]
    (
        send_sems, recv_sems, local_sems, do_send, do_recv, do_local, da_send, da_recv,
        vec_send, vec_recv, hg_send, hg_recv,
    ) = rest[-12:]
    h, i = pl.program_id(0), pl.program_id(1)
    steps = tp_size * heads
    step = h * tp_size + i
    dpi, tpi = lax.axis_index("dp"), lax.axis_index("tp")
    rows_dev = dos.shape[3]
    bits = [1 << b for b in range(dp_size.bit_length() - 1)]

    def remote(src, dst, ssem, rsem, axis, bit):
        dev = (partner_any(dpi, bit), tpi) if axis == "dp" else (dpi, partner_any(tpi, bit))
        return pltpu.make_async_remote_copy(
            src_ref=src, dst_ref=dst, send_sem=ssem, recv_sem=rsem,
            device_id=dev, device_id_type=pl.DeviceIdType.MESH,
        )

    def bit_of(bit):
        return lax.rem(lax.div(dpi, bit), 2)

    bufs, at = [], 0
    for c in chunks:
        n = 7 if c["tp"] else 5
        bufs.append(per[at : at + n])
        at += n

    class Chunk:
        def __init__(self, k):
            self.k, self.c = k, chunks[k]
            self.rows, self.order = self.c["rows"], self.c["order"]
            self.acc = bufs[k][0]
            self.halves = bufs[k][1:4]
            if self.c["tp"]:
                self.mid, self.fin, self.got_x = bufs[k][4:7]
            else:
                self.fin = bufs[k][4]
            self.stages = []
            if self.c["tp"]:
                self.stages.append(("C", 0, None))
            size, seq, far = self.rows, [], self.c["tp"]
            for name in self.order:
                if name == "X":
                    far = False
                    self.stages.append(("X", size, list(seq)))
                else:
                    self.stages.append(("R", name, (list(seq), size, far)))
                    size //= 2
                    seq.append((name, size))
            for name in bits[3:]:
                self.stages.append(("B", name, (list(seq), size)))
            if self.c.get("pre"):
                self.stages.pop(1)
            while seq:
                name, half = seq[-1]
                self.stages.append(("G", name, (list(seq), half)))
                seq.pop()

        def off(self, seq):
            total = 0
            for name, half in seq:
                total = total + bit_of(name) * half
            return total

        def copies(self, s):
            kind, name, info = self.stages[s]
            ss, rs = send_sems.at[self.k], recv_sems.at[self.k]
            if kind == "C":
                lo = self.c["part"] * self.rows
                blk = [self.c_src.at[p, pl.ds(lo, self.rows)] for p in range(2)]
                return [
                    pltpu.make_async_copy(blk[0], self.acc, local_sems.at[self.k, 0]),
                    pltpu.make_async_copy(blk[1], self.mid, local_sems.at[self.k, 1]),
                ]
            if kind == "X":
                off = self.off(info)
                return [
                    remote(
                        rows_at(self.mid, off, name), rows_at(self.got_x, off, name),
                        ss.at[2], rs.at[2], "tp", 2,
                    )
                ]
            if kind == "R":
                seq, size, far = info
                half = size // 2
                off = self.off(seq) + (1 - bit_of(name)) * half
                slot = self.slot(s)
                out = [
                    remote(
                        rows_at(self.acc, off, half), self.halves[slot].at[0, pl.ds(0, half)],
                        ss.at[3 + s], rs.at[3 + s], "dp", name,
                    )
                ]
                if far:
                    out.append(
                        remote(
                            rows_at(self.mid, off, half),
                            self.halves[slot].at[1, pl.ds(0, half)],
                            ss.at[2 + 14], rs.at[2 + 14], "dp", name,
                        )
                    )
                return out
            if kind == "B":
                seq, size = info
                off = self.off(seq)
                slot = 2
                return [
                    remote(
                        rows_at(self.acc, off, size),
                        self.halves[slot].at[2 + bits.index(name) - 3, pl.ds(0, size)],
                        ss.at[3 + s], rs.at[3 + s], "dp", name,
                    )
                ]
            seq, half = info
            off = self.off(seq)
            here = rows_at(self.fin, off, half)
            return [remote(here, here, ss.at[3 + s], rs.at[3 + s], "dp", name)]

        def slot(self, s):
            return sum(1 for t in self.stages[:s] if t[0] == "R")

        def start(self, s):
            for cp in self.copies(s):
                cp.start()

        def finish(self, s):
            kind, name, info = self.stages[s]
            for cp in self.copies(s):
                cp.wait()
            if kind == "X":
                off = self.off(info)
                add_rows(self.acc, self.got_x, None, off, off, name)
            if kind == "R":
                seq, size, far = info
                half = size // 2
                off = self.off(seq) + bit_of(name) * half
                got = self.halves[self.slot(s)]
                add_rows(self.acc, got, 0, off, 0, half)
                if far:
                    add_rows(self.mid, got, 1, off, 0, half)
            if kind == "B":
                seq, size = info
                add_rows(self.acc, self.halves[2], bits.index(name) - 1, self.off(seq), 0, size)

        def event(self, s):
            if s > 0:
                self.finish(s - 1)
            if s < len(self.stages):
                if self.stages[s][0] == "G" and self.stages[s - 1][0] != "G":
                    seq, size = self.stages[s][2]
                    here = pl.ds(pl.multiple_of(self.off(seq), 16), size)
                    self.fin[here] = self.acc[here]
                self.start(s)
            else:
                self.out_copy().start()
                if self.c.get("head"):
                    head_start(self)

        def out_copy(self):
            return pltpu.make_async_copy(
                self.fin, outs[self.c["out"][0]].at[pl.ds(self.c["out"][1], self.rows)],
                local_sems.at[self.k, 2],
            )

        @property
        def n(self):
            return len(self.stages)

    head_nh, hr = [c["head"] for c in chunks if c.get("head")][0]
    head_chunk = []

    def head_remote(ch, p):
        mine = ch.fin.at[pl.ds(head_nh, hr)]
        return remote(mine, hg.at[p - 1], hg_send.at[p - 1], hg_recv.at[p - 1], "tp", p)

    def head_local(ch):
        mine = ch.fin.at[pl.ds(head_nh, hr)]
        return pltpu.make_async_copy(mine, rows_at(head_ref, tpi * hr, hr), local_sems.at[0, 3])

    def head_start(ch):
        head_chunk.append(ch)
        for p in range(1, tp_size):
            head_remote(ch, p).start()
        head_local(ch).start()

    work, at = [], 0
    for k, c in enumerate(chunks):
        ch = Chunk(k)
        if c["tp"]:
            if c["part"] == 0:
                at += 1
            ch.c_src = srcs[at - 1]
        work.append(ch)
    done = [0] * len(work)

    def go(k, upto=None):
        if done[k] <= work[k].n:
            work[k].event(done[k])
            done[k] += 1

    def turn(ks):
        for k in ks:
            go(k)

    ladder = [("tp", 1), ("tp", 2)] + [("dp", b) for b in bits]

    def small_copy(s):
        return remote(
            small_in, small_got.at[s], vec_send.at[0, s], vec_recv.at[0, s], *ladder[s]
        )

    def small_event(s):
        if s > 0:
            small_copy(s - 1).wait()
            got = small_got[s - 1]
            small_in[0:8] += got[0:8]
            if s == 1:
                small_in[8:9] += got[9:10]
                small_in[10:11] += got[11:12]
            elif s == 2:
                small_in[8:9] += got[10:11]
            else:
                small_in[8:9] += got[8:9]
        if s < len(ladder):
            small_copy(s).start()

    def do_copy(p):
        if p == 0:
            return pltpu.make_async_copy(do_ref.at[0], dos.at[0], do_local)
        return remote(do_ref.at[p], dos.at[p], do_send.at[p], do_recv.at[p], "tp", p)

    @pl.when(step == 0)
    def _():
        barrier = pltpu.get_barrier_semaphore()
        others = [("tp", m) for m in range(1, tp_size)] + [("dp", m) for m in range(1, dp_size)]
        for axis, bit in others:
            dev = (partner_any(dpi, bit), tpi) if axis == "dp" else (dpi, partner_any(tpi, bit))
            pl.semaphore_signal(
                barrier, inc=1, device_id=dev, device_id_type=pl.DeviceIdType.MESH
            )
        pl.semaphore_wait(barrier, len(others))
        for p in (2, 3, 1, 0):
            do_copy(p).start()
        turn(PLAN_FIRST)
        small_in[...] = small_ref[...]
        small_event(0)

    for p in range(tp_size):

        @pl.when(step == p)
        def _():
            do_copy(p).wait()

    @pl.when(i == 0)
    def _():
        ks[...] = qkv_ref[1, h].T
        vs[...] = qkv_ref[2, h].T
        dks[...] = jnp.zeros_like(dks)
        dvs[...] = jnp.zeros_like(dvs)

    lanes = pl.ds(pl.multiple_of(i * rows_dev, rows_dev), rows_dev)
    qt = qkv_ref[0, h, :, lanes] * jnp.bfloat16(scale)
    dot_t = dos[i, h]
    dsum = jnp.sum(
        dot_t.astype(F32) * o_ref[i, h].astype(F32), axis=0, keepdims=True
    )
    s = dot(ks[...], qt)
    p = jnp.exp(s - lse_ref[i, h])
    dp = dot(vs[...], dot_t)
    ds = (p * (dp - dsum)).astype(BF16)
    dqkv[0, h, :, lanes] = (dot(qkv_ref[1, h], ds) * scale).astype(BF16)
    dvs[...] += dot(p.astype(BF16), dot_t.T)
    dks[...] += dot(ds, qt.T)

    @pl.when(i == tp_size - 1)
    def _():
        dqkv[1, h] = dks[...].astype(BF16).T
        dqkv[2, h] = dvs[...].astype(BF16).T

    qk = 3 * HD
    due = {}
    spot = 0
    for k in range(len(work)):
        if not chunks[k]["tp"]:
            n = min(chunks[k]["rows"] // qk, heads - spot)
            due[k] = (spot, n)
            spot += n

    def weight_grad(k):
        first, n = due[k]
        for sec in range(3):
            lhs = dqkv[sec, first : first + n].reshape(n * HD, tp_size * rows_dev)
            work[k].acc[sec * n * HD : (sec + 1) * n * HD] = dot(lhs, rows_ref[...]).astype(BF16)
        spare = chunks[k]["rows"] - n * qk
        if spare:
            work[k].acc[n * qk :] = jnp.zeros((spare, width), BF16)
        go(k)

    early = [k for k in due if sum(due[k]) < heads]
    small_done = [1]
    for st in range(steps):

        @pl.when(step == st)
        def _():
            for k in early:
                if st == sum(due[k]) * tp_size - 1:
                    weight_grad(k)
            if st < len(PLAN_STEPS):
                turn(PLAN_STEPS[st])
            if small_done[0] <= len(ladder):
                small_event(small_done[0])
                small_done[0] += 1

    @pl.when(step == steps - 1)
    def _():
        blk = 128

        def da_rows(p, store):
            def one(r, carry):
                lane = pl.ds(pl.multiple_of(p * rows_dev + r * blk, blk), blk)
                lhs = dqkv[:, :, :, lane].reshape(3 * heads * HD, blk)
                here = pl.ds(pl.multiple_of(r * blk, blk), blk)
                store(here, dot(lhs, wt_ref[...], ((0,), (0,))))
                return carry

            lax.fori_loop(0, rows_dev // blk, one, 0)

        def keep(slot):
            def store(here, val):
                da_far[slot, here] = val.astype(BF16)

            return store

        core3 = remote(da_far.at[0], da_core.at[0], da_send.at[0], da_recv.at[0], "tp", 1)
        core1 = remote(da_far.at[1], da_core.at[1], da_send.at[1], da_recv.at[1], "tp", 1)
        far = remote(da_far.at[2], da_across, da_send.at[2], da_recv.at[2], "tp", 2)
        da_rows(3, keep(0))
        core3.start()
        turn(PLAN_TAIL[0])
        da_rows(1, keep(1))
        core1.start()
        turn(PLAN_TAIL[1])
        core3.wait()

        def store2(here, val):
            da_far[2, here] = (val + da_core[0, here].astype(F32)).astype(BF16)

        da_rows(2, store2)
        far.start()
        turn(PLAN_TAIL[2])
        for k in due:
            if k not in early:
                weight_grad(k)
        turn(PLAN_TAIL[3])
        core1.wait()

        def store0(here, val):
            tok_ref[here] = val + da_core[1, here].astype(F32)

        da_rows(0, store0)
        turn(PLAN_TAIL[4])
        turn(PLAN_WAIT)
        far.wait()
        last_tp[tpi] = jnp.zeros((8, width), F32)

        def norm_rows(r, carry):
            here = pl.ds(pl.multiple_of(r * blk, blk), blk)
            da = tok_ref[here] + da_across[here].astype(F32)
            hat, rstd = norm_parts(tiles_ref[here].astype(F32))
            tok_ref[here] = norm_back(hat, rstd, row_of(gain_ref), da)
            last_tp[tpi, 0:1] += jnp.sum(da * hat, axis=0, keepdims=True)
            last_tp[tpi, 1:2] += jnp.sum(da, axis=0, keepdims=True)
            return carry

        lax.fori_loop(0, rows_dev // blk, norm_rows, 0)

        def last_copy(axis, m):
            buf, me = (last_tp, tpi) if axis == "tp" else (last_dp, dpi)
            at = 0 if axis == "tp" else tp_size
            return remote(
                buf.at[me], buf.at[me], vec_send.at[1, at + m], vec_recv.at[1, at + m], axis, m
            )

        for m in range(1, tp_size):
            last_copy("tp", m).start()
        turn(PLAN_LAST[0])
        for m in range(1, tp_size):
            last_copy("tp", m).wait()
        total = last_tp[0]
        for k in range(1, tp_size):
            total = total + last_tp[k]
        last_dp[dpi] = total
        last_dp[dpi, 2:3] = onehot_ref[...]
        for m in range(1, dp_size):
            last_copy("dp", m).start()
        turn(PLAN_LAST[1])
        for m in range(1, dp_size):
            last_copy("dp", m).wait()

        last_ref[0:1] = jnp.sum(last_dp[:, 0, :], axis=0, keepdims=True)
        shares = last_dp[:, 1, :]
        last_ref[1:2] = jnp.sum(shares, axis=0, keepdims=True)
        leads = last_ref.shape[0] - 8
        hot = last_dp[:, 2, 0:128]
        for k in range(leads):
            last_ref[8 + k : 9 + k] = jnp.sum(hot[:, k : k + 1] * shares, axis=0, keepdims=True)
        turn(PLAN_LAST[2])
        while small_done[0] <= len(ladder):
            small_event(small_done[0])
            small_done[0] += 1
        turn(PLAN_END)
        while any(done[k] <= work[k].n for k in range(len(work))):
            turn(range(len(work)))
        sum_ref[...] = small_in[...]
        head_out = [head_local(head_chunk[0])]
        for p in range(1, tp_size):
            head_remote(head_chunk[0], p).wait()
            out = pltpu.make_async_copy(
                hg.at[p - 1], rows_at(head_ref, partner_any(tpi, p) * hr, hr),
                local_sems.at[p, 3],
            )
            out.start()
            head_out.append(out)
        for out in head_out:
            out.wait()
        for ch in work:
            ch.out_copy().wait()


def partner_any(index, mask):
    bit = 1
    while bit <= mask:
        if mask & bit:
            index = partner(index, bit)
        bit *= 2
    return index


PLAN_FIRST = (2, 0)
PLAN_STEPS = ((2, 0, 4, 1), (4, 1, 3), (3,), (0,), (2, 1), (0,), (1,), (0, 4, 1), (2,), (0, 3, 5, 4, 1), (2,), (),)
PLAN_TAIL = ((0,), (), (2,), (5,), (),)
PLAN_WAIT = (3, 4, 2, 6, 5, 0, 4, 1, 3)
PLAN_LAST = ((2,), (6, 5), (4, 3),)
PLAN_END = (2, 6, 4, 3, 5, 1, 6, 3, 6, 5, 4, 6, 3)

ORDERS = (
    ("X", 2, 1, 4),
    (2, "X", 1, 4),
    (1, "X", 2, 4),
    ("X", 2, 1, 4),
    (2, "X", 1, 4),
    (1, 2, 4),
    (1, 2, 4),
)


def attn_bwd(qkv, o, lse, do, rows, wt, tiles, gain, onehot, leads, small, parts, mesh, scale):
    _, heads, _, frame = qkv.shape
    rows_dev, width = tiles.shape
    tp_size, dp_size = mesh.shape["tp"], mesh.shape["dp"]
    nbits = dp_size.bit_length() - 1
    half = width // 2
    ph_rows = parts[2].shape[1]
    chunks = [
        dict(tp=True, rows=half, part=0, pre=True, order=ORDERS[0], out=(0, 0)),
        dict(tp=True, rows=half, part=1, pre=True, order=ORDERS[1], out=(0, half)),
        dict(tp=True, rows=half, part=0, order=ORDERS[2], out=(1, 0)),
        dict(tp=True, rows=half, part=1, order=ORDERS[3], out=(1, half)),
        dict(tp=True, rows=ph_rows, part=0, order=ORDERS[4], out=(2, 0), head=(heads * HD, HEAD_ROWS)),
        dict(tp=False, rows=half, order=ORDERS[5], out=(3, 0)),
        dict(tp=False, rows=256, order=ORDERS[6], out=(3, half)),
    ]
    n_k = len(chunks)
    scratch = [
        pltpu.VMEM((frame, HD), BF16),
        pltpu.VMEM((frame, HD), BF16),
        pltpu.VMEM((frame, HD), F32),
        pltpu.VMEM((frame, HD), F32),
        pltpu.VMEM((tp_size, heads, HD, rows_dev), BF16),
        pltpu.VMEM((3, heads, HD, frame), BF16),
        pltpu.VMEM((3, rows_dev, width), BF16),
        pltpu.VMEM((2, rows_dev, width), BF16),
        pltpu.VMEM((rows_dev, width), BF16),
        pltpu.VMEM((16, width), F32),
        pltpu.VMEM((2 + nbits, 16, width), F32),
        pltpu.VMEM((tp_size, 8, width), F32),
        pltpu.VMEM((dp_size, 8, width), F32),
        pltpu.VMEM((tp_size - 1, HEAD_ROWS, width), BF16),
    ]
    for c in chunks:
        r = c["rows"]
        scratch.append(pltpu.VMEM((r, width), BF16))
        scratch.append(pltpu.VMEM((2, r // 2, width), BF16))
        scratch.append(pltpu.VMEM((2, r // 4, width), BF16))
        scratch.append(pltpu.VMEM((2 + max(nbits - 3, 0), r // 8, width), BF16))
        if c["tp"]:
            scratch += [pltpu.VMEM((r, width), BF16)] * 3
        else:
            scratch.append(pltpu.VMEM((r, width), BF16))
    scratch += [
        pltpu.SemaphoreType.DMA((n_k, 17)),
        pltpu.SemaphoreType.DMA((n_k, 17)),
        pltpu.SemaphoreType.DMA((n_k, 4)),
        pltpu.SemaphoreType.DMA((tp_size,)),
        pltpu.SemaphoreType.DMA((tp_size,)),
        pltpu.SemaphoreType.DMA,
        pltpu.SemaphoreType.DMA((3,)),
        pltpu.SemaphoreType.DMA((3,)),
        pltpu.SemaphoreType.DMA((2, tp_size + dp_size)),
        pltpu.SemaphoreType.DMA((2, tp_size + dp_size)),
        pltpu.SemaphoreType.DMA((tp_size - 1,)),
        pltpu.SemaphoreType.DMA((tp_size - 1,)),
    ]
    any_spec = pl.BlockSpec(memory_space=pl.ANY)
    vmem = pl.BlockSpec(memory_space=pltpu.VMEM)
    return pl.pallas_call(
        functools.partial(
            bwd_kernel, scale=scale, chunks=chunks, dp_size=dp_size, heads=heads,
            tp_size=tp_size, width=width,
        ),
        grid=(heads, tp_size),
        in_specs=[vmem, vmem, vmem, any_spec] + [vmem] * 6 + [any_spec] * len(parts),
        out_specs=[vmem, vmem, vmem, any_spec] + [any_spec] * 4,
        out_shape=[
            jax.ShapeDtypeStruct((rows_dev, width), F32),
            jax.ShapeDtypeStruct((16, width), F32),
            jax.ShapeDtypeStruct((8 + leads, width), F32),
            jax.ShapeDtypeStruct((tp_size * HEAD_ROWS, width), BF16),
        ]
        + [
            jax.ShapeDtypeStruct((rows, width), BF16)
            for rows in (width, width, ph_rows, half + chunks[-1]["rows"])
        ],
        scratch_shapes=scratch,
        compiler_params=pltpu.CompilerParams(
            vmem_limit_bytes=60 << 20, collective_id=1, has_side_effects=True
        ),
        cost_estimate=pl.CostEstimate(
            flops=60_000_000_000, bytes_accessed=30 << 20, transcendentals=heads * frame * frame
        ),
        name="attn_bwd",
    )(qkv, o, lse, do, rows, wt, tiles, gain, onehot, small, *parts)


def mid_kernel(
    tiles_ref, o_ref, dots_ref, off_ref, pb_ref, g2_ref, s2_ref, nb_ref, hw_ref, hb_ref, scale_ref,
    pj_own, pj_far, wi_own, wi_far, na_own, na_far,
    dn_ref, dw_ref, ph_ref, do_ref, dx1_ref, small_ref, gates_ref, corr_ref,
    pj, wi, na, x1, hat, rstd, c_low, act, slope, h_low, hg, dx2, dz, du, dc, dy, hd, dn, dw, ph, dos,
    got_n, got_w, got_p, got_x, got_z, c_send, c_recv, x_send, x_recv, in_sem, out_sem, *, tp_size, heads
):
    dpi = lax.axis_index("dp")
    tpi = lax.axis_index("tp")
    rows_dev, width = tiles_ref.shape
    nh = heads * HD
    half = rows_dev // 2
    blocks = [pl.ds(r * half, half) for r in range(2)]

    def loads(k, own, far, dst):
        out = []
        for p in range(tp_size):
            src = own if p == 0 else far.at[p - 1]
            n = src.shape[0]
            to = dst.at[pl.ds(p * n, n)] if len(dst.shape) == 2 else dst.at[p]
            out.append(pltpu.make_async_copy(src, to, in_sem.at[k, p]))
        return out

    load_pj = loads(0, pj_own, pj_far, pj)
    load_wi = loads(1, wi_own, wi_far, wi)
    load_na = loads(2, na_own, na_far, na)
    for cp in load_pj + load_wi + load_na:
        cp.start()
    other = (dpi, partner(tpi, 1))
    side = (partner(dpi, PRE_BIT), tpi)
    far = (dpi, partner(tpi, 2))
    barrier = pltpu.get_barrier_semaphore()
    for dev in (other, side, far):
        pl.semaphore_signal(
            barrier, inc=1, device_id=dev, device_id_type=pl.DeviceIdType.MESH
        )
    mine = lax.rem(lax.div(dpi, PRE_BIT), 2)
    top_rows, quarter = width // 2, width // 4

    def far_copy():
        return pltpu.make_async_remote_copy(
            src_ref=dn.at[2, pl.ds(0, top_rows)], dst_ref=got_x,
            send_sem=x_send.at[0], recv_sem=x_recv.at[0],
            device_id=far, device_id_type=pl.DeviceIdType.MESH,
        )

    def side_copy(j):
        rows = pl.ds(pl.multiple_of(top_rows + (1 - mine) * quarter, 16), quarter)
        return pltpu.make_async_remote_copy(
            src_ref=dn.at[2 * j, rows], dst_ref=got_z.at[j],
            send_sem=x_send.at[1 + j], recv_sem=x_recv.at[1 + j],
            device_id=side, device_id_type=pl.DeviceIdType.MESH,
        )

    def core_copy(k, j, src, got):
        return pltpu.make_async_remote_copy(
            src_ref=src.at[2 * j + 1], dst_ref=got.at[j],
            send_sem=c_send.at[k, j], recv_sem=c_recv.at[k, j],
            device_id=other, device_id_type=pl.DeviceIdType.MESH,
        )

    small_ref[...] = jnp.zeros_like(small_ref)
    proj_bias, gain2, shift2, out_bias = (row_of(v) for v in (pb_ref, g2_ref, s2_ref, nb_ref))
    for cp in load_pj:
        cp.wait()
    for r in blocks:
        v = tiles_ref[r].astype(F32) + dot(o_ref[:, r], pj[...], ((0,), (0,))) + proj_bias
        x1[r] = v
        hv, rs = norm_parts(v)
        hat[r] = hv
        rstd[r] = rs
        c_low[r] = (hv * gain2 + shift2).astype(BF16)
    for p in range(tp_size):
        load_wi[p].wait()
        cols = pl.ds(p * width, width)
        for r in blocks:
            m, d = gelu_parts(dot(c_low[r], wi[p]) + off_ref[p, 0:1])
            act[r, cols] = m.astype(BF16)
            slope[r, cols] = d.astype(BF16)
    for cp in load_na:
        cp.wait()
    for r in blocks:
        h_low[r] = (x1[r] + dot(act[r], na[...]) + out_bias).astype(BF16)

    logits = dot(hw_ref[...], h_low[...], ((1,), (1,))) + hb_ref[...]
    row_scale = scale_ref[0:1, 0:1]
    lg = [logits[e * HEAD_ROWS : (e + 1) * HEAD_ROWS] for e in range(EXPERTS)]
    top = jnp.maximum(jnp.maximum(lg[0], lg[1]), lg[2])
    ex = [jnp.exp(v - top) for v in lg]
    inv = 1.0 / (ex[0] + ex[1] + ex[2])
    gt = [v * inv for v in ex]
    mixed = gt[0] * dots_ref[0] + gt[1] * dots_ref[1] + gt[2] * dots_ref[2]
    for e in range(EXPERTS):
        gates_ref[e] = gt[e]
        hg[e * HEAD_ROWS : (e + 1) * HEAD_ROWS] = (gt[e] * (dots_ref[e] - mixed)).astype(BF16)
    hg[EXPERTS * HEAD_ROWS :] = (dots_ref[EXPERTS] * row_scale).astype(BF16)
    corr_ref[...] = logits[EXPERTS * HEAD_ROWS :] * row_scale
    d2 = dot(hg[...], hw_ref[...], ((0,), (0,)))
    dx2[...] = d2
    dz[...] = d2.astype(BF16)
    small_ref[0:1] = jnp.sum(d2, axis=0, keepdims=True)
    ones = jnp.ones((8, rows_dev), BF16)
    small_ref[4:5, : tp_size * HEAD_ROWS] = dot(ones, hg[...], ((1,), (1,)))[0:1]

    def send_out(k, p, src, dst):
        cp = pltpu.make_async_copy(src, dst, out_sem.at[k, p])
        cp.start()
        return cp

    outs = []
    pairs = range(tp_size // 2)

    def narrow_dot(p):
        return dot(act[:, p * width : (p + 1) * width], dz[...], ((0,), (0,)))

    def wide_dot(p):
        return dot(c_low[...], du[p], ((0,), (0,)))

    pl.semaphore_wait(barrier, 3)
    for j in (1, 0):
        dn[2 * j + 1] = narrow_dot(2 * j + 1).astype(BF16)
        core_copy(0, j, dn, got_n).start()
    def hidden_grad(p):
        cols = pl.ds(p * width, width)
        for r in blocks:
            v = dot(dz[r], na[cols], ((1,), (1,))) * slope[r, cols].astype(F32)
            low = v.astype(BF16)
            du[p, r] = low
            small_ref[8 + p : 9 + p] += jnp.sum(low.astype(F32), axis=0, keepdims=True)
    hidden_grad(1)
    hidden_grad(3)
    for j in (1, 0):
        core_copy(0, j, dn, got_n).wait()
        dn[2 * j] = (narrow_dot(2 * j) + got_n[j].astype(F32)).astype(BF16)
        if j == 1:
            far_copy().start()
        side_copy(j).start()
    hidden_grad(0)
    hidden_grad(2)
    for j in pairs:
        dw[2 * j + 1] = wide_dot(2 * j + 1).astype(BF16)
        core_copy(1, j, dw, got_w).start()
    for r in blocks:
        g = dot(du[0, r], wi[0], ((1,), (1,)))
        for p in range(1, tp_size):
            g = g + dot(du[p, r], wi[p], ((1,), (1,)))
        hv = hat[r]
        d1 = dx2[r] + norm_back(hv, rstd[r], gain2, g)
        dx1_ref[r] = d1
        dy[r] = d1.astype(BF16)
        small_ref[1:2] += jnp.sum(g * hv, axis=0, keepdims=True)
        small_ref[2:3] += jnp.sum(g, axis=0, keepdims=True)
        small_ref[3:4] += jnp.sum(d1, axis=0, keepdims=True)
    dos[...] = dot(pj[...], dy[...], ((1,), (1,))).astype(BF16).reshape(dos.shape)
    outs.append(send_out(2, 0, dos, do_ref))
    dp = dot(o_ref[...], dy[...]).astype(BF16)
    hd[...] = dot(hg[...], h_low[...]).astype(BF16)
    for p in range(tp_size):
        ph[p, 0:nh] = dp[p * nh : (p + 1) * nh]
        at = pl.ds(pl.multiple_of(partner_any(tpi, p) * HEAD_ROWS, 16), HEAD_ROWS)
        ph[p, nh : nh + HEAD_ROWS] = hd[at]
        ph[p, nh + HEAD_ROWS :] = jnp.zeros((ph.shape[1] - nh - HEAD_ROWS, width), BF16)
    for j in pairs:
        core_copy(2, j, ph, got_p).start()
    for j in pairs:
        core_copy(1, j, dw, got_w).wait()
        dw[2 * j] = (wide_dot(2 * j) + got_w[j].astype(F32)).astype(BF16)
        outs.append(send_out(1, j, dw.at[2 * j], dw_ref.at[j]))
    for j in pairs:
        core_copy(2, j, ph, got_p).wait()
        ph[2 * j] = (ph[2 * j].astype(F32) + got_p[j].astype(F32)).astype(BF16)
        outs.append(send_out(3, j, ph.at[2 * j], ph_ref.at[j]))
    far_copy().wait()
    add_rows(dn.at[0], got_x, None, 0, 0, top_rows)
    for j in (1, 0):
        side_copy(j).wait()
        add_rows(dn.at[2 * j], got_z, j, top_rows + mine * quarter, 0, quarter)
        outs.append(send_out(0, j, dn.at[2 * j], dn_ref.at[j]))
    for cp in outs:
        cp.wait()


def mid(tiles, o_own, dots, off, vecs, hw, hb, row_scale, weights, mesh, heads):
    rows_dev, width = tiles.shape
    tp_size = mesh.shape["tp"]
    nh = heads * HD
    ph_rows = -(-(nh + HEAD_ROWS) // 128) * 128
    n_head = hw.shape[0]
    any_spec = pl.BlockSpec(memory_space=pl.ANY)
    vmem = pl.BlockSpec(memory_space=pltpu.VMEM)
    big = (tp_size, width, width)
    pair = (tp_size // 2,)
    return pl.pallas_call(
        functools.partial(mid_kernel, tp_size=tp_size, heads=heads),
        in_specs=[vmem] * 11 + [any_spec] * 6,
        out_specs=[any_spec] * 4 + [vmem] * 4,
        out_shape=[
            jax.ShapeDtypeStruct(pair + (width, width), BF16),
            jax.ShapeDtypeStruct(pair + (width, width), BF16),
            jax.ShapeDtypeStruct(pair + (ph_rows, width), BF16),
            jax.ShapeDtypeStruct((tp_size, heads, HD, rows_dev), BF16),
            jax.ShapeDtypeStruct((rows_dev, width), F32),
            jax.ShapeDtypeStruct((16, width), F32),
            jax.ShapeDtypeStruct((EXPERTS, HEAD_ROWS, rows_dev), F32),
            jax.ShapeDtypeStruct((HEAD_ROWS, rows_dev), F32),
        ],
        scratch_shapes=[
            pltpu.VMEM((tp_size * nh, width), BF16),
            pltpu.VMEM(big, BF16),
            pltpu.VMEM((tp_size * width, width), BF16),
            pltpu.VMEM((rows_dev, width), F32),
            pltpu.VMEM((rows_dev, width), F32),
            pltpu.VMEM((rows_dev, 1), F32),
            pltpu.VMEM((rows_dev, width), BF16),
            pltpu.VMEM((rows_dev, tp_size * width), BF16),
            pltpu.VMEM((rows_dev, tp_size * width), BF16),
            pltpu.VMEM((rows_dev, width), BF16),
            pltpu.VMEM((n_head, rows_dev), BF16),
            pltpu.VMEM((rows_dev, width), F32),
            pltpu.VMEM((rows_dev, width), BF16),
            pltpu.VMEM((tp_size, rows_dev, width), BF16),
            pltpu.VMEM((8, width), F32),
            pltpu.VMEM((rows_dev, width), BF16),
            pltpu.VMEM((n_head, width), BF16),
            pltpu.VMEM(big, BF16),
            pltpu.VMEM(big, BF16),
            pltpu.VMEM((tp_size, ph_rows, width), BF16),
            pltpu.VMEM((tp_size, heads, HD, rows_dev), BF16),
            pltpu.VMEM(pair + (width, width), BF16),
            pltpu.VMEM(pair + (width, width), BF16),
            pltpu.VMEM(pair + (ph_rows, width), BF16),
            pltpu.VMEM((width // 2, width), BF16),
            pltpu.VMEM(pair + (width // 4, width), BF16),
            pltpu.SemaphoreType.DMA((3, tp_size // 2)),
            pltpu.SemaphoreType.DMA((3, tp_size // 2)),
            pltpu.SemaphoreType.DMA((3,)),
            pltpu.SemaphoreType.DMA((3,)),
            pltpu.SemaphoreType.DMA((3, tp_size)),
            pltpu.SemaphoreType.DMA((4, tp_size)),
        ],
        compiler_params=pltpu.CompilerParams(
            vmem_limit_bytes=MID_VMEM, collective_id=2, has_side_effects=True
        ),
        cost_estimate=pl.CostEstimate(
            flops=18_000_000_000, bytes_accessed=30 << 20, transcendentals=2_000_000
        ),
        name="mid",
    )(tiles, o_own, dots, off, *vecs, hw, hb, row_scale, *weights)


def finish_kernel(
    n_ref, i_ref, ph_ref, qa_ref, qb_ref, hd_ref, tok_ref, dx_ref, table_ref, small_ref,
    no_ref, io_ref, po_ref, qo_ref, g_ref, c_ref, to_ref, lead_ref, *vec_refs, fields
):
    no_ref[...] = n_ref[...].astype(F32)
    io_ref[...] = i_ref[...].astype(F32)
    po_ref[...] = ph_ref[...].astype(F32)
    na = qa_ref.shape[0]
    qo_ref[0, :na] = qa_ref[...].astype(F32)
    qo_ref[0, na:] = qb_ref[...].astype(F32)
    for e in range(EXPERTS):
        g_ref[e * fields : (e + 1) * fields] = hd_ref[pl.ds(e * HEAD_ROWS, HEAD_ROWS)].astype(F32)[
            :fields
        ]
    c_ref[...] = hd_ref[pl.ds(EXPERTS * HEAD_ROWS, HEAD_ROWS)].astype(F32)[:fields]
    to_ref[...] = tok_ref[...] + dx_ref[...]
    lead_ref[...] = table_ref[8:]
    rows = [table_ref[0:1], table_ref[1:2]] + [small_ref[k : k + 1] for k in (3, 1, 2, 8, 0)]
    for ref, row in zip(vec_refs, rows):
        ref[...] = row.reshape(row.shape[1])


def finish(n, i, ph, q, hd, tok, dx1, table, small, heads, fields):
    width = n.shape[0]
    nh = heads * HD
    steps = 3
    rows = width // steps
    first = (width // 2) // (3 * HD) * HD
    second = nh - first
    base = 3 * first // second
    tok_rows = tok.shape[0] // 2
    leads = table.shape[0] - 8

    def by_row(r):
        return pl.BlockSpec((r, width), lambda g: (g, 0))

    token = pl.BlockSpec((tok_rows, width), lambda g: (jnp.minimum(g, 1), 0))
    return pl.pallas_call(
        functools.partial(finish_kernel, fields=fields),
        grid=(steps,),
        in_specs=[
            by_row(rows),
            by_row(rows),
            by_row(nh // steps),
            by_row(first),
            pl.BlockSpec((second, width), lambda g: (base + g, 0)),
            pl.BlockSpec((hd.shape[0], rows), lambda g: (0, g)),
            token,
            token,
            pl.BlockSpec(table.shape, lambda g: (0, 0)),
            pl.BlockSpec(small.shape, lambda g: (0, 0)),
        ],
        out_specs=[
            by_row(rows),
            by_row(rows),
            by_row(nh // steps),
            pl.BlockSpec((1, nh, width), lambda g: (g, 0, 0)),
            pl.BlockSpec((EXPERTS * fields, rows), lambda g: (0, g)),
            pl.BlockSpec((fields, rows), lambda g: (0, g)),
            token,
            pl.BlockSpec((leads, width), lambda g: (0, 0)),
        ]
        + [pl.BlockSpec((width,), lambda g: (0,))] * 7,
        out_shape=[
            jax.ShapeDtypeStruct((width, width), F32),
            jax.ShapeDtypeStruct((width, width), F32),
            jax.ShapeDtypeStruct((nh, width), F32),
            jax.ShapeDtypeStruct((3, nh, width), F32),
            jax.ShapeDtypeStruct((EXPERTS * fields, width), F32),
            jax.ShapeDtypeStruct((fields, width), F32),
            jax.ShapeDtypeStruct(tok.shape, F32),
            jax.ShapeDtypeStruct((leads, width), F32),
        ]
        + [jax.ShapeDtypeStruct((width,), F32)] * 7,
        name="finish",
    )(n, i, ph, q, q, hd, tok, dx1, table, small)


def norm_parts(values):
    center = values - jnp.mean(values, axis=-1, keepdims=True)
    rstd = lax.rsqrt(jnp.mean(center * center, axis=-1, keepdims=True) + EPSILON)
    return center * rstd, rstd


def norm_back(hat, rstd, gain, grad):
    g = grad * gain
    return rstd * (
        g
        - jnp.mean(g, axis=-1, keepdims=True)
        - hat * jnp.mean(g * hat, axis=-1, keepdims=True)
    )


def gelu_parts(u):
    half = jnp.exp(-0.5 * u * u)
    t = 1.0 / (1.0 + (0.3275911 * 0.7071067811865476) * jnp.abs(u))
    poly = t * (
        0.254829592
        + t * (-0.284496736 + t * (1.421413741 + t * (-1.453152027 + t * 1.061405429)))
    )
    tail = 0.5 * poly * half
    cdf = jnp.where(u >= 0, 1.0 - tail, tail)
    return u * cdf, cdf + u * half * 0.3989422804014327


def make_body(mesh):
    tp_size = mesh.shape["tp"]

    def body(
        tile_vectors,
        snapshot_horizon_slot,
        horizon_sample_tally,
        specialist_outlooks,
        early_layernorm_scale,
        early_layernorm_shift,
        horizon_vectors,
        triple_head_matrix,
        attending_matrix,
        attending_offset,
        later_layernorm_scale,
        later_layernorm_shift,
        widening_matrix,
        widening_offset,
        narrowing_matrix,
        narrowing_offset,
        router_matrix,
        router_offset,
        adjuster_matrix,
        adjuster_offset,
        combined_loss_slope,
    ):
        rows_dev, width = tile_vectors.shape
        heads = triple_head_matrix.shape[2] // HD
        rows_frame = rows_dev * tp_size
        fields = adjuster_matrix.shape[1]
        sites = combined_loss_slope.shape[1]
        scale_val = HD ** (-0.5)
        tp_index = lax.axis_index("tp")
        lead = snapshot_horizon_slot[0]
        row_scale = lax.rsqrt(
            lax.dynamic_slice_in_dim(horizon_sample_tally, lead, 1, 0).astype(F32)
        )[0]
        nh = heads * HD
        w_t = jnp.transpose(triple_head_matrix, (0, 2, 1))
        (attn_rows, qkv, o_heads, lse, o_own, dots, off_all, proj_all, wide_all, narrow_all) = attn_fwd(
            snapshot_horizon_slot,
            tile_vectors,
            early_layernorm_scale,
            early_layernorm_shift,
            horizon_vectors,
            widening_offset,
            w_t,
            attending_matrix,
            widening_matrix,
            narrowing_matrix,
            specialist_outlooks,
            combined_loss_slope,
            mesh,
            scale_val,
        )

        def head_pad(x):
            x = x.reshape((EXPERTS + 1, fields) + x.shape[1:])
            x = jnp.pad(x, ((0, 0), (0, HEAD_ROWS - fields)) + ((0, 0),) * (x.ndim - 2))
            return x.reshape((-1,) + x.shape[2:])

        hw = head_pad(jnp.concatenate([router_matrix, adjuster_matrix], axis=1).T)
        hb = head_pad(jnp.concatenate([router_offset, adjuster_offset])[:, None])
        vec = (attending_offset, later_layernorm_scale, later_layernorm_shift, narrowing_offset)
        (d_narrow, d_wide, d_ph, do_all, dx1, small, gates, corr) = mid(
            tile_vectors,
            o_own.reshape(tp_size * nh, rows_dev),
            dots,
            off_all,
            vec,
            hw,
            hb,
            row_scale[None, None],
            [
                attending_matrix, proj_all, widening_matrix, wide_all,
                narrowing_matrix, narrow_all,
            ],
            mesh,
            heads,
        )
        gates = gates[:, :fields]
        corr = corr[:fields]

        blended = (corr)[:, None, :]
        for e in range(EXPERTS):
            blended = blended + gates[e][:, None, :] * specialist_outlooks[e].astype(F32)

        leads = horizon_vectors.shape[0]
        onehot = (jnp.arange(width, dtype=jnp.int32) == lead).astype(F32)[None, :]
        (token_part, small, table, head_sum, n_low, i_low, ph, q_low) = attn_bwd(
            qkv, o_heads, lse, do_all, attn_rows.reshape(rows_frame, width), w_t.reshape(3 * nh, width), tile_vectors,
            early_layernorm_scale, onehot, leads, small,
            [d_narrow, d_wide, d_ph], mesh, scale_val,
        )
        (
            narrow_sum, wide_sum, proj_weight_grad, qkv_sum, gate_sum, correct_sum, tokens_grad,
            lead_sum, gain1_sum, shift1_sum, proj_bias_sum, gain2_sum, shift2_sum, in_bias_sum,
            out_bias_sum,
        ) = finish(
            n_low, i_low, ph, q_low, head_sum, token_part, dx1, table, small, heads, fields
        )
        qkv_sum = jnp.transpose(qkv_sum, (0, 2, 1))
        gate_weight_grad = gate_sum.T
        correct_weight_grad = correct_sum.T
        head_bias = small[4, : (EXPERTS + 1) * HEAD_ROWS].reshape(EXPERTS + 1, HEAD_ROWS)
        head_bias = head_bias[:, :fields]

        return (
            blended,
            tokens_grad,
            gain1_sum,
            shift1_sum,
            lead_sum,
            qkv_sum,
            proj_weight_grad,
            proj_bias_sum,
            gain2_sum,
            shift2_sum,
            wide_sum,
            in_bias_sum,
            narrow_sum,
            out_bias_sum,
            gate_weight_grad,
            head_bias[:EXPERTS].reshape(EXPERTS * fields),
            correct_weight_grad,
            head_bias[EXPERTS],
        )

    return body


def solution(mesh):
    return jax.shard_map(
        make_body(mesh),
        mesh=mesh,
        in_specs=(
            P(("dp", "tp"), None),
            P("dp"),
            P(),
            P(None, None, None, ("dp", "tp")),
            P(),
            P(),
            P(),
            P(None, None, "tp"),
            P("tp", None),
            P(),
            P(),
            P(),
            P(None, "tp"),
            P("tp"),
            P("tp", None),
            P(),
            P(),
            P(),
            P(),
            P(),
            P(None, None, ("dp", "tp")),
        ),
        out_specs=(
            P(None, None, ("dp", "tp")),
            P(("dp", "tp"), None),
            P(),
            P(),
            P(),
            P(None, None, "tp"),
            P("tp", None),
            P(),
            P(),
            P(),
            P(None, "tp"),
            P("tp"),
            P("tp", None),
            P(),
            P(),
            P(),
            P(),
            P(),
        ),
        check_vma=False,
    )
```

```python
import functools
import jax
import jax.numpy as jnp
from jax import lax
from jax.experimental import pallas as pl
from jax.experimental.pallas import tpu as pltpu
from jax.sharding import PartitionSpec as P

HD = 64
EXPERTS = 3
HEAD_ROWS = 80
MID_VMEM = 62 << 20
PRE_BIT = 2
EPSILON = 1e-05
F32 = jnp.float32
BF16 = jnp.bfloat16


def dot(a, b, dims=((1,), (0,))):
    return lax.dot_general(a, b, (dims, ((), ())), preferred_element_type=F32)


def row_of(ref):
    return ref[...].reshape(1, ref.shape[0])


W_FLIGHT = 6
W_PLAN = (
    (0, (("far", 0),)),
    (1, (("far", 1),)),
    (3, (("far", 2), (0, 0))),
    (4, ((0, 1),)),
    (5, ((0, 2),)),
    (6, (("far", 3),)),
    (7, ((1, 1),)),
    (9, (("far", 4),)),
    (10, ((1, 2), (0, 3), ("far", 5))),
    (11, ((0, 4), (0, 5))),
)


def fwd_kernel(
    lead_ref, tiles_ref, gain_ref, shift_ref, table_ref, off_ref, wt_ref, proj_ref, wide_ref,
    narrow_ref, exp_ref, slope_ref,
    rows_out, qkv_ref, o_ref, lse_ref, own_out, dots_ref, off_out, proj_all, wide_all, narrow_all,
    offs, off_send, off_recv, rows_ref, own_ref, out_sem, ks, stream, stream_g, stream_sem, row_send, row_recv, o_send, o_recv, o_local,
    w_send, w_recv, *, scale, dp_size, tp_size, heads
):
    i, h = pl.program_id(0), pl.program_id(1)
    steps = tp_size * heads
    step = i * heads + h
    dpi, tpi = lax.axis_index("dp"), lax.axis_index("tp")
    rows_dev, width = tiles_ref.shape
    piece = rows_dev // 2

    def remote(src, dst, ssem, rsem, axis, bit):
        dev = (partner(dpi, bit), tpi) if axis == "dp" else (dpi, partner_any(tpi, bit))
        return pltpu.make_async_remote_copy(
            src_ref=src, dst_ref=dst, send_sem=ssem, recv_sem=rsem,
            device_id=dev, device_id_type=pl.DeviceIdType.MESH,
        )

    def row_copy(kind, c):
        a, b, bit = ((0, 1, 1), (0, 2, 2), (2, 3, 1))[kind]
        here = pl.ds(c * piece, piece)
        return remote(
            rows_ref.at[a, here], rows_ref.at[b, here],
            row_send.at[kind, c], row_recv.at[kind, c], "tp", bit,
        )

    def off_copy(m):
        return remote(offs.at[0], offs.at[m], off_send.at[m], off_recv.at[m], "tp", m)

    parts = []
    for src, dst, cuts, share in (
        (proj_ref, proj_all, (1,), (1,)),
        (narrow_ref, narrow_all, (2, 2), (1, 2)),
        (wide_ref, wide_all, (2, 3, 6), (1,)),
    ):
        lo = 0
        for cut in cuts:
            n = src.shape[0] // cut
            parts.append((src, dst, lo, n, share))
            lo += n

    def w_rows(n, stage, theirs=False):
        _, _, lo, size, share = parts[n]
        size = size // (1 << len(share))
        for bit in share[:stage]:
            size *= 2
        at = lo
        step = size
        for k, bit in enumerate(share[stage:]):
            mine = lax.rem(lax.div(dpi, bit), 2)
            if theirs and k == 0:
                mine = 1 - mine
            at = at + mine * step
            step *= 2
        return pl.ds(pl.multiple_of(at, 16), size)

    def w_far(n):
        src, dst = parts[n][:2]
        rows = w_rows(n, 0)
        return remote(
            src.at[rows], dst.at[1, rows], w_send.at[n, 0], w_recv.at[n, 0], "tp", 2
        )

    def w_side(n, k):
        rows = w_rows(n, k)
        here = parts[n][1].at[1, rows]
        return remote(
            here, here, w_send.at[n, 1 + k], w_recv.at[n, 1 + k], "dp", parts[n][4][k]
        )

    def w_fwd(n, k):
        dst = parts[n][1]
        rows = w_rows(n, 0) if k == 0 else w_rows(n, k - 1, True)
        return remote(
            dst.at[1, rows], dst.at[2, rows], w_send.at[n, 3 + k], w_recv.at[n, 3 + k], "tp", 1
        )

    def w_near(n):
        src, dst, lo, size, _ = parts[n]
        rows = pl.ds(lo, size)
        return remote(src.at[rows], dst.at[0, rows], w_send.at[n, 6], w_recv.at[n, 6], "tp", 1)

    def o_copy(p):
        if p == 0:
            return pltpu.make_async_copy(o_ref.at[0], own_ref.at[0], o_local)
        return remote(o_ref.at[p], own_ref.at[p], o_send.at[p], o_recv.at[p], "tp", p)

    fields, sites = slope_ref.shape[0], slope_ref.shape[1]
    per = stream.shape[2]
    groups = fields // per
    depth = stream.shape[0]

    def stream_copies(g):
        slot = lax.rem(g, depth)
        at = pl.ds(g * per, per)
        return (
            pltpu.make_async_copy(
                exp_ref.at[:, at], stream.at[slot], stream_sem.at[slot, 0]
            ),
            pltpu.make_async_copy(
                slope_ref.at[at], stream_g.at[slot], stream_sem.at[slot, 1]
            ),
        )

    @pl.when(step == 0)
    def _():
        barrier = pltpu.get_barrier_semaphore()
        others = [("tp", 1), ("tp", 2), ("tp", 3), ("dp", 1), ("dp", 2)]
        for axis, bit in others:
            dev = (partner(dpi, bit), tpi) if axis == "dp" else (dpi, partner_any(tpi, bit))
            pl.semaphore_signal(
                barrier, inc=1, device_id=dev, device_id_type=pl.DeviceIdType.MESH
            )
        for g in range(min(depth - 1, groups)):
            for cp in stream_copies(g):
                cp.start()
        blk = 64
        gain = row_of(gain_ref)
        shift = row_of(shift_ref) + table_ref[pl.ds(lead_ref[0], 1)]
        offs[0, 0:1] = row_of(off_ref)

        def norm_rows(r, carry):
            here = pl.ds(pl.multiple_of(r * blk, blk), blk)
            hat, _ = norm_parts(tiles_ref[here].astype(F32))
            rows_ref[0, here] = (hat * gain + shift).astype(BF16)
            return carry

        half = piece // blk
        lax.fori_loop(0, half, norm_rows, 0)
        pl.semaphore_wait(barrier, len(others))
        row_copy(1, 0).start()
        lax.fori_loop(half, 2 * half, norm_rows, 0)
        row_copy(1, 1).start()
        row_copy(0, 0).start()
        row_copy(0, 1).start()
        for m in range(1, tp_size):
            off_copy(m).start()
        for n in range(W_FLIGHT):
            w_far(n).start()

        def contract(g, carry):
            @pl.when(g + depth - 1 < groups)
            def _():
                for cp in stream_copies(g + depth - 1):
                    cp.start()

            for cp in stream_copies(g):
                cp.wait()
            slot = lax.rem(g, depth)
            for j in range(per):
                slope = stream_g[slot, j].astype(F32)
                for e in range(EXPERTS):
                    dots_ref[e, pl.ds(g * per + j, 1)] = jnp.sum(
                        stream[slot, e, j].astype(F32) * slope, axis=0, keepdims=True
                    )
                dots_ref[EXPERTS, pl.ds(g * per + j, 1)] = jnp.sum(slope, axis=0, keepdims=True)
            return carry

        dots_ref[...] = jnp.zeros_like(dots_ref)
        lax.fori_loop(0, groups, contract, 0)

        def project(p):
            lane = pl.ds(p * rows_dev, rows_dev)
            for s in range(3):
                part = dot(wt_ref[s], rows_ref[p], ((1,), (1,))).astype(BF16)
                qkv_ref[s, :, :, lane] = part.reshape(heads, HD, rows_dev)
            for hh in range(heads):
                ks[hh, lane] = qkv_ref[1, hh, :, lane].T

        project(0)
        for c in range(2):
            row_copy(0, c).wait()
        project(1)
        for c in range(2):
            row_copy(1, c).wait()
            row_copy(2, c).start()
        project(2)
        for c in range(2):
            row_copy(2, c).wait()
        for n in range(len(parts)):
            w_near(n).start()
        rows_copy = pltpu.make_async_copy(rows_ref, rows_out, out_sem.at[0])
        rows_copy.start()
        project(3)

    p = lax.rem(i + 2, tp_size)
    lanes = pl.ds(pl.multiple_of(p * rows_dev, rows_dev), rows_dev)
    q = qkv_ref[0, h, :, lanes] * jnp.bfloat16(scale)
    s = dot(ks[h], q)
    m = jnp.max(s, axis=0, keepdims=True)
    e = jnp.exp(s - m)
    l = jnp.sum(e, axis=0, keepdims=True)
    o_ref[p, h] = (dot(qkv_ref[2, h], e.astype(BF16)) / l).astype(BF16)
    lse_ref[p, h] = m + jnp.log(l)

    seq = {}

    def after(st, *what):
        seq.setdefault(min(st, steps - 1), []).extend(what)

    for st, what in W_PLAN:
        after(st, *what)
    for st, what in seq.items():

        @pl.when(step == st)
        def _():
            for kind, n in what:
                if kind == "far":
                    w_far(n).wait()
                    if n + W_FLIGHT < len(parts):
                        w_far(n + W_FLIGHT).start()
                    w_side(n, 0).start()
                    w_fwd(n, 0).start()
                else:
                    w_side(n, kind).wait()
                    if kind + 1 < len(parts[n][4]):
                        w_side(n, kind + 1).start()
                    w_fwd(n, kind + 1).start()

    for k in range(tp_size):

        @pl.when(step == k * heads + heads - 1)
        def _():
            o_copy((k + 2) % tp_size).start()

    @pl.when(step == steps - 1)
    def _():
        for k in range(tp_size):
            o_copy(k).wait()
        for m in range(1, tp_size):
            off_copy(m).wait()
        off_out[...] = offs[...]
        own_copy = pltpu.make_async_copy(own_ref, own_out, out_sem.at[1])
        own_copy.start()
        for n in range(len(parts)):
            w_near(n).wait()
            for k in range(1 + len(parts[n][4])):
                w_fwd(n, k).wait()
        own_copy.wait()
        pltpu.make_async_copy(rows_ref, rows_out, out_sem.at[0]).wait()


def attn_fwd(
    lead, tiles, gain, shift, table, off, wt, proj, wide, narrow, experts, slope, mesh, scale
):
    rows_dev, width = tiles.shape
    heads = proj.shape[0] // HD
    tp_size, dp_size = mesh.shape["tp"], mesh.shape["dp"]
    frame = tp_size * rows_dev
    fields, sites = slope.shape[0], slope.shape[1]
    per = 3 if fields % 3 == 0 else 1
    depth = 4
    any_spec = pl.BlockSpec(memory_space=pl.ANY)
    vmem = pl.BlockSpec(memory_space=pltpu.VMEM)
    return pl.pallas_call(
        functools.partial(
            fwd_kernel, scale=scale, dp_size=dp_size, tp_size=tp_size, heads=heads
        ),
        grid=(tp_size, heads),
        in_specs=[pl.BlockSpec(memory_space=pltpu.SMEM)] + [vmem] * 6 + [any_spec] * 5,
        out_specs=[any_spec] + [vmem] * 3 + [any_spec, vmem, vmem] + [any_spec] * 3,
        out_shape=[
            jax.ShapeDtypeStruct((tp_size, rows_dev, width), BF16),
            jax.ShapeDtypeStruct((3, heads, HD, frame), BF16),
            jax.ShapeDtypeStruct((tp_size, heads, HD, rows_dev), BF16),
            jax.ShapeDtypeStruct((tp_size, heads, 1, rows_dev), F32),
            jax.ShapeDtypeStruct((tp_size, heads, HD, rows_dev), BF16),
            jax.ShapeDtypeStruct((EXPERTS + 1, HEAD_ROWS, rows_dev), F32),
            jax.ShapeDtypeStruct((tp_size, 8, width), F32),
            jax.ShapeDtypeStruct((tp_size - 1,) + proj.shape, BF16),
            jax.ShapeDtypeStruct((tp_size - 1,) + wide.shape, BF16),
            jax.ShapeDtypeStruct((tp_size - 1,) + narrow.shape, BF16),
        ],
        scratch_shapes=[
            pltpu.VMEM((tp_size, 8, width), F32),
            pltpu.SemaphoreType.DMA((tp_size,)),
            pltpu.SemaphoreType.DMA((tp_size,)),
            pltpu.VMEM((tp_size, rows_dev, width), BF16),
            pltpu.VMEM((tp_size, heads, HD, rows_dev), BF16),
            pltpu.SemaphoreType.DMA((2,)),
            pltpu.VMEM((heads, frame, HD), BF16),
            pltpu.VMEM((depth, EXPERTS, per, sites, rows_dev), BF16),
            pltpu.VMEM((depth, per, sites, rows_dev), BF16),
            pltpu.SemaphoreType.DMA((depth, 2)),
            pltpu.SemaphoreType.DMA((3, 2)),
            pltpu.SemaphoreType.DMA((3, 2)),
            pltpu.SemaphoreType.DMA((tp_size,)),
            pltpu.SemaphoreType.DMA((tp_size,)),
            pltpu.SemaphoreType.DMA,
            pltpu.SemaphoreType.DMA((6, 7)),
            pltpu.SemaphoreType.DMA((6, 7)),
        ],
        compiler_params=pltpu.CompilerParams(
            vmem_limit_bytes=56 << 20, collective_id=0, has_side_effects=True
        ),
        cost_estimate=pl.CostEstimate(
            flops=30_000_000_000, bytes_accessed=40 << 20, transcendentals=heads * frame * frame
        ),
        name="attn_fwd",
    )(lead, tiles, gain, shift, table, off, wt, proj, wide, narrow, experts, slope)


def partner(index, bit):
    return index + bit - 2 * bit * lax.rem(lax.div(index, bit), 2)


def rows_at(ref, start, size):
    return ref.at[pl.ds(pl.multiple_of(start, 16), size)]


def add_rows(dst, src, lead, dst_off, src_off, size):
    step = 48 if size % 48 == 0 else 32

    def one(r, carry):
        here = pl.ds(pl.multiple_of(dst_off + r * step, 16), step)
        there = pl.ds(pl.multiple_of(src_off + r * step, 16), step)
        got = src[there] if lead is None else src[lead, there]
        dst[here] = (dst[here].astype(F32) + got.astype(F32)).astype(BF16)
        return carry

    lax.fori_loop(0, size // step, one, 0)


def bwd_kernel(
    qkv_ref, o_ref, lse_ref, do_ref, rows_ref, wt_ref, tiles_ref, gain_ref, onehot_ref, small_ref,
    *rest, scale, chunks, dp_size, heads, tp_size, width
):
    n_src = sum(1 for c in chunks if c["tp"] and c["part"] == 0)
    srcs = rest[:n_src]
    tok_ref, sum_ref, last_ref, head_ref = rest[n_src : n_src + 4]
    n_out = n_src + 4 + 4
    outs = rest[n_src + 4 : n_out]
    (
        ks, vs, dks, dvs, dos, dqkv, da_far, da_core, da_across,
        small_in, small_got, last_tp, last_dp, hg,
    ) = rest[n_out : n_out + 14]
    per = rest[n_out + 14 : -12]
    (
        send_sems, recv_sems, local_sems, do_send, do_recv, do_local, da_send, da_recv,
        vec_send, vec_recv, hg_send, hg_recv,
    ) = rest[-12:]
    h, i = pl.program_id(0), pl.program_id(1)
    steps = tp_size * heads
    step = h * tp_size + i
    dpi, tpi = lax.axis_index("dp"), lax.axis_index("tp")
    rows_dev = dos.shape[3]
    bits = [1 << b for b in range(dp_size.bit_length() - 1)]

    def remote(src, dst, ssem, rsem, axis, bit):
        dev = (partner_any(dpi, bit), tpi) if axis == "dp" else (dpi, partner_any(tpi, bit))
        return pltpu.make_async_remote_copy(
            src_ref=src, dst_ref=dst, send_sem=ssem, recv_sem=rsem,
            device_id=dev, device_id_type=pl.DeviceIdType.MESH,
        )

    def bit_of(bit):
        return lax.rem(lax.div(dpi, bit), 2)

    bufs, at = [], 0
    for c in chunks:
        n = 7 if c["tp"] else 5
        bufs.append(per[at : at + n])
        at += n

    class Chunk:
        def __init__(self, k):
            self.k, self.c = k, chunks[k]
            self.rows, self.order = self.c["rows"], self.c["order"]
            self.acc = bufs[k][0]
            self.halves = bufs[k][1:4]
            if self.c["tp"]:
                self.mid, self.fin, self.got_x = bufs[k][4:7]
            else:
                self.fin = bufs[k][4]
            self.stages = []
            if self.c["tp"]:
                self.stages.append(("C", 0, None))
            size, seq, far = self.rows, [], self.c["tp"]
            for name in self.order:
                if name == "X":
                    far = False
                    self.stages.append(("X", size, list(seq)))
                else:
                    self.stages.append(("R", name, (list(seq), size, far)))
                    size //= 2
                    seq.append((name, size))
            for name in bits[3:]:
                self.stages.append(("B", name, (list(seq), size)))
            if self.c.get("pre"):
                self.stages.pop(1)
            while seq:
                name, half = seq[-1]
                self.stages.append(("G", name, (list(seq), half)))
                seq.pop()

        def off(self, seq):
            total = 0
            for name, half in seq:
                total = total + bit_of(name) * half
            return total

        def copies(self, s):
            kind, name, info = self.stages[s]
            ss, rs = send_sems.at[self.k], recv_sems.at[self.k]
            if kind == "C":
                lo = self.c["part"] * self.rows
                blk = [self.c_src.at[p, pl.ds(lo, self.rows)] for p in range(2)]
                return [
                    pltpu.make_async_copy(blk[0], self.acc, local_sems.at[self.k, 0]),
                    pltpu.make_async_copy(blk[1], self.mid, local_sems.at[self.k, 1]),
                ]
            if kind == "X":
                off = self.off(info)
                return [
                    remote(
                        rows_at(self.mid, off, name), rows_at(self.got_x, off, name),
                        ss.at[2], rs.at[2], "tp", 2,
                    )
                ]
            if kind == "R":
                seq, size, far = info
                half = size // 2
                off = self.off(seq) + (1 - bit_of(name)) * half
                slot = self.slot(s)
                out = [
                    remote(
                        rows_at(self.acc, off, half), self.halves[slot].at[0, pl.ds(0, half)],
                        ss.at[3 + s], rs.at[3 + s], "dp", name,
                    )
                ]
                if far:
                    out.append(
                        remote(
                            rows_at(self.mid, off, half),
                            self.halves[slot].at[1, pl.ds(0, half)],
                            ss.at[2 + 14], rs.at[2 + 14], "dp", name,
                        )
                    )
                return out
            if kind == "B":
                seq, size = info
                off = self.off(seq)
                slot = 2
                return [
                    remote(
                        rows_at(self.acc, off, size),
                        self.halves[slot].at[2 + bits.index(name) - 3, pl.ds(0, size)],
                        ss.at[3 + s], rs.at[3 + s], "dp", name,
                    )
                ]
            seq, half = info
            off = self.off(seq)
            here = rows_at(self.fin, off, half)
            return [remote(here, here, ss.at[3 + s], rs.at[3 + s], "dp", name)]

        def slot(self, s):
            return sum(1 for t in self.stages[:s] if t[0] == "R")

        def start(self, s):
            for cp in self.copies(s):
                cp.start()

        def finish(self, s):
            kind, name, info = self.stages[s]
            for cp in self.copies(s):
                cp.wait()
            if kind == "X":
                off = self.off(info)
                add_rows(self.acc, self.got_x, None, off, off, name)
            if kind == "R":
                seq, size, far = info
                half = size // 2
                off = self.off(seq) + bit_of(name) * half
                got = self.halves[self.slot(s)]
                add_rows(self.acc, got, 0, off, 0, half)
                if far:
                    add_rows(self.mid, got, 1, off, 0, half)
            if kind == "B":
                seq, size = info
                add_rows(self.acc, self.halves[2], bits.index(name) - 1, self.off(seq), 0, size)

        def event(self, s):
            if s > 0:
                self.finish(s - 1)
            if s < len(self.stages):
                if self.stages[s][0] == "G" and self.stages[s - 1][0] != "G":
                    seq, size = self.stages[s][2]
                    here = pl.ds(pl.multiple_of(self.off(seq), 16), size)
                    self.fin[here] = self.acc[here]
                self.start(s)
            else:
                self.out_copy().start()
                if self.c.get("head"):
                    head_start(self)

        def out_copy(self):
            return pltpu.make_async_copy(
                self.fin, outs[self.c["out"][0]].at[pl.ds(self.c["out"][1], self.rows)],
                local_sems.at[self.k, 2],
            )

        @property
        def n(self):
            return len(self.stages)

    head_nh, hr = [c["head"] for c in chunks if c.get("head")][0]
    head_chunk = []

    def head_remote(ch, p):
        mine = ch.fin.at[pl.ds(head_nh, hr)]
        return remote(mine, hg.at[p - 1], hg_send.at[p - 1], hg_recv.at[p - 1], "tp", p)

    def head_local(ch):
        mine = ch.fin.at[pl.ds(head_nh, hr)]
        return pltpu.make_async_copy(mine, rows_at(head_ref, tpi * hr, hr), local_sems.at[0, 3])

    def head_start(ch):
        head_chunk.append(ch)
        for p in range(1, tp_size):
            head_remote(ch, p).start()
        head_local(ch).start()

    work, at = [], 0
    for k, c in enumerate(chunks):
        ch = Chunk(k)
        if c["tp"]:
            if c["part"] == 0:
                at += 1
            ch.c_src = srcs[at - 1]
        work.append(ch)
    done = [0] * len(work)

    def go(k, upto=None):
        if done[k] <= work[k].n:
            work[k].event(done[k])
            done[k] += 1

    def turn(ks):
        for k in ks:
            go(k)

    ladder = [("tp", 1), ("tp", 2)] + [("dp", b) for b in bits]

    def small_copy(s):
        return remote(
            small_in, small_got.at[s], vec_send.at[0, s], vec_recv.at[0, s], *ladder[s]
        )

    def small_event(s):
        if s > 0:
            small_copy(s - 1).wait()
            got = small_got[s - 1]
            small_in[0:8] += got[0:8]
            if s == 1:
                small_in[8:9] += got[9:10]
                small_in[10:11] += got[11:12]
            elif s == 2:
                small_in[8:9] += got[10:11]
            else:
                small_in[8:9] += got[8:9]
        if s < len(ladder):
            small_copy(s).start()

    def do_copy(p):
        if p == 0:
            return pltpu.make_async_copy(do_ref.at[0], dos.at[0], do_local)
        return remote(do_ref.at[p], dos.at[p], do_send.at[p], do_recv.at[p], "tp", p)

    @pl.when(step == 0)
    def _():
        barrier = pltpu.get_barrier_semaphore()
        others = [("tp", m) for m in range(1, tp_size)] + [("dp", m) for m in range(1, dp_size)]
        for axis, bit in others:
            dev = (partner_any(dpi, bit), tpi) if axis == "dp" else (dpi, partner_any(tpi, bit))
            pl.semaphore_signal(
                barrier, inc=1, device_id=dev, device_id_type=pl.DeviceIdType.MESH
            )
        pl.semaphore_wait(barrier, len(others))
        for p in (2, 3, 1, 0):
            do_copy(p).start()
        turn(PLAN_FIRST)
        small_in[...] = small_ref[...]
        small_event(0)

    for p in range(tp_size):

        @pl.when(step == p)
        def _():
            do_copy(p).wait()

    @pl.when(i == 0)
    def _():
        ks[...] = qkv_ref[1, h].T
        vs[...] = qkv_ref[2, h].T
        dks[...] = jnp.zeros_like(dks)
        dvs[...] = jnp.zeros_like(dvs)

    lanes = pl.ds(pl.multiple_of(i * rows_dev, rows_dev), rows_dev)
    qt = qkv_ref[0, h, :, lanes] * jnp.bfloat16(scale)
    dot_t = dos[i, h]
    dsum = jnp.sum(
        dot_t.astype(F32) * o_ref[i, h].astype(F32), axis=0, keepdims=True
    )
    s = dot(ks[...], qt)
    p = jnp.exp(s - lse_ref[i, h])
    dp = dot(vs[...], dot_t)
    ds = (p * (dp - dsum)).astype(BF16)
    dqkv[0, h, :, lanes] = (dot(qkv_ref[1, h], ds) * scale).astype(BF16)
    dvs[...] += dot(p.astype(BF16), dot_t.T)
    dks[...] += dot(ds, qt.T)

    @pl.when(i == tp_size - 1)
    def _():
        dqkv[1, h] = dks[...].astype(BF16).T
        dqkv[2, h] = dvs[...].astype(BF16).T

    qk = 3 * HD
    due = {}
    spot = 0
    for k in range(len(work)):
        if not chunks[k]["tp"]:
            n = min(chunks[k]["rows"] // qk, heads - spot)
            due[k] = (spot, n)
            spot += n

    def weight_grad(k):
        first, n = due[k]
        for sec in range(3):
            lhs = dqkv[sec, first : first + n].reshape(n * HD, tp_size * rows_dev)
            work[k].acc[sec * n * HD : (sec + 1) * n * HD] = dot(lhs, rows_ref[...]).astype(BF16)
        spare = chunks[k]["rows"] - n * qk
        if spare:
            work[k].acc[n * qk :] = jnp.zeros((spare, width), BF16)
        go(k)

    early = [k for k in due if sum(due[k]) < heads]
    small_done = [1]
    for st in range(steps):

        @pl.when(step == st)
        def _():
            for k in early:
                if st == sum(due[k]) * tp_size - 1:
                    weight_grad(k)
            if st < len(PLAN_STEPS):
                turn(PLAN_STEPS[st])
            if small_done[0] <= len(ladder):
                small_event(small_done[0])
                small_done[0] += 1

    @pl.when(step == steps - 1)
    def _():
        blk = 128

        def da_rows(p, store):
            def one(r, carry):
                lane = pl.ds(pl.multiple_of(p * rows_dev + r * blk, blk), blk)
                lhs = dqkv[:, :, :, lane].reshape(3 * heads * HD, blk)
                here = pl.ds(pl.multiple_of(r * blk, blk), blk)
                store(here, dot(lhs, wt_ref[...], ((0,), (0,))))
                return carry

            lax.fori_loop(0, rows_dev // blk, one, 0)

        def keep(slot):
            def store(here, val):
                da_far[slot, here] = val.astype(BF16)

            return store

        core3 = remote(da_far.at[0], da_core.at[0], da_send.at[0], da_recv.at[0], "tp", 1)
        core1 = remote(da_far.at[1], da_core.at[1], da_send.at[1], da_recv.at[1], "tp", 1)
        far = remote(da_far.at[2], da_across, da_send.at[2], da_recv.at[2], "tp", 2)
        da_rows(3, keep(0))
        core3.start()
        turn(PLAN_TAIL[0])
        da_rows(1, keep(1))
        core1.start()
        turn(PLAN_TAIL[1])
        core3.wait()

        def store2(here, val):
            da_far[2, here] = (val + da_core[0, here].astype(F32)).astype(BF16)

        da_rows(2, store2)
        far.start()
        turn(PLAN_TAIL[2])
        for k in due:
            if k not in early:
                weight_grad(k)
        turn(PLAN_TAIL[3])
        core1.wait()

        def store0(here, val):
            tok_ref[here] = val + da_core[1, here].astype(F32)

        da_rows(0, store0)
        turn(PLAN_TAIL[4])
        turn(PLAN_WAIT)
        far.wait()
        last_tp[tpi] = jnp.zeros((8, width), F32)

        def norm_rows(r, carry):
            here = pl.ds(pl.multiple_of(r * blk, blk), blk)
            da = tok_ref[here] + da_across[here].astype(F32)
            hat, rstd = norm_parts(tiles_ref[here].astype(F32))
            tok_ref[here] = norm_back(hat, rstd, row_of(gain_ref), da)
            last_tp[tpi, 0:1] += jnp.sum(da * hat, axis=0, keepdims=True)
            last_tp[tpi, 1:2] += jnp.sum(da, axis=0, keepdims=True)
            return carry

        lax.fori_loop(0, rows_dev // blk, norm_rows, 0)

        def last_copy(axis, m):
            buf, me = (last_tp, tpi) if axis == "tp" else (last_dp, dpi)
            at = 0 if axis == "tp" else tp_size
            return remote(
                buf.at[me], buf.at[me], vec_send.at[1, at + m], vec_recv.at[1, at + m], axis, m
            )

        for m in range(1, tp_size):
            last_copy("tp", m).start()
        turn(PLAN_LAST[0])
        for m in range(1, tp_size):
            last_copy("tp", m).wait()
        total = last_tp[0]
        for k in range(1, tp_size):
            total = total + last_tp[k]
        last_dp[dpi] = total
        last_dp[dpi, 2:3] = onehot_ref[...]
        for m in range(1, dp_size):
            last_copy("dp", m).start()
        turn(PLAN_LAST[1])
        for m in range(1, dp_size):
            last_copy("dp", m).wait()

        last_ref[0:1] = jnp.sum(last_dp[:, 0, :], axis=0, keepdims=True)
        shares = last_dp[:, 1, :]
        last_ref[1:2] = jnp.sum(shares, axis=0, keepdims=True)
        leads = last_ref.shape[0] - 8
        hot = last_dp[:, 2, 0:128]
        for k in range(leads):
            last_ref[8 + k : 9 + k] = jnp.sum(hot[:, k : k + 1] * shares, axis=0, keepdims=True)
        turn(PLAN_LAST[2])
        while small_done[0] <= len(ladder):
            small_event(small_done[0])
            small_done[0] += 1
        turn(PLAN_END)
        while any(done[k] <= work[k].n for k in range(len(work))):
            turn(range(len(work)))
        sum_ref[...] = small_in[...]
        head_out = [head_local(head_chunk[0])]
        for p in range(1, tp_size):
            head_remote(head_chunk[0], p).wait()
            out = pltpu.make_async_copy(
                hg.at[p - 1], rows_at(head_ref, partner_any(tpi, p) * hr, hr),
                local_sems.at[p, 3],
            )
            out.start()
            head_out.append(out)
        for out in head_out:
            out.wait()
        for ch in work:
            ch.out_copy().wait()


def partner_any(index, mask):
    bit = 1
    while bit <= mask:
        if mask & bit:
            index = partner(index, bit)
        bit *= 2
    return index


PLAN_FIRST = (2, 0)
PLAN_STEPS = ((2, 0, 4, 1), (4, 1, 3), (3,), (0,), (2, 1), (0,), (1,), (0, 4, 1), (2,), (0, 3, 5, 4, 1), (2,), (),)
PLAN_TAIL = ((0,), (), (2,), (5,), (),)
PLAN_WAIT = (3, 4, 2, 6, 5, 0, 4, 1, 3)
PLAN_LAST = ((2,), (6, 5), (4, 3),)
PLAN_END = (2, 6, 4, 3, 5, 1, 6, 3, 6, 5, 4, 6, 3)

ORDERS = (
    ("X", 2, 1, 4),
    (2, "X", 1, 4),
    (1, "X", 2, 4),
    ("X", 2, 1, 4),
    (2, "X", 1, 4),
    (1, 2, 4),
    (1, 2, 4),
)


def attn_bwd(qkv, o, lse, do, rows, wt, tiles, gain, onehot, leads, small, parts, mesh, scale):
    _, heads, _, frame = qkv.shape
    rows_dev, width = tiles.shape
    tp_size, dp_size = mesh.shape["tp"], mesh.shape["dp"]
    nbits = dp_size.bit_length() - 1
    half = width // 2
    ph_rows = parts[2].shape[1]
    chunks = [
        dict(tp=True, rows=half, part=0, pre=True, order=ORDERS[0], out=(0, 0)),
        dict(tp=True, rows=half, part=1, pre=True, order=ORDERS[1], out=(0, half)),
        dict(tp=True, rows=half, part=0, order=ORDERS[2], out=(1, 0)),
        dict(tp=True, rows=half, part=1, order=ORDERS[3], out=(1, half)),
        dict(tp=True, rows=ph_rows, part=0, order=ORDERS[4], out=(2, 0), head=(heads * HD, HEAD_ROWS)),
        dict(tp=False, rows=half, order=ORDERS[5], out=(3, 0)),
        dict(tp=False, rows=256, order=ORDERS[6], out=(3, half)),
    ]
    n_k = len(chunks)
    scratch = [
        pltpu.VMEM((frame, HD), BF16),
        pltpu.VMEM((frame, HD), BF16),
        pltpu.VMEM((frame, HD), F32),
        pltpu.VMEM((frame, HD), F32),
        pltpu.VMEM((tp_size, heads, HD, rows_dev), BF16),
        pltpu.VMEM((3, heads, HD, frame), BF16),
        pltpu.VMEM((3, rows_dev, width), BF16),
        pltpu.VMEM((2, rows_dev, width), BF16),
        pltpu.VMEM((rows_dev, width), BF16),
        pltpu.VMEM((16, width), F32),
        pltpu.VMEM((2 + nbits, 16, width), F32),
        pltpu.VMEM((tp_size, 8, width), F32),
        pltpu.VMEM((dp_size, 8, width), F32),
        pltpu.VMEM((tp_size - 1, HEAD_ROWS, width), BF16),
    ]
    for c in chunks:
        r = c["rows"]
        scratch.append(pltpu.VMEM((r, width), BF16))
        scratch.append(pltpu.VMEM((2, r // 2, width), BF16))
        scratch.append(pltpu.VMEM((2, r // 4, width), BF16))
        scratch.append(pltpu.VMEM((2 + max(nbits - 3, 0), r // 8, width), BF16))
        if c["tp"]:
            scratch += [pltpu.VMEM((r, width), BF16)] * 3
        else:
            scratch.append(pltpu.VMEM((r, width), BF16))
    scratch += [
        pltpu.SemaphoreType.DMA((n_k, 17)),
        pltpu.SemaphoreType.DMA((n_k, 17)),
        pltpu.SemaphoreType.DMA((n_k, 4)),
        pltpu.SemaphoreType.DMA((tp_size,)),
        pltpu.SemaphoreType.DMA((tp_size,)),
        pltpu.SemaphoreType.DMA,
        pltpu.SemaphoreType.DMA((3,)),
        pltpu.SemaphoreType.DMA((3,)),
        pltpu.SemaphoreType.DMA((2, tp_size + dp_size)),
        pltpu.SemaphoreType.DMA((2, tp_size + dp_size)),
        pltpu.SemaphoreType.DMA((tp_size - 1,)),
        pltpu.SemaphoreType.DMA((tp_size - 1,)),
    ]
    any_spec = pl.BlockSpec(memory_space=pl.ANY)
    vmem = pl.BlockSpec(memory_space=pltpu.VMEM)
    return pl.pallas_call(
        functools.partial(
            bwd_kernel, scale=scale, chunks=chunks, dp_size=dp_size, heads=heads,
            tp_size=tp_size, width=width,
        ),
        grid=(heads, tp_size),
        in_specs=[vmem, vmem, vmem, any_spec] + [vmem] * 6 + [any_spec] * len(parts),
        out_specs=[vmem, vmem, vmem, any_spec] + [any_spec] * 4,
        out_shape=[
            jax.ShapeDtypeStruct((rows_dev, width), F32),
            jax.ShapeDtypeStruct((16, width), F32),
            jax.ShapeDtypeStruct((8 + leads, width), F32),
            jax.ShapeDtypeStruct((tp_size * HEAD_ROWS, width), BF16),
        ]
        + [
            jax.ShapeDtypeStruct((rows, width), BF16)
            for rows in (width, width, ph_rows, half + chunks[-1]["rows"])
        ],
        scratch_shapes=scratch,
        compiler_params=pltpu.CompilerParams(
            vmem_limit_bytes=60 << 20, collective_id=1, has_side_effects=True
        ),
        cost_estimate=pl.CostEstimate(
            flops=60_000_000_000, bytes_accessed=30 << 20, transcendentals=heads * frame * frame
        ),
        name="attn_bwd",
    )(qkv, o, lse, do, rows, wt, tiles, gain, onehot, small, *parts)


def mid_kernel(
    tiles_ref, o_ref, dots_ref, off_ref, pb_ref, g2_ref, s2_ref, nb_ref, hw_ref, hb_ref, lead_ref, tally_ref,
    pj_own, pj_far, wi_own, wi_far, na_own, na_far,
    dn_ref, dw_ref, ph_ref, do_ref, dx1_ref, small_ref, gates_ref, corr_ref,
    pj, wi, na, x1, hat, rstd, c_low, act, slope, h_low, hg, dx2, dz, du, dc, dy, hd, dn, dw, ph, dos,
    got_n, got_w, got_p, got_x, got_z, c_send, c_recv, x_send, x_recv, in_sem, out_sem, *, tp_size, heads
):
    dpi = lax.axis_index("dp")
    tpi = lax.axis_index("tp")
    rows_dev, width = tiles_ref.shape
    nh = heads * HD
    half = rows_dev // 2
    blocks = [pl.ds(r * half, half) for r in range(2)]

    def loads(k, own, far, dst):
        out = []
        for p in range(tp_size):
            src = own if p == 0 else far.at[p - 1]
            n = src.shape[0]
            to = dst.at[pl.ds(p * n, n)] if len(dst.shape) == 2 else dst.at[p]
            out.append(pltpu.make_async_copy(src, to, in_sem.at[k, p]))
        return out

    load_pj = loads(0, pj_own, pj_far, pj)
    load_wi = loads(1, wi_own, wi_far, wi)
    load_na = loads(2, na_own, na_far, na)
    for cp in load_pj + load_wi + load_na:
        cp.start()
    other = (dpi, partner(tpi, 1))
    side = (partner(dpi, PRE_BIT), tpi)
    far = (dpi, partner(tpi, 2))
    barrier = pltpu.get_barrier_semaphore()
    for dev in (other, side, far):
        pl.semaphore_signal(
            barrier, inc=1, device_id=dev, device_id_type=pl.DeviceIdType.MESH
        )
    mine = lax.rem(lax.div(dpi, PRE_BIT), 2)
    top_rows, quarter = width // 2, width // 4

    def far_copy():
        return pltpu.make_async_remote_copy(
            src_ref=dn.at[2, pl.ds(0, top_rows)], dst_ref=got_x,
            send_sem=x_send.at[0], recv_sem=x_recv.at[0],
            device_id=far, device_id_type=pl.DeviceIdType.MESH,
        )

    def side_copy(j):
        rows = pl.ds(pl.multiple_of(top_rows + (1 - mine) * quarter, 16), quarter)
        return pltpu.make_async_remote_copy(
            src_ref=dn.at[2 * j, rows], dst_ref=got_z.at[j],
            send_sem=x_send.at[1 + j], recv_sem=x_recv.at[1 + j],
            device_id=side, device_id_type=pl.DeviceIdType.MESH,
        )

    def core_copy(k, j, src, got):
        return pltpu.make_async_remote_copy(
            src_ref=src.at[2 * j + 1], dst_ref=got.at[j],
            send_sem=c_send.at[k, j], recv_sem=c_recv.at[k, j],
            device_id=other, device_id_type=pl.DeviceIdType.MESH,
        )

    small_ref[...] = jnp.zeros_like(small_ref)
    proj_bias, gain2, shift2, out_bias = (row_of(v) for v in (pb_ref, g2_ref, s2_ref, nb_ref))
    for cp in load_pj:
        cp.wait()
    for r in blocks:
        v = tiles_ref[r].astype(F32) + dot(o_ref[:, r], pj[...], ((0,), (0,))) + proj_bias
        x1[r] = v
        hv, rs = norm_parts(v)
        hat[r] = hv
        rstd[r] = rs
        c_low[r] = (hv * gain2 + shift2).astype(BF16)
    for p in range(tp_size):
        load_wi[p].wait()
        cols = pl.ds(p * width, width)
        for r in blocks:
            m, d = gelu_parts(dot(c_low[r], wi[p]) + off_ref[p, 0:1])
            act[r, cols] = m.astype(BF16)
            slope[r, cols] = d.astype(BF16)
    for cp in load_na:
        cp.wait()
    for r in blocks:
        h_low[r] = (x1[r] + dot(act[r], na[...]) + out_bias).astype(BF16)

    logits = dot(hw_ref[...], h_low[...], ((1,), (1,))) + hb_ref[...]
    row_scale = lax.rsqrt(jnp.full((1, 1), tally_ref[lead_ref[0]].astype(F32)))
    lg = [logits[e * HEAD_ROWS : (e + 1) * HEAD_ROWS] for e in range(EXPERTS)]
    top = jnp.maximum(jnp.maximum(lg[0], lg[1]), lg[2])
    ex = [jnp.exp(v - top) for v in lg]
    inv = 1.0 / (ex[0] + ex[1] + ex[2])
    gt = [v * inv for v in ex]
    mixed = gt[0] * dots_ref[0] + gt[1] * dots_ref[1] + gt[2] * dots_ref[2]
    for e in range(EXPERTS):
        gates_ref[e] = gt[e]
        hg[e * HEAD_ROWS : (e + 1) * HEAD_ROWS] = (gt[e] * (dots_ref[e] - mixed)).astype(BF16)
    hg[EXPERTS * HEAD_ROWS :] = (dots_ref[EXPERTS] * row_scale).astype(BF16)
    corr_ref[...] = logits[EXPERTS * HEAD_ROWS :] * row_scale
    d2 = dot(hg[...], hw_ref[...], ((0,), (0,)))
    dx2[...] = d2
    dz[...] = d2.astype(BF16)
    small_ref[0:1] = jnp.sum(d2, axis=0, keepdims=True)
    ones = jnp.ones((8, rows_dev), BF16)
    small_ref[4:5, : tp_size * HEAD_ROWS] = dot(ones, hg[...], ((1,), (1,)))[0:1]

    def send_out(k, p, src, dst):
        cp = pltpu.make_async_copy(src, dst, out_sem.at[k, p])
        cp.start()
        return cp

    outs = []
    pairs = range(tp_size // 2)

    def narrow_dot(p):
        return dot(act[:, p * width : (p + 1) * width], dz[...], ((0,), (0,)))

    def wide_dot(p):
        return dot(c_low[...], du[p], ((0,), (0,)))

    pl.semaphore_wait(barrier, 3)
    for j in (1, 0):
        dn[2 * j + 1] = narrow_dot(2 * j + 1).astype(BF16)
        core_copy(0, j, dn, got_n).start()
    def hidden_grad(p):
        cols = pl.ds(p * width, width)
        for r in blocks:
            v = dot(dz[r], na[cols], ((1,), (1,))) * slope[r, cols].astype(F32)
            low = v.astype(BF16)
            du[p, r] = low
            small_ref[8 + p : 9 + p] += jnp.sum(low.astype(F32), axis=0, keepdims=True)
    hidden_grad(1)
    hidden_grad(3)
    for j in (1, 0):
        core_copy(0, j, dn, got_n).wait()
        dn[2 * j] = (narrow_dot(2 * j) + got_n[j].astype(F32)).astype(BF16)
        if j == 1:
            far_copy().start()
        side_copy(j).start()
    hidden_grad(0)
    hidden_grad(2)
    for j in pairs:
        dw[2 * j + 1] = wide_dot(2 * j + 1).astype(BF16)
        core_copy(1, j, dw, got_w).start()
    for r in blocks:
        g = dot(du[0, r], wi[0], ((1,), (1,)))
        for p in range(1, tp_size):
            g = g + dot(du[p, r], wi[p], ((1,), (1,)))
        hv = hat[r]
        d1 = dx2[r] + norm_back(hv, rstd[r], gain2, g)
        dx1_ref[r] = d1
        dy[r] = d1.astype(BF16)
        small_ref[1:2] += jnp.sum(g * hv, axis=0, keepdims=True)
        small_ref[2:3] += jnp.sum(g, axis=0, keepdims=True)
        small_ref[3:4] += jnp.sum(d1, axis=0, keepdims=True)
    dos[...] = dot(pj[...], dy[...], ((1,), (1,))).astype(BF16).reshape(dos.shape)
    outs.append(send_out(2, 0, dos, do_ref))
    dp = dot(o_ref[...], dy[...]).astype(BF16)
    hd[...] = dot(hg[...], h_low[...]).astype(BF16)
    for p in range(tp_size):
        ph[p, 0:nh] = dp[p * nh : (p + 1) * nh]
        at = pl.ds(pl.multiple_of(partner_any(tpi, p) * HEAD_ROWS, 16), HEAD_ROWS)
        ph[p, nh : nh + HEAD_ROWS] = hd[at]
        ph[p, nh + HEAD_ROWS :] = jnp.zeros((ph.shape[1] - nh - HEAD_ROWS, width), BF16)
    for j in pairs:
        core_copy(2, j, ph, got_p).start()
    for j in pairs:
        core_copy(1, j, dw, got_w).wait()
        dw[2 * j] = (wide_dot(2 * j) + got_w[j].astype(F32)).astype(BF16)
        outs.append(send_out(1, j, dw.at[2 * j], dw_ref.at[j]))
    for j in pairs:
        core_copy(2, j, ph, got_p).wait()
        ph[2 * j] = (ph[2 * j].astype(F32) + got_p[j].astype(F32)).astype(BF16)
        outs.append(send_out(3, j, ph.at[2 * j], ph_ref.at[j]))
    far_copy().wait()
    add_rows(dn.at[0], got_x, None, 0, 0, top_rows)
    for j in (1, 0):
        side_copy(j).wait()
        add_rows(dn.at[2 * j], got_z, j, top_rows + mine * quarter, 0, quarter)
        outs.append(send_out(0, j, dn.at[2 * j], dn_ref.at[j]))
    for cp in outs:
        cp.wait()


def mid(tiles, o_own, dots, off, vecs, hw, hb, lead, tally, weights, mesh, heads):
    rows_dev, width = tiles.shape
    tp_size = mesh.shape["tp"]
    nh = heads * HD
    ph_rows = -(-(nh + HEAD_ROWS) // 128) * 128
    n_head = hw.shape[0]
    any_spec = pl.BlockSpec(memory_space=pl.ANY)
    vmem = pl.BlockSpec(memory_space=pltpu.VMEM)
    big = (tp_size, width, width)
    pair = (tp_size // 2,)
    return pl.pallas_call(
        functools.partial(mid_kernel, tp_size=tp_size, heads=heads),
        in_specs=[vmem] * 10 + [pl.BlockSpec(memory_space=pltpu.SMEM)] * 2 + [any_spec] * 6,
        out_specs=[any_spec] * 4 + [vmem] * 4,
        out_shape=[
            jax.ShapeDtypeStruct(pair + (width, width), BF16),
            jax.ShapeDtypeStruct(pair + (width, width), BF16),
            jax.ShapeDtypeStruct(pair + (ph_rows, width), BF16),
            jax.ShapeDtypeStruct((tp_size, heads, HD, rows_dev), BF16),
            jax.ShapeDtypeStruct((rows_dev, width), F32),
            jax.ShapeDtypeStruct((16, width), F32),
            jax.ShapeDtypeStruct((EXPERTS, HEAD_ROWS, rows_dev), F32),
            jax.ShapeDtypeStruct((HEAD_ROWS, rows_dev), F32),
        ],
        scratch_shapes=[
            pltpu.VMEM((tp_size * nh, width), BF16),
            pltpu.VMEM(big, BF16),
            pltpu.VMEM((tp_size * width, width), BF16),
            pltpu.VMEM((rows_dev, width), F32),
            pltpu.VMEM((rows_dev, width), F32),
            pltpu.VMEM((rows_dev, 1), F32),
            pltpu.VMEM((rows_dev, width), BF16),
            pltpu.VMEM((rows_dev, tp_size * width), BF16),
            pltpu.VMEM((rows_dev, tp_size * width), BF16),
            pltpu.VMEM((rows_dev, width), BF16),
            pltpu.VMEM((n_head, rows_dev), BF16),
            pltpu.VMEM((rows_dev, width), F32),
            pltpu.VMEM((rows_dev, width), BF16),
            pltpu.VMEM((tp_size, rows_dev, width), BF16),
            pltpu.VMEM((8, width), F32),
            pltpu.VMEM((rows_dev, width), BF16),
            pltpu.VMEM((n_head, width), BF16),
            pltpu.VMEM(big, BF16),
            pltpu.VMEM(big, BF16),
            pltpu.VMEM((tp_size, ph_rows, width), BF16),
            pltpu.VMEM((tp_size, heads, HD, rows_dev), BF16),
            pltpu.VMEM(pair + (width, width), BF16),
            pltpu.VMEM(pair + (width, width), BF16),
            pltpu.VMEM(pair + (ph_rows, width), BF16),
            pltpu.VMEM((width // 2, width), BF16),
            pltpu.VMEM(pair + (width // 4, width), BF16),
            pltpu.SemaphoreType.DMA((3, tp_size // 2)),
            pltpu.SemaphoreType.DMA((3, tp_size // 2)),
            pltpu.SemaphoreType.DMA((3,)),
            pltpu.SemaphoreType.DMA((3,)),
            pltpu.SemaphoreType.DMA((3, tp_size)),
            pltpu.SemaphoreType.DMA((4, tp_size)),
        ],
        compiler_params=pltpu.CompilerParams(
            vmem_limit_bytes=MID_VMEM, collective_id=2, has_side_effects=True
        ),
        cost_estimate=pl.CostEstimate(
            flops=18_000_000_000, bytes_accessed=30 << 20, transcendentals=2_000_000
        ),
        name="mid",
    )(tiles, o_own, dots, off, *vecs, hw, hb, lead, tally, *weights)


def finish_kernel(
    n_ref, i_ref, ph_ref, qa_ref, qb_ref, hd_ref, tok_ref, dx_ref, table_ref, small_ref,
    no_ref, io_ref, po_ref, qo_ref, g_ref, c_ref, to_ref, lead_ref, *vec_refs, fields
):
    no_ref[...] = n_ref[...].astype(F32)
    io_ref[...] = i_ref[...].astype(F32)
    po_ref[...] = ph_ref[...].astype(F32)
    na = qa_ref.shape[0]
    qo_ref[0, :na] = qa_ref[...].astype(F32)
    qo_ref[0, na:] = qb_ref[...].astype(F32)
    for e in range(EXPERTS):
        g_ref[e * fields : (e + 1) * fields] = hd_ref[pl.ds(e * HEAD_ROWS, HEAD_ROWS)].astype(F32)[
            :fields
        ]
    c_ref[...] = hd_ref[pl.ds(EXPERTS * HEAD_ROWS, HEAD_ROWS)].astype(F32)[:fields]
    to_ref[...] = tok_ref[...] + dx_ref[...]
    lead_ref[...] = table_ref[8:]
    rows = [table_ref[0:1], table_ref[1:2]] + [small_ref[k : k + 1] for k in (3, 1, 2, 8, 0)]
    for ref, row in zip(vec_refs, rows):
        ref[...] = row.reshape(row.shape[1])


def finish(n, i, ph, q, hd, tok, dx1, table, small, heads, fields):
    width = n.shape[0]
    nh = heads * HD
    steps = 3
    rows = width // steps
    first = (width // 2) // (3 * HD) * HD
    second = nh - first
    base = 3 * first // second
    tok_rows = tok.shape[0] // 2
    leads = table.shape[0] - 8

    def by_row(r):
        return pl.BlockSpec((r, width), lambda g: (g, 0))

    token = pl.BlockSpec((tok_rows, width), lambda g: (jnp.minimum(g, 1), 0))
    return pl.pallas_call(
        functools.partial(finish_kernel, fields=fields),
        grid=(steps,),
        in_specs=[
            by_row(rows),
            by_row(rows),
            by_row(nh // steps),
            by_row(first),
            pl.BlockSpec((second, width), lambda g: (base + g, 0)),
            pl.BlockSpec((hd.shape[0], rows), lambda g: (0, g)),
            token,
            token,
            pl.BlockSpec(table.shape, lambda g: (0, 0)),
            pl.BlockSpec(small.shape, lambda g: (0, 0)),
        ],
        out_specs=[
            by_row(rows),
            by_row(rows),
            by_row(nh // steps),
            pl.BlockSpec((1, nh, width), lambda g: (g, 0, 0)),
            pl.BlockSpec((EXPERTS * fields, rows), lambda g: (0, g)),
            pl.BlockSpec((fields, rows), lambda g: (0, g)),
            token,
            pl.BlockSpec((leads, width), lambda g: (0, 0)),
        ]
        + [pl.BlockSpec((width,), lambda g: (0,))] * 7,
        out_shape=[
            jax.ShapeDtypeStruct((width, width), F32),
            jax.ShapeDtypeStruct((width, width), F32),
            jax.ShapeDtypeStruct((nh, width), F32),
            jax.ShapeDtypeStruct((3, nh, width), F32),
            jax.ShapeDtypeStruct((EXPERTS * fields, width), F32),
            jax.ShapeDtypeStruct((fields, width), F32),
            jax.ShapeDtypeStruct(tok.shape, F32),
            jax.ShapeDtypeStruct((leads, width), F32),
        ]
        + [jax.ShapeDtypeStruct((width,), F32)] * 7,
        name="finish",
    )(n, i, ph, q, q, hd, tok, dx1, table, small)


def norm_parts(values):
    center = values - jnp.mean(values, axis=-1, keepdims=True)
    rstd = lax.rsqrt(jnp.mean(center * center, axis=-1, keepdims=True) + EPSILON)
    return center * rstd, rstd


def norm_back(hat, rstd, gain, grad):
    g = grad * gain
    return rstd * (
        g
        - jnp.mean(g, axis=-1, keepdims=True)
        - hat * jnp.mean(g * hat, axis=-1, keepdims=True)
    )


def gelu_parts(u):
    half = jnp.exp(-0.5 * u * u)
    t = 1.0 / (1.0 + (0.3275911 * 0.7071067811865476) * jnp.abs(u))
    poly = t * (
        0.254829592
        + t * (-0.284496736 + t * (1.421413741 + t * (-1.453152027 + t * 1.061405429)))
    )
    tail = 0.5 * poly * half
    cdf = jnp.where(u >= 0, 1.0 - tail, tail)
    return u * cdf, cdf + u * half * 0.3989422804014327


def make_body(mesh):
    tp_size = mesh.shape["tp"]

    def body(
        tile_vectors,
        snapshot_horizon_slot,
        horizon_sample_tally,
        specialist_outlooks,
        early_layernorm_scale,
        early_layernorm_shift,
        horizon_vectors,
        triple_head_matrix,
        attending_matrix,
        attending_offset,
        later_layernorm_scale,
        later_layernorm_shift,
        widening_matrix,
        widening_offset,
        narrowing_matrix,
        narrowing_offset,
        router_matrix,
        router_offset,
        adjuster_matrix,
        adjuster_offset,
        combined_loss_slope,
    ):
        rows_dev, width = tile_vectors.shape
        heads = triple_head_matrix.shape[2] // HD
        rows_frame = rows_dev * tp_size
        fields = adjuster_matrix.shape[1]
        sites = combined_loss_slope.shape[1]
        scale_val = HD ** (-0.5)
        tp_index = lax.axis_index("tp")
        lead = snapshot_horizon_slot[0]
        nh = heads * HD
        w_t = jnp.transpose(triple_head_matrix, (0, 2, 1))
        (attn_rows, qkv, o_heads, lse, o_own, dots, off_all, proj_all, wide_all, narrow_all) = attn_fwd(
            snapshot_horizon_slot,
            tile_vectors,
            early_layernorm_scale,
            early_layernorm_shift,
            horizon_vectors,
            widening_offset,
            w_t,
            attending_matrix,
            widening_matrix,
            narrowing_matrix,
            specialist_outlooks,
            combined_loss_slope,
            mesh,
            scale_val,
        )

        def head_pad(x):
            x = x.reshape((EXPERTS + 1, fields) + x.shape[1:])
            x = jnp.pad(x, ((0, 0), (0, HEAD_ROWS - fields)) + ((0, 0),) * (x.ndim - 2))
            return x.reshape((-1,) + x.shape[2:])

        hw = head_pad(jnp.concatenate([router_matrix, adjuster_matrix], axis=1).T)
        hb = head_pad(jnp.concatenate([router_offset, adjuster_offset])[:, None])
        vec = (attending_offset, later_layernorm_scale, later_layernorm_shift, narrowing_offset)
        (d_narrow, d_wide, d_ph, do_all, dx1, small, gates, corr) = mid(
            tile_vectors,
            o_own.reshape(tp_size * nh, rows_dev),
            dots,
            off_all,
            vec,
            hw,
            hb,
            snapshot_horizon_slot,
            horizon_sample_tally,
            [
                attending_matrix, proj_all, widening_matrix, wide_all,
                narrowing_matrix, narrow_all,
            ],
            mesh,
            heads,
        )
        gates = gates[:, :fields]
        corr = corr[:fields]

        blended = (corr)[:, None, :]
        for e in range(EXPERTS):
            blended = blended + gates[e][:, None, :] * specialist_outlooks[e].astype(F32)

        leads = horizon_vectors.shape[0]
        onehot = (jnp.arange(width, dtype=jnp.int32) == lead).astype(F32)[None, :]
        (token_part, small, table, head_sum, n_low, i_low, ph, q_low) = attn_bwd(
            qkv, o_heads, lse, do_all, attn_rows.reshape(rows_frame, width), w_t.reshape(3 * nh, width), tile_vectors,
            early_layernorm_scale, onehot, leads, small,
            [d_narrow, d_wide, d_ph], mesh, scale_val,
        )
        (
            narrow_sum, wide_sum, proj_weight_grad, qkv_sum, gate_sum, correct_sum, tokens_grad,
            lead_sum, gain1_sum, shift1_sum, proj_bias_sum, gain2_sum, shift2_sum, in_bias_sum,
            out_bias_sum,
        ) = finish(
            n_low, i_low, ph, q_low, head_sum, token_part, dx1, table, small, heads, fields
        )
        qkv_sum = jnp.transpose(qkv_sum, (0, 2, 1))
        gate_weight_grad = gate_sum.T
        correct_weight_grad = correct_sum.T
        head_bias = small[4, : (EXPERTS + 1) * HEAD_ROWS].reshape(EXPERTS + 1, HEAD_ROWS)
        head_bias = head_bias[:, :fields]

        return (
            blended,
            tokens_grad,
            gain1_sum,
            shift1_sum,
            lead_sum,
            qkv_sum,
            proj_weight_grad,
            proj_bias_sum,
            gain2_sum,
            shift2_sum,
            wide_sum,
            in_bias_sum,
            narrow_sum,
            out_bias_sum,
            gate_weight_grad,
            head_bias[:EXPERTS].reshape(EXPERTS * fields),
            correct_weight_grad,
            head_bias[EXPERTS],
        )

    return body


def solution(mesh):
    return jax.shard_map(
        make_body(mesh),
        mesh=mesh,
        in_specs=(
            P(("dp", "tp"), None),
            P("dp"),
            P(),
            P(None, None, None, ("dp", "tp")),
            P(),
            P(),
            P(),
            P(None, None, "tp"),
            P("tp", None),
            P(),
            P(),
            P(),
            P(None, "tp"),
            P("tp"),
            P("tp", None),
            P(),
            P(),
            P(),
            P(),
            P(),
            P(None, None, ("dp", "tp")),
        ),
        out_specs=(
            P(None, None, ("dp", "tp")),
            P(("dp", "tp"), None),
            P(),
            P(),
            P(),
            P(None, None, "tp"),
            P("tp", None),
            P(),
            P(),
            P(),
            P(None, "tp"),
            P("tp"),
            P("tp", None),
            P(),
            P(),
            P(),
            P(),
            P(),
        ),
        check_vma=False,
    )
```
